32 devices in a mesh: groups: 2 (over x), ctx: 4 (over y, core), tp: 4 (over z).
Axes of the slice: x: 2, y: 2, z: 4, core: 2. Of those that a mesh axis runs over, the one named last changes fastest.
Arguments:
- queries: bfloat16 [3072, 8192], P(('groups', 'ctx'), 'tp'), parts along dimension 0, may hold values from -6 to 6
- key_states: bfloat16 [3072, 1024], P(('groups', 'ctx'), 'tp'), parts along dimension 0, may hold values from -6 to 6
- value_tensor: bfloat16 [3072, 1024], P(('groups', 'ctx'), 'tp'), parts along dimension 0, may hold values from -6 to 6
- output_gradient: bfloat16 [3072, 8192], P(('groups', 'ctx'), 'tp'), parts along dimension 0, may hold values from -6 to 6
- parent: int32 [24], P('groups'), parts along dimension 0, may hold values from -1 to 8, as said below
- block_owner: int32 [24], P('groups'), parts along dimension 0, may hold values from 0 to 11, as said below
Outputs:
- attn_out: bfloat16 [3072, 8192], P(('groups', 'ctx'), 'tp'), parts along dimension 0
- d_queries: bfloat16 [3072, 8192], P(('groups', 'ctx'), 'tp'), parts along dimension 0
- d_keys: bfloat16 [3072, 1024], P(('groups', 'ctx'), 'tp'), parts along dimension 0
- d_values: bfloat16 [3072, 1024], P(('groups', 'ctx'), 'tp'), parts along dimension 0
The draws below stay inside these ranges and needn't reach their ends.
There are 2 independent parts, one for each index of `groups`. The reference program is written for one: setup_inputs(seed, part) draws one part's arguments, and reference() takes and returns one part's arrays. A program takes and returns all parts, laid end to end along the dimension named above; each array names one. Nothing has to cross between parts.
Inputs may be any that keep to these rules, and one draw needn't show every extreme that they name: Tree block ids are ordered so that a parent comes before its children. All blocks of one stored shard (3 blocks in a row) lie at one depth of the tree, and their parents lie on one other shard, so a block's ancestors are never on its own shard. A path from a root holds at most 16 blocks; some path reaches 16 where the group has 16 shards or more. The blocks of one shard have ancestors among at most 2 blocks of any other one shard, and every shard that is not at depth 0 reaches 2 with its parent shard. `block_owner`: A permutation of the stored blocks that keeps each shard's blocks together.
All inputs are finite; a program needn't handle non-finite values.
Results may differ from the reference program's by a relative error of at most 0.015.
Values may be sent and summed in bfloat16 or wider, within the bound.
No kernel may reach another device: no remote copies, remote signals or barrier semaphores. Data moves between devices by JAX's collectives and lax.ppermute only.
A program may use at most 192 MiB of HBM per device.

```python
import math
import jax
import jax.numpy as jnp
from jax import lax

QUERY_HEADS = 64
KEY_VALUE_HEADS = 8
HEAD_SIZE = 128
TREE_BLOCK_SIZE = 128
PATH_DEPTH_MAX = 16
BLK_DEV = 3
GROUP_TOKENS = 1536
GROUP_BLOCKS = 12


def shared_forest(key):
    design_key, branch_key, place_key = jax.random.split(key, 3)
    group_count = GROUP_BLOCKS // BLK_DEV
    first_pick = jax.vmap(lambda sub_key: jax.random.permutation(sub_key, BLK_DEV - 1)[0])(jax.random.split(design_key, group_count))
    last_pick = jnp.full((group_count,), BLK_DEV - 1, dtype=first_pick.dtype)
    designated = jnp.stack([first_pick, last_pick], axis=1)
    branch_index = jax.random.randint(branch_key, (group_count, BLK_DEV), 0, 2)
    branch_index = branch_index.at[:, 0].set(0).at[:, 1].set(1)
    previous = jnp.roll(designated, 1, axis=0)
    chosen = jnp.take_along_axis(previous, branch_index, axis=1)
    group_index = jnp.arange(group_count)[:, None]
    parents = jnp.where(group_index % PATH_DEPTH_MAX == 0, -1, (group_index - 1) * BLK_DEV + chosen)
    shard_order = jax.random.permutation(place_key, group_count)
    owners = shard_order[:, None] * BLK_DEV + jnp.arange(BLK_DEV)[None, :]
    return (parents.reshape(-1).astype(jnp.int32), owners.reshape(-1).astype(jnp.int32))


def draw_parent(key, part):
    parents, owners = shared_forest(key)
    return parents


def draw_block_owner(key, part):
    parents, owners = shared_forest(key)
    return owners


def draw_queries(key, part):
    key = jax.random.fold_in(key, 7)
    return jnp.clip(jax.random.normal(key, (GROUP_TOKENS, QUERY_HEADS * HEAD_SIZE), jnp.float32), -4.0, 4.0).astype(jnp.bfloat16)


def draw_key_states(key, part):
    key = jax.random.fold_in(key, 9)
    return jnp.clip(jax.random.normal(key, (GROUP_TOKENS, KEY_VALUE_HEADS * HEAD_SIZE), jnp.float32), -4.0, 4.0).astype(jnp.bfloat16)


def block_levels(key, shape, pieces, smallest, largest):
    def one(dim, parts):
        steps = jax.random.uniform(jax.random.fold_in(jax.random.fold_in(key, 6), dim), (parts,), jnp.float32, smallest / len(pieces), largest / len(pieces))
        return jnp.repeat(jnp.exp(steps), shape[dim] // parts).reshape((-1,) + (1,) * (len(shape) - dim - 1))

    factor_of = one(*pieces[0])
    for cut in pieces[1:]:
        factor_of = factor_of * one(*cut)
    return factor_of


def centred(stream_key, dims, width, reach, pieces=(), kind=jnp.bfloat16):
    array = width * jax.random.normal(stream_key, dims, jnp.float32)
    if pieces:
        array = array * block_levels(stream_key, dims, pieces, -0.22, 0.18)
    return jnp.clip(array, -reach, reach).astype(kind)


def setup_inputs(seed: int = 0, part: int = 0) -> dict:
    keys = jax.random.split(jax.random.key(seed), 7)
    part_splits = jax.random.split(jax.random.fold_in(keys[6], part), 7)
    queries = draw_queries(jax.random.fold_in(jax.random.fold_in(keys[6], part), 71), part)
    key_states = draw_key_states(jax.random.fold_in(jax.random.fold_in(keys[6], part), 71), part)
    value_tensor = centred(part_splits[2], (GROUP_TOKENS, KEY_VALUE_HEADS * HEAD_SIZE), 1.0, 6.0, ((0, 4), (1, 4)))
    output_gradient = centred(part_splits[3], (GROUP_TOKENS, QUERY_HEADS * HEAD_SIZE), 1.0, 6.0, ((0, 4), (1, 4)))
    parent = draw_parent(jax.random.fold_in(jax.random.fold_in(keys[6], part), 71), part)
    block_owner = draw_block_owner(jax.random.fold_in(jax.random.fold_in(keys[6], part), 71), part)
    return dict(queries=queries, key_states=key_states, value_tensor=value_tensor, output_gradient=output_gradient, parent=parent, block_owner=block_owner)


def lookup_table(lookup_values, index):
    places = jnp.arange(lookup_values.shape[0], dtype=jnp.int32)
    matches = index[..., None] == places
    return lax.optimization_barrier(jnp.sum(jnp.where(matches, lookup_values, 0), axis=-1)).astype(jnp.int32)

def ancestor_table(parent, block_owner, chain_depth):
    places = jnp.arange(block_owner.shape[0], dtype=jnp.int32)
    holder = lax.optimization_barrier(jnp.sum(jnp.where(block_owner[None, :] == places[:, None], places[None, :], 0), axis=1)).astype(jnp.int32)
    current = holder
    columns = [places]
    for hop_index in range(chain_depth - 1):
        current = jnp.where(current >= 0, lookup_table(parent, jnp.maximum(current, 0)), -1)
        columns.append(jnp.where(current >= 0, lookup_table(block_owner, jnp.maximum(current, 0)), -1))
    return jnp.stack(columns, axis=1)

def visible_mask(ancestry, block_len):
    row_index = jnp.arange(block_len)[:, None]
    key_index = jnp.arange(ancestry.shape[0] * block_len)[None, :]
    live_slot = jnp.repeat(ancestry >= 0, block_len)[None, :]
    return jnp.where(key_index // block_len == 0, key_index % block_len <= row_index, live_slot)

def rounded(full_values):
    return lax.optimization_barrier(full_values.astype(jnp.bfloat16)).astype(jnp.float32)

def attend_exact(query_block, grad_block, key_row_list, value_row_list, visible, score_scale):
    highest_precision = lax.Precision.HIGHEST
    query_full = query_block.astype(jnp.float32)
    grad_full = grad_block.astype(jnp.float32)
    key_full = key_row_list.astype(jnp.float32)
    value_full = value_row_list.astype(jnp.float32)
    scores = jnp.einsum('qhgd,khd->hgqk', query_full, key_full, precision=highest_precision) * score_scale
    scores = jnp.where(visible, scores, -jnp.inf)
    highest = lax.optimization_barrier(jnp.max(scores, axis=-1, keepdims=True))
    totals = lax.optimization_barrier(jnp.sum(jnp.exp(scores - highest), axis=-1, keepdims=True))
    probabilities = jnp.exp(scores - (highest + jnp.log(totals)))
    weights = rounded(probabilities)
    attended = jnp.einsum('hgqk,khd->qhgd', weights, value_full, precision=highest_precision)
    attended_low = attended.astype(jnp.bfloat16)
    attended_back = rounded(attended)
    row_inner = jnp.transpose(lax.optimization_barrier(jnp.sum(grad_full * attended_back, axis=-1)), (1, 2, 0))
    dprobs = jnp.einsum('qhgd,khd->hgqk', grad_full, value_full, precision=highest_precision)
    dscores = rounded(probabilities * (dprobs - row_inner[..., None]))
    dquery = (jnp.einsum('hgqk,khd->qhgd', dscores, key_full, precision=highest_precision) * score_scale).astype(jnp.bfloat16)
    key_grad = jnp.einsum('hgqk,qhgd->khd', dscores, query_full, precision=highest_precision) * score_scale
    dvalues = jnp.einsum('hgqk,qhgd->khd', weights, grad_full, precision=highest_precision)
    return (attended_low, dquery, key_grad, dvalues)

def reference(queries, key_states, value_tensor, output_gradient, parent, block_owner):
    ancestry_all = ancestor_table(parent, block_owner, PATH_DEPTH_MAX)
    row_span_width = KEY_VALUE_HEADS * HEAD_SIZE
    groups_each_split = QUERY_HEADS // KEY_VALUE_HEADS
    score_scale = 1.0 / math.sqrt(HEAD_SIZE)
    key_block_list = key_states.reshape(GROUP_BLOCKS, TREE_BLOCK_SIZE, row_span_width)
    value_block_list = value_tensor.reshape(GROUP_BLOCKS, TREE_BLOCK_SIZE, row_span_width)
    query_block_list = queries.reshape(GROUP_BLOCKS, TREE_BLOCK_SIZE, KEY_VALUE_HEADS, groups_each_split, HEAD_SIZE)
    gradient_block_list = output_gradient.reshape(GROUP_BLOCKS, TREE_BLOCK_SIZE, KEY_VALUE_HEADS, groups_each_split, HEAD_SIZE)

    def advance(running, block_items):
        key_sums, value_sums = running
        query_block, grad_block, ancestry = block_items
        allowed_flags = jnp.maximum(ancestry, 0).astype(jnp.int32)
        key_row_list = key_block_list[allowed_flags].reshape(PATH_DEPTH_MAX * TREE_BLOCK_SIZE, KEY_VALUE_HEADS, HEAD_SIZE)
        value_row_list = value_block_list[allowed_flags].reshape(PATH_DEPTH_MAX * TREE_BLOCK_SIZE, KEY_VALUE_HEADS, HEAD_SIZE)
        visible = visible_mask(ancestry, TREE_BLOCK_SIZE)
        attended, dquery, key_grad, dvalues = attend_exact(query_block, grad_block, key_row_list, value_row_list, visible, score_scale)
        live_slot = (ancestry >= 0)[:, None, None]
        key_sums = key_sums.at[allowed_flags].add(jnp.where(live_slot, key_grad.reshape(PATH_DEPTH_MAX, TREE_BLOCK_SIZE, row_span_width), 0.0))
        value_sums = value_sums.at[allowed_flags].add(jnp.where(live_slot, dvalues.reshape(PATH_DEPTH_MAX, TREE_BLOCK_SIZE, row_span_width), 0.0))
        return ((key_sums, value_sums), (attended, dquery))
    zero_grads = jnp.zeros((GROUP_BLOCKS, TREE_BLOCK_SIZE, row_span_width), jnp.float32)
    (key_sums, value_sums), (attended, dquery) = lax.scan(advance, (zero_grads, zero_grads), (query_block_list, gradient_block_list, ancestry_all))
    attn_out = attended.reshape(GROUP_TOKENS, QUERY_HEADS * HEAD_SIZE)
    d_queries = dquery.reshape(GROUP_TOKENS, QUERY_HEADS * HEAD_SIZE)
    d_keys = key_sums.reshape(GROUP_TOKENS, row_span_width).astype(jnp.bfloat16)
    d_values = value_sums.reshape(GROUP_TOKENS, row_span_width).astype(jnp.bfloat16)
    return (attn_out, d_queries, d_keys, d_values)
```

```python
import functools
import math

import jax
import jax.numpy as jnp
from jax import lax
import jax.experimental.pallas as pl
import jax.experimental.pallas.tpu as pltpu
from jax.sharding import PartitionSpec as P

HEAD_SIZE = 128
TREE_BLOCK_SIZE = 128
PATH_DEPTH_MAX = 16
QUERY_HEADS = 64
KEY_VALUE_HEADS = 8

D = HEAD_SIZE
T = TREE_BLOCK_SIZE
NT = (((1,), (1,)), ((), ()))
TN = (((0,), (0,)), ((), ()))
BF = jnp.bfloat16
F32 = jnp.float32
SCALE = 1.0 / math.sqrt(D)
LOG2E = math.log2(math.e)


def fill_table(info, table, me, blocks, group_blocks, depth, pairwise):
    for b in range(blocks):
        mine = me * blocks + b

        def find(t, found):
            return jnp.where(info[1 + group_blocks + t] == mine, t, found)

        current = lax.fori_loop(0, group_blocks, find, jnp.int32(0))
        for d in range(depth):
            if d:
                current = jnp.where(current >= 0, info[1 + jnp.maximum(current, 0)], -1)
            owner = info[1 + group_blocks + jnp.maximum(current, 0)]
            if pairwise:
                shard = lax.div(owner, jnp.int32(blocks))
                place = (shard ^ me) * blocks + owner - shard * blocks
            else:
                place = owner
            table[b * depth + d] = jnp.where(current >= 0, place, -1)


def attend_kernel(*refs, head, blocks, group_blocks, depth, groups, shards, pairwise, chained):
    source_count = shards if pairwise else 1
    info, q_ref, do_ref = refs[:3]
    sources = refs[3 : 3 + source_count]
    at = 3 + source_count + (2 if chained else 0)
    o_out, dq_out, sum_ref = refs[at : at + 3]
    at += 3
    if pairwise:
        core_ref, far_ref = refs[at : at + 2]
        at += 2
    kv, acc, kb, vb, pt, dst, o_buf, dq_buf, table, kv_sem, out_sem = refs[at:]
    rows_each = blocks * T
    part_rows = kv.shape[0] // source_count

    def source_copy(i):
        return pltpu.make_async_copy(sources[i], kv.at[pl.ds(i * part_rows, part_rows)], kv_sem.at[i])

    for i in range(source_count):
        source_copy(i).start()
    me = info[0]
    fill_table(info, table, me, blocks, group_blocks, depth, pairwise)
    acc[...] = jnp.zeros_like(acc)
    for i in range(source_count):
        source_copy(i).wait()

    tri = lax.broadcasted_iota(jnp.int32, (T, T), 0) <= lax.broadcasted_iota(jnp.int32, (T, T), 1)

    def place(b, d):
        return pl.ds(pl.multiple_of(jnp.maximum(table[b * depth + d], 0) * T, T), T)

    def out_copies(b):
        rows = pl.ds(pl.multiple_of(b * T, T), T)
        columns = pl.ds(head * groups * D, groups * D)
        return (
            pltpu.make_async_copy(o_buf.at[b], o_out.at[rows, columns], out_sem.at[0, b]),
            pltpu.make_async_copy(dq_buf.at[b], dq_out.at[rows, columns], out_sem.at[1, b]),
        )

    def block(b, carry):
        rows = pl.ds(pl.multiple_of(b * T, T), T)
        for d in range(depth):
            kb[pl.ds(d * T, T), :] = kv[place(b, d), :D]
            vb[pl.ds(d * T, T), :] = kv[place(b, d), D:]
        bias = [
            jnp.where(table[b * depth + d] >= 0, 0.0, -jnp.inf).astype(F32) for d in range(depth)
        ]
        for g in range(groups):
            col = pl.ds(g * T, T)
            head_col = pl.ds((head * groups + g) * D, D)
            scores = lax.dot_general(kb[...], q_ref[rows, head_col], NT, preferred_element_type=F32)
            dprobs = lax.dot_general(vb[...], do_ref[rows, head_col], NT, preferred_element_type=F32)
            parts = [scores[d * T : (d + 1) * T] * (SCALE * LOG2E) for d in range(depth)]
            parts[0] = jnp.where(tri, parts[0], -jnp.inf)
            highs = [jnp.max(x, axis=0, keepdims=True) + bias[d] for d, x in enumerate(parts)]
            high = functools.reduce(jnp.maximum, highs)
            exps = [jnp.exp2(x - (high - bias[d])) for d, x in enumerate(parts)]
            total = functools.reduce(
                jnp.add, [jnp.sum(x, axis=0, keepdims=True) for x in exps]
            )
            inverse = 1.0 / total
            dparts = [dprobs[d * T : (d + 1) * T] for d in range(depth)]
            inner = inverse * functools.reduce(
                jnp.add,
                [jnp.sum(x * y, axis=0, keepdims=True) for x, y in zip(exps, dparts)],
            )
            for d in range(depth):
                weights = exps[d] * inverse
                pt[pl.ds(d * T, T), col] = weights.astype(BF)
                dst[pl.ds(d * T, T), col] = (weights * (dparts[d] - inner)).astype(BF)
        q_rows = jnp.concatenate(
            [q_ref[rows, (head * groups + g) * D : (head * groups + g + 1) * D] for g in range(groups)], 0
        )
        do_rows = jnp.concatenate(
            [do_ref[rows, (head * groups + g) * D : (head * groups + g + 1) * D] for g in range(groups)], 0
        )
        dv = jnp.dot(pt[...], do_rows, preferred_element_type=F32)
        dk = jnp.dot(dst[...], q_rows, preferred_element_type=F32) * SCALE
        for d in range(depth):
            acc[place(b, d), :D] += dk[d * T : (d + 1) * T]
            acc[place(b, d), D:] += dv[d * T : (d + 1) * T]
        out_t = lax.dot_general(vb[...], pt[...], TN, preferred_element_type=F32)
        dq_t = lax.dot_general(kb[...], dst[...], TN, preferred_element_type=F32) * SCALE
        for g in range(groups):
            col = pl.ds(g * T, T)
            o_buf[b, :, col] = out_t[:, g * T : (g + 1) * T].T.astype(BF)
            dq_buf[b, :, col] = dq_t[:, g * T : (g + 1) * T].T.astype(BF)
        for copy in out_copies(b):
            copy.start()
        return carry

    lax.fori_loop(0, blocks, block, 0)
    if pairwise:
        sum_ref[...] = acc[:rows_each]
        core_ref[:rows_each] = acc[rows_each : 2 * rows_each].astype(BF)
        core_ref[rows_each:] = acc[3 * rows_each :].astype(BF)
        far_ref[...] = acc[2 * rows_each : 3 * rows_each].astype(BF)
    else:
        sum_ref[...] = acc[...]
    for b in range(blocks):
        for copy in out_copies(b):
            copy.wait()


def attend(info, queries, output_gradient, sources, outputs, head, shards, pairwise):
    tokens = queries.shape[0]
    blocks = tokens // T
    group_blocks = blocks * shards
    depth = min(PATH_DEPTH_MAX, shards)
    groups = QUERY_HEADS // KEY_VALUE_HEADS
    vmem = pl.BlockSpec(memory_space=pltpu.VMEM)
    hbm = pl.BlockSpec(memory_space=pl.ANY)
    chained = outputs is not None
    operands = [
        info,
        pltpu.with_memory_space_constraint(queries, pltpu.VMEM),
        pltpu.with_memory_space_constraint(output_gradient, pltpu.VMEM),
        *sources,
        *(outputs if chained else ()),
    ]
    in_specs = [pl.BlockSpec(memory_space=pltpu.SMEM), vmem, vmem]
    in_specs += [hbm] * (len(operands) - 3)
    full = jax.ShapeDtypeStruct(queries.shape, BF)
    total_rows = tokens * shards
    if pairwise:
        sums = [
            jax.ShapeDtypeStruct((tokens, 2 * D), F32),
            jax.ShapeDtypeStruct((2 * tokens, 2 * D), BF),
            jax.ShapeDtypeStruct((tokens, 2 * D), BF),
        ]
    else:
        sums = [jax.ShapeDtypeStruct((total_rows, 2 * D), F32)]
    first = 3 + len(sources)
    kernel = functools.partial(
        attend_kernel,
        head=head,
        blocks=blocks,
        group_blocks=group_blocks,
        depth=depth,
        groups=groups,
        shards=shards,
        pairwise=pairwise,
        chained=chained,
    )
    flops = 12 * blocks * groups * depth * T * T * D
    return pl.pallas_call(
        kernel,
        in_specs=in_specs,
        out_specs=[hbm, hbm] + [vmem] * len(sums),
        out_shape=[full, full] + sums,
        input_output_aliases={first: 0, first + 1: 1} if chained else {},
        scratch_shapes=[
            pltpu.VMEM((total_rows, 2 * D), BF),
            pltpu.VMEM((total_rows, 2 * D), F32),
            pltpu.VMEM((depth * T, D), BF),
            pltpu.VMEM((depth * T, D), BF),
            pltpu.VMEM((depth * T, groups * T), BF),
            pltpu.VMEM((depth * T, groups * T), BF),
            pltpu.VMEM((blocks, T, groups * D), BF),
            pltpu.VMEM((blocks, T, groups * D), BF),
            pltpu.SMEM((blocks * depth,), jnp.int32),
            pltpu.SemaphoreType.DMA((len(sources),)),
            pltpu.SemaphoreType.DMA((2, blocks)),
        ],
        compiler_params=pltpu.CompilerParams(vmem_limit_bytes=40 * 2**20),
        cost_estimate=pl.CostEstimate(
            flops=2 * flops, bytes_accessed=8 * tokens * groups * D, transcendentals=0
        ),
        name="attend",
    )(*operands)


def body(queries, key_states, value_tensor, output_gradient, parent, block_owner, shards):
    tokens = queries.shape[0]
    kv_heads = key_states.shape[1] // D
    pairwise = shards == 4
    me = lax.axis_index("ctx").astype(jnp.int32)
    info = jnp.concatenate([me[None], parent, block_owner])
    core = [(i, i ^ 1) for i in range(shards)]
    across = [(i, i ^ 2) for i in range(shards)]
    packed = [
        jnp.concatenate([key_states[:, h * D : (h + 1) * D], value_tensor[:, h * D : (h + 1) * D]], 1)
        for h in range(kv_heads)
    ]
    gathered = []
    for own in packed:
        if pairwise:
            far = lax.ppermute(own, "ctx", across)
            near = lax.ppermute(own, "ctx", core)
            gathered.append([own, near, far, lax.ppermute(far, "ctx", core)])
        else:
            gathered.append([lax.all_gather(own, "ctx", axis=0, tiled=True)])
    outputs = None
    summed = []
    for h in range(kv_heads):
        done = attend(info, queries, output_gradient, gathered[h], outputs, h, shards, pairwise)
        outputs = done[:2]
        if pairwise:
            sums, to_core, to_far = done[2:]
            from_core = lax.ppermute(to_core, "ctx", core)
            onward = (to_far.astype(F32) + from_core[tokens:].astype(F32)).astype(BF)
            from_far = lax.ppermute(onward, "ctx", across)
            summed.append(sums + from_core[:tokens].astype(F32) + from_far.astype(F32))
        else:
            summed.append(lax.psum_scatter(done[2], "ctx", scatter_dimension=0, tiled=True))
    d_keys = jnp.concatenate([s[:, :D] for s in summed], 1).astype(BF)
    d_values = jnp.concatenate([s[:, D:] for s in summed], 1).astype(BF)
    return (outputs[0], outputs[1], d_keys, d_values)


def solution(mesh):
    tokens_split = P(("groups", "ctx"), "tp")
    return jax.shard_map(
        functools.partial(body, shards=mesh.shape["ctx"]),
        mesh=mesh,
        in_specs=(tokens_split,) * 4 + (P("groups"),) * 2,
        out_specs=(tokens_split,) * 4,
        check_vma=False,
    )
```

```python
import functools
import math

import jax
import jax.numpy as jnp
from jax import lax
import jax.experimental.pallas as pl
import jax.experimental.pallas.tpu as pltpu
from jax.sharding import PartitionSpec as P

HEAD_SIZE = 128
TREE_BLOCK_SIZE = 128
PATH_DEPTH_MAX = 16
QUERY_HEADS = 64
KEY_VALUE_HEADS = 8

D = HEAD_SIZE
T = TREE_BLOCK_SIZE
NT = (((1,), (1,)), ((), ()))
TN = (((0,), (0,)), ((), ()))
BF = jnp.bfloat16
F32 = jnp.float32
SCALE = 1.0 / math.sqrt(D)
LOG2E = math.log2(math.e)
LINKED = 4
WIDE = 2
ONES = 16
SAFE_EXPONENT = 96.0


def fill_table(info, table, me, blocks, group_blocks, depth):
    for b in range(blocks):
        mine = me * blocks + b

        def find(t, found):
            return jnp.where(info[1 + group_blocks + t] == mine, t, found)

        current = lax.fori_loop(0, group_blocks, find, jnp.int32(0))
        for d in range(depth):
            if d:
                current = jnp.where(current >= 0, info[1 + jnp.maximum(current, 0)], -1)
            owner = info[1 + group_blocks + jnp.maximum(current, 0)]
            table[b * depth + d] = jnp.where(current >= 0, owner, -1)


def attend_kernel(*refs, head, blocks, group_blocks, depth, groups, chained):
    info, q_ref, do_ref, gathered = refs[:4]
    at = 6 if chained else 4
    o_out, dq_out, sum_ref = refs[at : at + 3]
    kv, acc, kb, vb, pt, dst, o_buf, dq_buf, table, kv_sem, out_sem = refs[at + 3 :]
    source_copy = pltpu.make_async_copy(gathered, kv, kv_sem)
    source_copy.start()
    fill_table(info, table, info[0], blocks, group_blocks, depth)
    acc[...] = jnp.zeros_like(acc)
    source_copy.wait()

    tri = lax.broadcasted_iota(jnp.int32, (T, T), 0) <= lax.broadcasted_iota(jnp.int32, (T, T), 1)

    def place(b, d):
        return pl.ds(pl.multiple_of(jnp.maximum(table[b * depth + d], 0) * T, T), T)

    def out_copies(b):
        rows = pl.ds(pl.multiple_of(b * T, T), T)
        columns = pl.ds(head * groups * D, groups * D)
        return (
            pltpu.make_async_copy(o_buf.at[b], o_out.at[rows, columns], out_sem.at[0, b]),
            pltpu.make_async_copy(dq_buf.at[b], dq_out.at[rows, columns], out_sem.at[1, b]),
        )

    def block(b, carry):
        rows = pl.ds(pl.multiple_of(b * T, T), T)
        for d in range(depth):
            kb[pl.ds(d * T, T), :] = kv[place(b, d), :D]
            vb[pl.ds(d * T, T), :] = kv[place(b, d), D:]
        bias = [
            jnp.where(table[b * depth + d] >= 0, 0.0, -jnp.inf).astype(F32) for d in range(depth)
        ]
        for g in range(groups):
            col = pl.ds(g * T, T)
            head_col = pl.ds((head * groups + g) * D, D)
            scores = lax.dot_general(kb[...], q_ref[rows, head_col], NT, preferred_element_type=F32)
            dprobs = lax.dot_general(vb[...], do_ref[rows, head_col], NT, preferred_element_type=F32)
            parts = [scores[d * T : (d + 1) * T] * (SCALE * LOG2E) for d in range(depth)]
            parts[0] = jnp.where(tri, parts[0], -jnp.inf)
            highs = [jnp.max(x, axis=0, keepdims=True) + bias[d] for d, x in enumerate(parts)]
            high = functools.reduce(jnp.maximum, highs)
            exps = [jnp.exp2(x - (high - bias[d])) for d, x in enumerate(parts)]
            total = functools.reduce(
                jnp.add, [jnp.sum(x, axis=0, keepdims=True) for x in exps]
            )
            inverse = 1.0 / total
            dparts = [dprobs[d * T : (d + 1) * T] for d in range(depth)]
            inner = inverse * functools.reduce(
                jnp.add,
                [jnp.sum(x * y, axis=0, keepdims=True) for x, y in zip(exps, dparts)],
            )
            for d in range(depth):
                weights = exps[d] * inverse
                pt[pl.ds(d * T, T), col] = weights.astype(BF)
                dst[pl.ds(d * T, T), col] = (weights * (dparts[d] - inner)).astype(BF)
        q_rows = jnp.concatenate(
            [q_ref[rows, (head * groups + g) * D : (head * groups + g + 1) * D] for g in range(groups)], 0
        )
        do_rows = jnp.concatenate(
            [do_ref[rows, (head * groups + g) * D : (head * groups + g + 1) * D] for g in range(groups)], 0
        )
        dv = jnp.dot(pt[...], do_rows, preferred_element_type=F32)
        dk = jnp.dot(dst[...], q_rows, preferred_element_type=F32) * SCALE
        for d in range(depth):
            acc[place(b, d), :D] += dk[d * T : (d + 1) * T]
            acc[place(b, d), D:] += dv[d * T : (d + 1) * T]
        out_t = lax.dot_general(vb[...], pt[...], TN, preferred_element_type=F32)
        dq_t = lax.dot_general(kb[...], dst[...], TN, preferred_element_type=F32) * SCALE
        for g in range(groups):
            col = pl.ds(g * T, T)
            o_buf[b, :, col] = out_t[:, g * T : (g + 1) * T].T.astype(BF)
            dq_buf[b, :, col] = dq_t[:, g * T : (g + 1) * T].T.astype(BF)
        for copy in out_copies(b):
            copy.start()
        return carry

    lax.fori_loop(0, blocks, block, 0)
    sum_ref[...] = acc[...]
    for b in range(blocks):
        for copy in out_copies(b):
            copy.wait()


def attend(info, queries, output_gradient, gathered, outputs, head, shards):
    tokens = queries.shape[0]
    blocks = tokens // T
    group_blocks = blocks * shards
    depth = min(PATH_DEPTH_MAX, shards)
    groups = QUERY_HEADS // KEY_VALUE_HEADS
    vmem = pl.BlockSpec(memory_space=pltpu.VMEM)
    hbm = pl.BlockSpec(memory_space=pl.ANY)
    chained = outputs is not None
    operands = [
        info,
        pltpu.with_memory_space_constraint(queries, pltpu.VMEM),
        pltpu.with_memory_space_constraint(output_gradient, pltpu.VMEM),
        gathered,
        *(outputs if chained else ()),
    ]
    in_specs = [pl.BlockSpec(memory_space=pltpu.SMEM), vmem, vmem]
    in_specs += [hbm] * (len(operands) - 3)
    full = jax.ShapeDtypeStruct(queries.shape, BF)
    total_rows = tokens * shards
    sums = [jax.ShapeDtypeStruct((total_rows, 2 * D), F32)]
    kernel = functools.partial(
        attend_kernel,
        head=head,
        blocks=blocks,
        group_blocks=group_blocks,
        depth=depth,
        groups=groups,
        chained=chained,
    )
    flops = 12 * blocks * groups * depth * T * T * D
    return pl.pallas_call(
        kernel,
        in_specs=in_specs,
        out_specs=[hbm, hbm] + [vmem] * len(sums),
        out_shape=[full, full] + sums,
        input_output_aliases={4: 0, 5: 1} if chained else {},
        scratch_shapes=[
            pltpu.VMEM((total_rows, 2 * D), BF),
            pltpu.VMEM((total_rows, 2 * D), F32),
            pltpu.VMEM((depth * T, D), BF),
            pltpu.VMEM((depth * T, D), BF),
            pltpu.VMEM((depth * T, groups * T), BF),
            pltpu.VMEM((depth * T, groups * T), BF),
            pltpu.VMEM((blocks, T, groups * D), BF),
            pltpu.VMEM((blocks, T, groups * D), BF),
            pltpu.SMEM((blocks * depth,), jnp.int32),
            pltpu.SemaphoreType.DMA,
            pltpu.SemaphoreType.DMA((2, blocks)),
        ],
        compiler_params=pltpu.CompilerParams(vmem_limit_bytes=40 * 2**20),
        cost_estimate=pl.CostEstimate(
            flops=2 * flops, bytes_accessed=8 * tokens * groups * D, transcendentals=0
        ),
        name="attend",
    )(*operands)


def relation_table(info, table, blocks, depth):
    me = info[0]
    group_blocks = blocks * LINKED
    for b in range(blocks):
        for r in range(LINKED):
            table[b * LINKED + r] = -1
        current = jnp.int32(0)
        for t in range(group_blocks):
            current = jnp.where(info[1 + group_blocks + t] == me * blocks + b, t, current)
        for d in range(depth):
            if d:
                current = jnp.where(current >= 0, info[1 + jnp.maximum(current, 0)], -1)
            owner = info[1 + group_blocks + jnp.maximum(current, 0)]
            shard = lax.div(owner, jnp.int32(blocks))
            slot = b * LINKED + (shard ^ me)
            table[slot] = jnp.where(current >= 0, owner - shard * blocks, table[slot])


def row_span(index):
    return pl.ds(pl.multiple_of(jnp.maximum(index, 0) * T, T), T)


def live_factor(index):
    return jnp.where(index >= 0, 1.0, 0.0).astype(BF)


def norm_top(rows):
    wide = rows.astype(F32)
    return jnp.max(jnp.sum(wide * wide, axis=1, keepdims=True))


def causal(width):
    keys = lax.broadcasted_iota(jnp.int32, (T, T), 0)
    queries = lax.broadcasted_iota(jnp.int32, (T, T), 1)
    return jnp.concatenate([keys <= queries] * width, 1)


def near_kernel(*refs, blocks, heads, groups, depth):
    info, q_in, do_in = refs[:3]
    own = refs[3 : 3 + heads]
    near = refs[3 + heads : 3 + 2 * heads]
    table, top, q_v, do_v, qt, dt, kbn, vtn, pn, dpn, on = refs[3 + 2 * heads : 14 + 2 * heads]
    kv, vb, row_sem, kv_sem = refs[14 + 2 * heads :]

    def row_copies(b):
        rows = pl.ds(b * T, T)
        return (
            pltpu.make_async_copy(q_in.at[rows], q_v.at[rows], row_sem.at[0, b]),
            pltpu.make_async_copy(do_in.at[rows], do_v.at[rows], row_sem.at[1, b]),
        )

    kv_copies = [
        pltpu.make_async_copy(source, kv.at[i], kv_sem.at[i]) for i, source in enumerate(own + near)
    ]
    for copy in kv_copies:
        copy.start()
    for b in range(blocks):
        for copy in row_copies(b):
            copy.start()
    relation_table(info, table, blocks, depth)
    for copy in kv_copies:
        copy.wait()
    for h in range(heads):
        top[1 + h] = jnp.maximum(norm_top(kv[h, :, :D]), norm_top(kv[heads + h, :, :D]))
    highest = jnp.zeros((1, heads * groups * T), F32)
    for b in range(blocks):
        for copy in row_copies(b):
            copy.wait()
        for g in range(heads * groups):
            col = pl.ds(g * D, D)
            qt[b, :, col] = q_v[pl.ds(b * T, T), col].T
            dt[b, :, col] = do_v[pl.ds(b * T, T), col].T
        wide = qt[b].astype(F32)
        highest = jnp.maximum(highest, jnp.sum(wide * wide, axis=0, keepdims=True))
    top[0] = jnp.max(highest)
    tri = causal(WIDE)
    for h in range(heads):
        for b in range(blocks):
            for r in range(2):
                index = table[b * LINKED + r]
                here = pl.ds(r * T, T)
                source = kv.at[r * heads + h]
                kbn[h, b, here, :] = source[row_span(index), :D] * live_factor(index)
                values = source[row_span(index), D:] * live_factor(index)
                vb[here, :] = values
                vtn[h, b, :D, here] = values.T
                vtn[h, b, D:, here] = jnp.full((ONES, T), live_factor(index), BF)
            for j in range(0, groups, WIDE):
                col = pl.ds(j * T, WIDE * T)
                head_col = pl.ds((h * groups + j) * D, WIDE * D)
                scores = jnp.dot(kbn[h, b], qt[b, :, head_col], preferred_element_type=F32)
                exps = jnp.exp2(scores * (SCALE * LOG2E))
                pn[h, b, :T, col] = jnp.where(tri, exps[:T], 0.0).astype(BF)
                pn[h, b, T:, col] = exps[T:].astype(BF)
                dpn[h, b, :, col] = jnp.dot(vb[...], dt[b, :, head_col], preferred_element_type=F32)
                on[h, b, :, col] = jnp.dot(
                    vtn[h, b], pn[h, b, :, col], preferred_element_type=F32
                )[: D + 8]


def far_kernel(*refs, head, blocks, groups, chained):
    table, top, q_v, do_v, qt, dt, kbn, vtn, pn, dpn, on = refs[:11]
    sources = refs[11:13]
    at = 14 if chained else 13
    o_out, pt, dst, kb, far_ref, diagonal_ref = refs[at : at + 6]
    kv, vb, vt, acc, o_buf, kv_sem, out_sem = refs[at + 6 :]
    tokens = blocks * T
    kv_copies = [
        pltpu.make_async_copy(source, kv.at[i], kv_sem.at[i]) for i, source in enumerate(sources)
    ]
    for copy in kv_copies:
        copy.start()
    acc[...] = jnp.zeros_like(acc)
    for b in range(blocks):
        kb[b, : 2 * T, :] = kbn[head, b]
    for copy in kv_copies:
        copy.wait()
    for b in range(blocks):
        for r in range(2):
            index = table[b * LINKED + 2 + r]
            here = pl.ds(r * T, T)
            kb[b, pl.ds((2 + r) * T, T), :] = kv[r, row_span(index), :D] * live_factor(index)
            values = kv[r, row_span(index), D:] * live_factor(index)
            vb[b, here, :] = values
            vt[b, :D, here] = values.T
            vt[b, D:, here] = jnp.full((ONES, T), live_factor(index), BF)

    def out_copy(b):
        rows = pl.ds(pl.multiple_of(b * T, T), T)
        columns = pl.ds(head * groups * D, groups * D)
        return pltpu.make_async_copy(o_buf.at[b], o_out.at[rows, columns], out_sem.at[b])

    keys_top = jnp.maximum(norm_top(kv[0, :, :D]), norm_top(kv[1, :, :D]))
    keys_top = jnp.maximum(keys_top, top[1 + head])
    safe = top[0] * keys_top <= (SAFE_EXPONENT / (SCALE * LOG2E)) ** 2

    @pl.when(safe)
    def _():
        for b in range(blocks):
            for j in range(0, groups, WIDE):
                col = pl.ds(j * T, WIDE * T)
                head_col = pl.ds((head * groups + j) * D, WIDE * D)
                scores = jnp.dot(kb[b, 2 * T :], qt[b, :, head_col], preferred_element_type=F32)
                exps = jnp.exp2(scores * (SCALE * LOG2E)).astype(BF)
                pt[b, 2 * T :, col] = exps
                sums = jnp.dot(vt[b], pt[b, 2 * T :, col], preferred_element_type=F32)
                sums = sums[: D + 8] + on[head, b, :, col]
                inverse = 1.0 / sums[D : D + 1]
                out_t = sums[:D] * inverse
                inner = jnp.sum(out_t * dt[b, :, head_col].astype(F32), axis=0, keepdims=True)
                for w in range(WIDE):
                    o_buf[b, :, pl.ds((j + w) * D, D)] = out_t[:, w * T : (w + 1) * T].astype(BF).T
                dprobs = jnp.dot(vb[b], dt[b, :, head_col], preferred_element_type=F32)
                weights = pn[head, b, :, col].astype(F32) * inverse
                pt[b, : 2 * T, col] = weights.astype(BF)
                dst[b, : 2 * T, col] = (weights * (dpn[head, b, :, col] - inner)).astype(BF)
                weights = pt[b, 2 * T :, col].astype(F32) * inverse
                pt[b, 2 * T :, col] = weights.astype(BF)
                dst[b, 2 * T :, col] = (weights * (dprobs - inner)).astype(BF)
            out_copy(b).start()

    @pl.when(jnp.logical_not(safe))
    def _():
        tri = causal(1)

        def block(b, carry):
            bias = [
                jnp.where(table[b * LINKED + r] >= 0, 0.0, -jnp.inf).astype(F32)
                for r in range(LINKED)
            ]
            for g in range(groups):
                col = pl.ds(g * T, T)
                head_col = pl.ds((head * groups + g) * D, D)
                scores = jnp.dot(kb[b], qt[b, :, head_col], preferred_element_type=F32)
                dprobs = jnp.dot(vb[b], dt[b, :, head_col], preferred_element_type=F32)
                dparts = [dpn[head, b, pl.ds(r * T, T), col] for r in range(2)]
                dparts += [dprobs[:T], dprobs[T:]]
                parts = [scores[r * T : (r + 1) * T] * (SCALE * LOG2E) for r in range(LINKED)]
                parts[0] = jnp.where(tri, parts[0], -jnp.inf)
                highs = [jnp.max(x, axis=0, keepdims=True) + bias[r] for r, x in enumerate(parts)]
                high = functools.reduce(jnp.maximum, highs)
                exps = [jnp.exp2(x - (high - bias[r])) for r, x in enumerate(parts)]
                total = functools.reduce(
                    jnp.add, [jnp.sum(x, axis=0, keepdims=True) for x in exps]
                )
                inverse = 1.0 / total
                inner = inverse * functools.reduce(
                    jnp.add,
                    [jnp.sum(x * y, axis=0, keepdims=True) for x, y in zip(exps, dparts)],
                )
                for r in range(LINKED):
                    weights = exps[r] * inverse
                    here = pl.ds(r * T, T)
                    pt[b, here, col] = weights.astype(BF)
                    dst[b, here, col] = (weights * (dparts[r] - inner)).astype(BF)
                out_t = jnp.dot(
                    vtn[head, b], pt[b, : 2 * T, col], preferred_element_type=F32
                ) + jnp.dot(vt[b], pt[b, 2 * T :, col], preferred_element_type=F32)
                o_buf[b, :, pl.ds(g * D, D)] = out_t[:D].astype(BF).T
            out_copy(b).start()
            return carry

        lax.fori_loop(0, blocks, block, 0)

    for b in range(blocks):
        rows = pl.ds(b * T, T)
        q_rows, do_rows = (
            jnp.concatenate(
                [ref[rows, pl.ds((head * groups + g) * D, D)] for g in range(groups)], 0
            )
            for ref in (q_v, do_v)
        )
        dv = jnp.dot(pt[b, 2 * T :], do_rows, preferred_element_type=F32)
        dk = jnp.dot(dst[b, 2 * T :], q_rows, preferred_element_type=F32) * SCALE
        for r in range(2):
            index = table[b * LINKED + 2 + r]
            here = row_span(jnp.where(index >= 0, index + r * blocks, 2 * blocks))
            acc[here, :D] += dk[r * T : (r + 1) * T]
            acc[here, D:] += dv[r * T : (r + 1) * T]
    far_ref[...] = acc[:tokens].astype(BF)
    diagonal_ref[...] = acc[tokens : 2 * tokens].astype(BF)
    for b in range(blocks):
        out_copy(b).wait()


def tail_kernel(*refs, blocks, heads, groups):
    table, q_v, do_v = refs[:3]
    probs = refs[3 : 3 + 3 * heads]
    dq_out, own_ref, core_ref = refs[3 + 3 * heads : 6 + 3 * heads]
    acc, dq_buf, out_sem = refs[6 + 3 * heads :]
    tokens = blocks * T

    def out_copy(h, b):
        rows = pl.ds(b * T, T)
        columns = pl.ds(h * groups * D, groups * D)
        return pltpu.make_async_copy(dq_buf.at[h, b], dq_out.at[rows, columns], out_sem.at[h, b])

    acc[...] = jnp.zeros_like(acc)
    for h in range(heads):
        pt, dst, kb = probs[3 * h : 3 * h + 3]
        key_col = pl.ds(h * D, D)
        value_col = pl.ds((heads + h) * D, D)
        for b in range(blocks):
            rows = pl.ds(b * T, T)
            q_rows, do_rows = (
                jnp.concatenate(
                    [ref[rows, pl.ds((h * groups + g) * D, D)] for g in range(groups)], 0
                )
                for ref in (q_v, do_v)
            )
            dv = jnp.dot(pt[b, : 2 * T], do_rows, preferred_element_type=F32)
            dk = jnp.dot(dst[b, : 2 * T], q_rows, preferred_element_type=F32) * SCALE
            own_ref[rows, key_col] = dk[:T]
            own_ref[rows, value_col] = dv[:T]
            index = table[b * LINKED + 1]
            here = row_span(jnp.where(index >= 0, index, blocks))
            acc[here, key_col] += dk[T:]
            acc[here, value_col] += dv[T:]
        core_ref[:, key_col] = acc[:tokens, key_col].astype(BF)
        core_ref[:, value_col] = acc[:tokens, value_col].astype(BF)
        for b in range(blocks):
            for j in range(0, groups, WIDE):
                dq_t = SCALE * lax.dot_general(
                    kb[b], dst[b, :, pl.ds(j * T, WIDE * T)], TN, preferred_element_type=F32
                )
                for w in range(WIDE):
                    dq_buf[h, b, :, pl.ds((j + w) * D, D)] = (
                        dq_t[:, w * T : (w + 1) * T].astype(BF).T
                    )
            out_copy(h, b).start()
    for h in range(heads):
        for b in range(blocks):
            out_copy(h, b).wait()


def linked_body(info, queries, output_gradient, packed):
    tokens = queries.shape[0]
    heads = len(packed)
    blocks = tokens // T
    groups = QUERY_HEADS // KEY_VALUE_HEADS
    width = groups * T
    depth = min(PATH_DEPTH_MAX, LINKED)
    core = [(i, i ^ 1) for i in range(LINKED)]
    across = [(i, i ^ 2) for i in range(LINKED)]
    far = [lax.ppermute(own, "ctx", across) for own in packed]
    near = [lax.ppermute(own, "ctx", core) for own in packed]
    diagonal = [lax.ppermute(x, "ctx", core) for x in far]

    vmem = pl.BlockSpec(memory_space=pltpu.VMEM)
    smem = pl.BlockSpec(memory_space=pltpu.SMEM)
    hbm = pl.BlockSpec(memory_space=pl.ANY)
    kept = pltpu.VMEM

    def keep(x):
        return pltpu.with_memory_space_constraint(x, pltpu.VMEM)

    shared = pl.pallas_call(
        functools.partial(near_kernel, blocks=blocks, heads=heads, groups=groups, depth=depth),
        in_specs=[smem] + [hbm] * (2 + 2 * heads),
        out_specs=[smem, smem] + [vmem] * 9,
        out_shape=[
            jax.ShapeDtypeStruct((blocks * LINKED,), jnp.int32),
            jax.ShapeDtypeStruct((1 + heads,), F32),
            kept(queries.shape, BF),
            kept(queries.shape, BF),
            kept((blocks, D, heads * width), BF),
            kept((blocks, D, heads * width), BF),
            kept((heads, blocks, 2 * T, D), BF),
            kept((heads, blocks, D + ONES, 2 * T), BF),
            kept((heads, blocks, 2 * T, width), BF),
            kept((heads, blocks, 2 * T, width), F32),
            kept((heads, blocks, D + 8, width), F32),
        ],
        scratch_shapes=[
            pltpu.VMEM((2 * heads, tokens, 2 * D), BF),
            pltpu.VMEM((2 * T, D), BF),
            pltpu.SemaphoreType.DMA((2, blocks)),
            pltpu.SemaphoreType.DMA((2 * heads,)),
        ],
        compiler_params=pltpu.CompilerParams(vmem_limit_bytes=12 * 2**20),
        name="near",
    )(info, queries, output_gradient, *packed, *near)
    table, top = shared[:2]
    local = [keep(x) for x in shared[2:]]

    attended = None
    probs = []
    far_sums = []
    for h in range(heads):
        chained = attended is not None
        operands = [table, top, *local, far[h], diagonal[h]]
        done = pl.pallas_call(
            functools.partial(far_kernel, head=h, blocks=blocks, groups=groups, chained=chained),
            in_specs=[smem, smem] + [vmem] * 9 + [hbm] * (3 if chained else 2),
            out_specs=[hbm] + [vmem] * 5,
            out_shape=[
                jax.ShapeDtypeStruct(queries.shape, BF),
                kept((blocks, LINKED * T, width), BF),
                kept((blocks, LINKED * T, width), BF),
                kept((blocks, LINKED * T, D), BF),
                jax.ShapeDtypeStruct((tokens, 2 * D), BF),
                jax.ShapeDtypeStruct((tokens, 2 * D), BF),
            ],
            input_output_aliases={len(operands): 0} if chained else {},
            scratch_shapes=[
                pltpu.VMEM((2, tokens, 2 * D), BF),
                pltpu.VMEM((blocks, 2 * T, D), BF),
                pltpu.VMEM((blocks, D + ONES, 2 * T), BF),
                pltpu.VMEM((2 * tokens + T, 2 * D), F32),
                pltpu.VMEM((blocks, T, groups * D), BF),
                pltpu.SemaphoreType.DMA((2,)),
                pltpu.SemaphoreType.DMA((blocks,)),
            ],
            compiler_params=pltpu.CompilerParams(vmem_limit_bytes=12 * 2**20),
            name="far",
        )(*operands, *([attended] if chained else []))
        attended = done[0]
        probs += [keep(x) for x in done[1:4]]
        to_far, to_diagonal = done[4:]
        onward = lax.ppermute(to_diagonal, "ctx", core)
        onward = (to_far.astype(F32) + onward.astype(F32)).astype(BF)
        far_sums.append(lax.ppermute(onward, "ctx", across))

    d_queries, own_sums, to_core = pl.pallas_call(
        functools.partial(tail_kernel, blocks=blocks, heads=heads, groups=groups),
        in_specs=[smem] + [vmem] * (2 + 3 * heads),
        out_specs=[hbm, vmem, vmem],
        out_shape=[
            jax.ShapeDtypeStruct(queries.shape, BF),
            jax.ShapeDtypeStruct((tokens, 2 * heads * D), F32),
            jax.ShapeDtypeStruct((tokens, 2 * heads * D), BF),
        ],
        scratch_shapes=[
            pltpu.VMEM((tokens + T, 2 * heads * D), F32),
            pltpu.VMEM((heads, blocks, T, groups * D), BF),
            pltpu.SemaphoreType.DMA((heads, blocks)),
        ],
        compiler_params=pltpu.CompilerParams(vmem_limit_bytes=12 * 2**20),
        name="tail",
    )(table, local[0], local[1], *probs)
    near_sums = own_sums + lax.ppermute(to_core, "ctx", core).astype(F32)
    d_keys = near_sums[:, : heads * D] + jnp.concatenate(
        [x[:, :D].astype(F32) for x in far_sums], 1
    )
    d_values = near_sums[:, heads * D :] + jnp.concatenate(
        [x[:, D:].astype(F32) for x in far_sums], 1
    )
    return attended, d_queries, d_keys.astype(BF), d_values.astype(BF)


def body(queries, key_states, value_tensor, output_gradient, parent, block_owner, shards):
    heads = key_states.shape[1] // D
    me = lax.axis_index("ctx").astype(jnp.int32)
    info = jnp.concatenate([me[None], parent, block_owner])
    packed = [
        jnp.concatenate([key_states[:, h * D : (h + 1) * D], value_tensor[:, h * D : (h + 1) * D]], 1)
        for h in range(heads)
    ]
    if shards == LINKED:
        return linked_body(info, queries, output_gradient, packed)
    outputs = None
    summed = []
    for h in range(heads):
        gathered = lax.all_gather(packed[h], "ctx", axis=0, tiled=True)
        done = attend(info, queries, output_gradient, gathered, outputs, h, shards)
        outputs = done[:2]
        summed.append(lax.psum_scatter(done[2], "ctx", scatter_dimension=0, tiled=True))
    d_keys = jnp.concatenate([s[:, :D] for s in summed], 1).astype(BF)
    d_values = jnp.concatenate([s[:, D:] for s in summed], 1).astype(BF)
    return (outputs[0], outputs[1], d_keys, d_values)


def solution(mesh):
    tokens_split = P(("groups", "ctx"), "tp")
    return jax.shard_map(
        functools.partial(body, shards=mesh.shape["ctx"]),
        mesh=mesh,
        in_specs=(tokens_split,) * 4 + (P("groups"),) * 2,
        out_specs=(tokens_split,) * 4,
        check_vma=False,
    )
```

```python
import functools
import math

import jax
import jax.numpy as jnp
from jax import lax
import jax.experimental.pallas as pl
import jax.experimental.pallas.tpu as pltpu
from jax.sharding import PartitionSpec as P

HEAD_SIZE = 128
TREE_BLOCK_SIZE = 128
PATH_DEPTH_MAX = 16
QUERY_HEADS = 64
KEY_VALUE_HEADS = 8

D = HEAD_SIZE
T = TREE_BLOCK_SIZE
NT = (((1,), (1,)), ((), ()))
TN = (((0,), (0,)), ((), ()))
BF = jnp.bfloat16
F32 = jnp.float32
SCALE = 1.0 / math.sqrt(D)
LOG2E = math.log2(math.e)
LINKED = 4
WIDE = 2
ONES = 16
SAFE_EXPONENT = 96.0


def fill_table(info, table, me, blocks, group_blocks, depth):
    for b in range(blocks):
        mine = me * blocks + b

        def find(t, found):
            return jnp.where(info[1 + group_blocks + t] == mine, t, found)

        current = lax.fori_loop(0, group_blocks, find, jnp.int32(0))
        for d in range(depth):
            if d:
                current = jnp.where(current >= 0, info[1 + jnp.maximum(current, 0)], -1)
            owner = info[1 + group_blocks + jnp.maximum(current, 0)]
            table[b * depth + d] = jnp.where(current >= 0, owner, -1)


def attend_kernel(*refs, head, blocks, group_blocks, depth, groups, chained):
    info, q_ref, do_ref, gathered = refs[:4]
    at = 6 if chained else 4
    o_out, dq_out, sum_ref = refs[at : at + 3]
    kv, acc, kb, vb, pt, dst, o_buf, dq_buf, table, kv_sem, out_sem = refs[at + 3 :]
    source_copy = pltpu.make_async_copy(gathered, kv, kv_sem)
    source_copy.start()
    fill_table(info, table, info[0], blocks, group_blocks, depth)
    acc[...] = jnp.zeros_like(acc)
    source_copy.wait()

    tri = lax.broadcasted_iota(jnp.int32, (T, T), 0) <= lax.broadcasted_iota(jnp.int32, (T, T), 1)

    def place(b, d):
        return pl.ds(pl.multiple_of(jnp.maximum(table[b * depth + d], 0) * T, T), T)

    def out_copies(b):
        rows = pl.ds(pl.multiple_of(b * T, T), T)
        columns = pl.ds(head * groups * D, groups * D)
        return (
            pltpu.make_async_copy(o_buf.at[b], o_out.at[rows, columns], out_sem.at[0, b]),
            pltpu.make_async_copy(dq_buf.at[b], dq_out.at[rows, columns], out_sem.at[1, b]),
        )

    def block(b, carry):
        rows = pl.ds(pl.multiple_of(b * T, T), T)
        for d in range(depth):
            kb[pl.ds(d * T, T), :] = kv[place(b, d), :D]
            vb[pl.ds(d * T, T), :] = kv[place(b, d), D:]
        bias = [
            jnp.where(table[b * depth + d] >= 0, 0.0, -jnp.inf).astype(F32) for d in range(depth)
        ]
        for g in range(groups):
            col = pl.ds(g * T, T)
            head_col = pl.ds((head * groups + g) * D, D)
            scores = lax.dot_general(kb[...], q_ref[rows, head_col], NT, preferred_element_type=F32)
            dprobs = lax.dot_general(vb[...], do_ref[rows, head_col], NT, preferred_element_type=F32)
            parts = [scores[d * T : (d + 1) * T] * (SCALE * LOG2E) for d in range(depth)]
            parts[0] = jnp.where(tri, parts[0], -jnp.inf)
            highs = [jnp.max(x, axis=0, keepdims=True) + bias[d] for d, x in enumerate(parts)]
            high = functools.reduce(jnp.maximum, highs)
            exps = [jnp.exp2(x - (high - bias[d])) for d, x in enumerate(parts)]
            total = functools.reduce(
                jnp.add, [jnp.sum(x, axis=0, keepdims=True) for x in exps]
            )
            inverse = 1.0 / total
            dparts = [dprobs[d * T : (d + 1) * T] for d in range(depth)]
            inner = inverse * functools.reduce(
                jnp.add,
                [jnp.sum(x * y, axis=0, keepdims=True) for x, y in zip(exps, dparts)],
            )
            for d in range(depth):
                weights = exps[d] * inverse
                pt[pl.ds(d * T, T), col] = weights.astype(BF)
                dst[pl.ds(d * T, T), col] = (weights * (dparts[d] - inner)).astype(BF)
        q_rows = jnp.concatenate(
            [q_ref[rows, (head * groups + g) * D : (head * groups + g + 1) * D] for g in range(groups)], 0
        )
        do_rows = jnp.concatenate(
            [do_ref[rows, (head * groups + g) * D : (head * groups + g + 1) * D] for g in range(groups)], 0
        )
        dv = jnp.dot(pt[...], do_rows, preferred_element_type=F32)
        dk = jnp.dot(dst[...], q_rows, preferred_element_type=F32) * SCALE
        for d in range(depth):
            acc[place(b, d), :D] += dk[d * T : (d + 1) * T]
            acc[place(b, d), D:] += dv[d * T : (d + 1) * T]
        out_t = lax.dot_general(vb[...], pt[...], TN, preferred_element_type=F32)
        dq_t = lax.dot_general(kb[...], dst[...], TN, preferred_element_type=F32) * SCALE
        for g in range(groups):
            col = pl.ds(g * T, T)
            o_buf[b, :, col] = out_t[:, g * T : (g + 1) * T].T.astype(BF)
            dq_buf[b, :, col] = dq_t[:, g * T : (g + 1) * T].T.astype(BF)
        for copy in out_copies(b):
            copy.start()
        return carry

    lax.fori_loop(0, blocks, block, 0)
    sum_ref[...] = acc[...]
    for b in range(blocks):
        for copy in out_copies(b):
            copy.wait()


def attend(info, queries, output_gradient, gathered, outputs, head, shards):
    tokens = queries.shape[0]
    blocks = tokens // T
    group_blocks = blocks * shards
    depth = min(PATH_DEPTH_MAX, shards)
    groups = QUERY_HEADS // KEY_VALUE_HEADS
    vmem = pl.BlockSpec(memory_space=pltpu.VMEM)
    hbm = pl.BlockSpec(memory_space=pl.ANY)
    chained = outputs is not None
    operands = [
        info,
        pltpu.with_memory_space_constraint(queries, pltpu.VMEM),
        pltpu.with_memory_space_constraint(output_gradient, pltpu.VMEM),
        gathered,
        *(outputs if chained else ()),
    ]
    in_specs = [pl.BlockSpec(memory_space=pltpu.SMEM), vmem, vmem]
    in_specs += [hbm] * (len(operands) - 3)
    full = jax.ShapeDtypeStruct(queries.shape, BF)
    total_rows = tokens * shards
    sums = [jax.ShapeDtypeStruct((total_rows, 2 * D), F32)]
    kernel = functools.partial(
        attend_kernel,
        head=head,
        blocks=blocks,
        group_blocks=group_blocks,
        depth=depth,
        groups=groups,
        chained=chained,
    )
    flops = 12 * blocks * groups * depth * T * T * D
    return pl.pallas_call(
        kernel,
        in_specs=in_specs,
        out_specs=[hbm, hbm] + [vmem] * len(sums),
        out_shape=[full, full] + sums,
        input_output_aliases={4: 0, 5: 1} if chained else {},
        scratch_shapes=[
            pltpu.VMEM((total_rows, 2 * D), BF),
            pltpu.VMEM((total_rows, 2 * D), F32),
            pltpu.VMEM((depth * T, D), BF),
            pltpu.VMEM((depth * T, D), BF),
            pltpu.VMEM((depth * T, groups * T), BF),
            pltpu.VMEM((depth * T, groups * T), BF),
            pltpu.VMEM((blocks, T, groups * D), BF),
            pltpu.VMEM((blocks, T, groups * D), BF),
            pltpu.SMEM((blocks * depth,), jnp.int32),
            pltpu.SemaphoreType.DMA,
            pltpu.SemaphoreType.DMA((2, blocks)),
        ],
        compiler_params=pltpu.CompilerParams(vmem_limit_bytes=40 * 2**20),
        cost_estimate=pl.CostEstimate(
            flops=2 * flops, bytes_accessed=8 * tokens * groups * D, transcendentals=0
        ),
        name="attend",
    )(*operands)


def relation_table(info, table, blocks, depth):
    me = info[0]
    group_blocks = blocks * LINKED
    for b in range(blocks):
        for r in range(LINKED):
            table[b * LINKED + r] = -1
        current = jnp.int32(0)
        for t in range(group_blocks):
            current = jnp.where(info[1 + group_blocks + t] == me * blocks + b, t, current)
        for d in range(depth):
            if d:
                current = jnp.where(current >= 0, info[1 + jnp.maximum(current, 0)], -1)
            owner = info[1 + group_blocks + jnp.maximum(current, 0)]
            shard = lax.div(owner, jnp.int32(blocks))
            slot = b * LINKED + (shard ^ me)
            table[slot] = jnp.where(current >= 0, owner - shard * blocks, table[slot])


def row_span(index):
    return pl.ds(pl.multiple_of(jnp.maximum(index, 0) * T, T), T)


def live_factor(index):
    return jnp.where(index >= 0, 1.0, 0.0).astype(BF)


def norm_top(rows):
    wide = rows.astype(F32)
    return jnp.max(jnp.sum(wide * wide, axis=1, keepdims=True))


def causal(width):
    keys = lax.broadcasted_iota(jnp.int32, (T, T), 0)
    queries = lax.broadcasted_iota(jnp.int32, (T, T), 1)
    return jnp.concatenate([keys <= queries] * width, 1)


def near_kernel(*refs, head, blocks, heads, groups, depth):
    if head == 0:
        info, q_in, do_in, own, near = refs[:5]
        table, top, q_v, do_v, qt, dt, kbn, vtn, pn, dpn, on = refs[5:16]
        kv, vb, kv_sem, row_sem = refs[16:]
    else:
        table, qt, dt, own, near = refs[:5]
        top, kbn, vtn, pn, dpn, on = refs[5:11]
        kv, vb, kv_sem = refs[11:]

    kv_copies = [
        pltpu.make_async_copy(source, kv.at[i], kv_sem.at[i]) for i, source in enumerate((own, near))
    ]
    for copy in kv_copies:
        copy.start()
    if head == 0:

        def row_copies(b):
            rows = pl.ds(b * T, T)
            return (
                pltpu.make_async_copy(q_in.at[rows], q_v.at[rows], row_sem.at[0, b]),
                pltpu.make_async_copy(do_in.at[rows], do_v.at[rows], row_sem.at[1, b]),
            )

        for b in range(blocks):
            for copy in row_copies(b):
                copy.start()
        relation_table(info, table, blocks, depth)
        highest = jnp.zeros((1, heads * groups * T), F32)
        for b in range(blocks):
            for copy in row_copies(b):
                copy.wait()
            for g in range(heads * groups):
                col = pl.ds(g * D, D)
                qt[b, :, col] = q_v[pl.ds(b * T, T), col].T
                dt[b, :, col] = do_v[pl.ds(b * T, T), col].T
            wide = qt[b].astype(F32)
            highest = jnp.maximum(highest, jnp.sum(wide * wide, axis=0, keepdims=True))
        top[0] = jnp.max(highest)
    for copy in kv_copies:
        copy.wait()
    top[1 if head == 0 else 0] = jnp.maximum(norm_top(kv[0, :, :D]), norm_top(kv[1, :, :D]))
    for b in range(blocks):
        for r in range(2):
            index = table[b * LINKED + r]
            here = pl.ds(r * T, T)
            kbn[b, here, :] = kv[r, row_span(index), :D] * live_factor(index)
            values = kv[r, row_span(index), D:] * live_factor(index)
            vb[b, here, :] = values
            vtn[b, :D, here] = values.T
            vtn[b, D:, here] = jnp.full((ONES, T), live_factor(index), BF)
    tri = causal(WIDE)
    pieces = [
        (b, pl.ds(j * T, WIDE * T), pl.ds((head * groups + j) * D, WIDE * D))
        for b in range(blocks)
        for j in range(0, groups, WIDE)
    ]
    for b, col, head_col in pieces:
        scores = jnp.dot(kbn[b], qt[b, :, head_col], preferred_element_type=F32)
        exps = jnp.exp2(scores * (SCALE * LOG2E))
        pn[b, :T, col] = jnp.where(tri, exps[:T], 0.0).astype(BF)
        pn[b, T:, col] = exps[T:].astype(BF)
    for b, col, head_col in pieces:
        dpn[b, :, col] = jnp.dot(vb[b], dt[b, :, head_col], preferred_element_type=F32)
    for b, col, head_col in pieces:
        on[b, :, col] = jnp.dot(vtn[b], pn[b, :, col], preferred_element_type=F32)[: D + 8]


def far_kernel(*refs, head, blocks, groups, chained):
    table, top, near_top, q_v, do_v, qt, dt, kbn, vtn, pn, dpn, on = refs[:12]
    sources = refs[12:14]
    at = 15 if chained else 14
    o_out, pt, dst, kb, far_ref, diagonal_ref = refs[at : at + 6]
    vb, vt, acc, o_buf, out_sem = refs[at + 6 :]
    tokens = blocks * T
    acc[...] = jnp.zeros_like(acc)
    for b in range(blocks):
        kb[b, : 2 * T, :] = kbn[b]
    for b in range(blocks):
        for r in range(2):
            index = table[b * LINKED + 2 + r]
            here = pl.ds(r * T, T)
            kb[b, pl.ds((2 + r) * T, T), :] = sources[r][row_span(index), :D] * live_factor(index)
            values = sources[r][row_span(index), D:] * live_factor(index)
            vb[b, here, :] = values
            vt[b, :D, here] = values.T
            vt[b, D:, here] = jnp.full((ONES, T), live_factor(index), BF)

    def out_copy(b):
        rows = pl.ds(pl.multiple_of(b * T, T), T)
        columns = pl.ds(head * groups * D, groups * D)
        return pltpu.make_async_copy(o_buf.at[b], o_out.at[rows, columns], out_sem.at[b])

    keys_top = jnp.maximum(norm_top(sources[0][:, :D]), norm_top(sources[1][:, :D]))
    keys_top = jnp.maximum(keys_top, near_top[1 if head == 0 else 0])
    safe = top[0] * keys_top <= (SAFE_EXPONENT / (SCALE * LOG2E)) ** 2

    @pl.when(safe)
    def _():
        pieces = [
            (b, j, pl.ds(j * T, WIDE * T), pl.ds((head * groups + j) * D, WIDE * D))
            for b in range(blocks)
            for j in range(0, groups, WIDE)
        ]
        for b, j, col, head_col in pieces:
            scores = jnp.dot(kb[b, 2 * T :], qt[b, :, head_col], preferred_element_type=F32)
            pt[b, 2 * T :, col] = jnp.exp2(scores * (SCALE * LOG2E)).astype(BF)
        rows_done = []
        for b, j, col, head_col in pieces:
            sums = jnp.dot(vt[b], pt[b, 2 * T :, col], preferred_element_type=F32)
            sums = sums[: D + 8] + on[b, :, col]
            inverse = 1.0 / sums[D : D + 1]
            out_t = sums[:D] * inverse
            inner = jnp.sum(out_t * dt[b, :, head_col].astype(F32), axis=0, keepdims=True)
            rows_done.append((inverse, inner))
            for w in range(WIDE):
                o_buf[b, :, pl.ds((j + w) * D, D)] = out_t[:, w * T : (w + 1) * T].astype(BF).T
            if j + WIDE == groups:
                out_copy(b).start()
        for (b, j, col, head_col), (inverse, inner) in zip(pieces, rows_done):
            dprobs = jnp.dot(vb[b], dt[b, :, head_col], preferred_element_type=F32)
            weights = pn[b, :, col].astype(F32) * inverse
            pt[b, : 2 * T, col] = weights.astype(BF)
            dst[b, : 2 * T, col] = (weights * (dpn[b, :, col] - inner)).astype(BF)
            weights = pt[b, 2 * T :, col].astype(F32) * inverse
            pt[b, 2 * T :, col] = weights.astype(BF)
            dst[b, 2 * T :, col] = (weights * (dprobs - inner)).astype(BF)

    @pl.when(jnp.logical_not(safe))
    def _():
        tri = causal(1)

        def block(b, carry):
            bias = [
                jnp.where(table[b * LINKED + r] >= 0, 0.0, -jnp.inf).astype(F32)
                for r in range(LINKED)
            ]
            for g in range(groups):
                col = pl.ds(g * T, T)
                head_col = pl.ds((head * groups + g) * D, D)
                scores = jnp.dot(kb[b], qt[b, :, head_col], preferred_element_type=F32)
                dprobs = jnp.dot(vb[b], dt[b, :, head_col], preferred_element_type=F32)
                dparts = [dpn[b, pl.ds(r * T, T), col] for r in range(2)]
                dparts += [dprobs[:T], dprobs[T:]]
                parts = [scores[r * T : (r + 1) * T] * (SCALE * LOG2E) for r in range(LINKED)]
                parts[0] = jnp.where(tri, parts[0], -jnp.inf)
                highs = [jnp.max(x, axis=0, keepdims=True) + bias[r] for r, x in enumerate(parts)]
                high = functools.reduce(jnp.maximum, highs)
                exps = [jnp.exp2(x - (high - bias[r])) for r, x in enumerate(parts)]
                total = functools.reduce(
                    jnp.add, [jnp.sum(x, axis=0, keepdims=True) for x in exps]
                )
                inverse = 1.0 / total
                inner = inverse * functools.reduce(
                    jnp.add,
                    [jnp.sum(x * y, axis=0, keepdims=True) for x, y in zip(exps, dparts)],
                )
                for r in range(LINKED):
                    weights = exps[r] * inverse
                    here = pl.ds(r * T, T)
                    pt[b, here, col] = weights.astype(BF)
                    dst[b, here, col] = (weights * (dparts[r] - inner)).astype(BF)
                out_t = jnp.dot(
                    vtn[b], pt[b, : 2 * T, col], preferred_element_type=F32
                ) + jnp.dot(vt[b], pt[b, 2 * T :, col], preferred_element_type=F32)
                o_buf[b, :, pl.ds(g * D, D)] = out_t[:D].astype(BF).T
            out_copy(b).start()
            return carry

        lax.fori_loop(0, blocks, block, 0)

    for b in range(blocks):
        rows = pl.ds(b * T, T)
        q_rows, do_rows = (
            jnp.concatenate(
                [ref[rows, pl.ds((head * groups + g) * D, D)] for g in range(groups)], 0
            )
            for ref in (q_v, do_v)
        )
        dv = jnp.dot(pt[b, 2 * T :], do_rows, preferred_element_type=F32)
        dk = jnp.dot(dst[b, 2 * T :], q_rows, preferred_element_type=F32) * SCALE
        for r in range(2):
            index = table[b * LINKED + 2 + r]
            here = row_span(jnp.where(index >= 0, index + r * blocks, 2 * blocks))
            acc[here, :D] += dk[r * T : (r + 1) * T]
            acc[here, D:] += dv[r * T : (r + 1) * T]
    far_ref[...] = acc[:tokens].astype(BF)
    diagonal_ref[...] = acc[tokens : 2 * tokens].astype(BF)
    for b in range(blocks):
        out_copy(b).wait()


def tail_kernel(*refs, head, blocks, groups, chained):
    table, q_v, do_v, pt, dst, kb = refs[:6]
    dq_out, own_ref, core_ref = refs[7:10] if chained else refs[6:9]
    acc, dq_buf, out_sem = refs[10:] if chained else refs[9:]
    tokens = blocks * T

    def out_copy(b):
        rows = pl.ds(b * T, T)
        columns = pl.ds(head * groups * D, groups * D)
        return pltpu.make_async_copy(dq_buf.at[b], dq_out.at[rows, columns], out_sem.at[b])

    acc[...] = jnp.zeros_like(acc)
    for b in range(blocks):
        for j in range(0, groups, WIDE):
            dq_t = SCALE * lax.dot_general(
                kb[b], dst[b, :, pl.ds(j * T, WIDE * T)], TN, preferred_element_type=F32
            )
            for w in range(WIDE):
                dq_buf[b, :, pl.ds((j + w) * D, D)] = dq_t[:, w * T : (w + 1) * T].astype(BF).T
        out_copy(b).start()
    for b in range(blocks):
        rows = pl.ds(b * T, T)
        q_rows, do_rows = (
            jnp.concatenate(
                [ref[rows, pl.ds((head * groups + g) * D, D)] for g in range(groups)], 0
            )
            for ref in (q_v, do_v)
        )
        dv = jnp.dot(pt[b, : 2 * T], do_rows, preferred_element_type=F32)
        dk = jnp.dot(dst[b, : 2 * T], q_rows, preferred_element_type=F32) * SCALE
        own_ref[rows, :D] = dk[:T]
        own_ref[rows, D:] = dv[:T]
        index = table[b * LINKED + 1]
        here = row_span(jnp.where(index >= 0, index, blocks))
        acc[here, :D] += dk[T:]
        acc[here, D:] += dv[T:]
    core_ref[...] = acc[:tokens].astype(BF)
    for b in range(blocks):
        out_copy(b).wait()


def work(microseconds):
    return pl.CostEstimate(flops=microseconds * 10**9, bytes_accessed=0, transcendentals=0)


def linked_body(info, queries, output_gradient, packed):
    tokens = queries.shape[0]
    heads = len(packed)
    blocks = tokens // T
    groups = QUERY_HEADS // KEY_VALUE_HEADS
    width = groups * T
    depth = min(PATH_DEPTH_MAX, LINKED)
    core = [(i, i ^ 1) for i in range(LINKED)]
    across = [(i, i ^ 2) for i in range(LINKED)]
    near = [lax.ppermute(own, "ctx", core) for own in packed]
    far = [lax.ppermute(own, "ctx", across) for own in packed]

    vmem = pl.BlockSpec(memory_space=pltpu.VMEM)
    smem = pl.BlockSpec(memory_space=pltpu.SMEM)
    hbm = pl.BlockSpec(memory_space=pl.ANY)
    kept = pltpu.VMEM

    def keep(x):
        return pltpu.with_memory_space_constraint(x, pltpu.VMEM)

    def near_work(h, local):
        first = local is None
        parts = [
            kept((blocks, 2 * T, D), BF),
            kept((blocks, D + ONES, 2 * T), BF),
            kept((blocks, 2 * T, width), BF),
            kept((blocks, 2 * T, width), F32),
            kept((blocks, D + 8, width), F32),
        ]
        whole = [
            kept(queries.shape, BF),
            kept(queries.shape, BF),
            kept((blocks, D, heads * width), BF),
            kept((blocks, D, heads * width), BF),
        ]
        table_shape = jax.ShapeDtypeStruct((blocks * LINKED,), jnp.int32)
        if first:
            wide = pl.BlockSpec(memory_space=pltpu.HBM)
            operands = [
                info,
                pltpu.with_memory_space_constraint(queries, pltpu.HBM),
                pltpu.with_memory_space_constraint(output_gradient, pltpu.HBM),
            ]
            in_specs = [smem, wide, wide]
            out_specs = [smem, smem] + [vmem] * 9
            out_shape = [table_shape, jax.ShapeDtypeStruct((2,), F32)] + whole + parts
        else:
            operands = [local[0], local[4], local[5]]
            in_specs = [smem, vmem, vmem]
            out_specs = [smem] + [vmem] * 5
            out_shape = [jax.ShapeDtypeStruct((1,), F32)] + parts
        done = pl.pallas_call(
            functools.partial(
                near_kernel, head=h, blocks=blocks, heads=heads, groups=groups, depth=depth
            ),
            in_specs=in_specs + [hbm, hbm],
            out_specs=out_specs,
            out_shape=out_shape,
            scratch_shapes=[
                pltpu.VMEM((2, tokens, 2 * D), BF),
                pltpu.VMEM((blocks, 2 * T, D), BF),
                pltpu.SemaphoreType.DMA((2,)),
            ]
            + ([pltpu.SemaphoreType.DMA((2, blocks))] if first else []),
            compiler_params=pltpu.CompilerParams(vmem_limit_bytes=12 * 2**20),
            cost_estimate=work(4),
            name="near",
        )(*operands, packed[h], near[h])
        return [x if x.ndim == 1 else keep(x) for x in done]

    shared = near_work(0, None)
    table, top = shared[:2]
    local = shared[2:6]
    far[0], table = lax.optimization_barrier((far[0], table))
    diagonal = [lax.ppermute(far[0], "ctx", core)]
    near_parts = [[top] + shared[6:]]
    for h in range(1, heads):
        near_parts.append(near_work(h, [table, None] + local))
        far[h], near_parts[h][0] = lax.optimization_barrier((far[h], near_parts[h][0]))
        diagonal.append(lax.ppermute(far[h], "ctx", core))

    attended = None
    probs = []
    far_parts = []
    for h in range(heads):
        chained = attended is not None
        operands = [table, top, near_parts[h][0], *local, *near_parts[h][1:], keep(far[h]), keep(diagonal[h])]
        done = pl.pallas_call(
            functools.partial(far_kernel, head=h, blocks=blocks, groups=groups, chained=chained),
            in_specs=[smem] * 3 + [vmem] * 11 + [hbm] * (1 if chained else 0),
            out_specs=[hbm] + [vmem] * 5,
            out_shape=[
                jax.ShapeDtypeStruct(queries.shape, BF),
                kept((blocks, LINKED * T, width), BF),
                kept((blocks, LINKED * T, width), BF),
                kept((blocks, LINKED * T, D), BF),
                jax.ShapeDtypeStruct((tokens, 2 * D), BF),
                jax.ShapeDtypeStruct((tokens, 2 * D), BF),
            ],
            input_output_aliases={len(operands): 0} if chained else {},
            scratch_shapes=[
                pltpu.VMEM((blocks, 2 * T, D), BF),
                pltpu.VMEM((blocks, D + ONES, 2 * T), BF),
                pltpu.VMEM((2 * tokens + T, 2 * D), F32),
                pltpu.VMEM((blocks, T, groups * D), BF),
                pltpu.SemaphoreType.DMA((blocks,)),
            ],
            compiler_params=pltpu.CompilerParams(vmem_limit_bytes=12 * 2**20),
            cost_estimate=work(5),
            name="far",
        )(*operands, *([attended] if chained else []))
        attended = done[0]
        probs.append([keep(x) for x in done[1:4]])
        far_parts.append(done[4:])

    onward = []
    d_queries = None
    summed = []
    for h in range(heads):
        to_far, to_diagonal = far_parts[h]
        received = lax.ppermute(to_diagonal, "ctx", core)
        sums = (to_far.astype(F32) + received.astype(F32)).astype(BF)
        onward.append(lax.ppermute(sums, "ctx", across))
        chained = d_queries is not None
        operands = [table, local[0], local[1], *probs[h]]
        operands[0], _ = lax.optimization_barrier((table, sums))
        done = pl.pallas_call(
            functools.partial(
                tail_kernel, head=h, blocks=blocks, groups=groups, chained=chained
            ),
            in_specs=[smem] + [vmem] * 5 + ([hbm] if chained else []),
            out_specs=[hbm, vmem, vmem],
            out_shape=[
                jax.ShapeDtypeStruct(queries.shape, BF),
                jax.ShapeDtypeStruct((tokens, 2 * D), F32),
                jax.ShapeDtypeStruct((tokens, 2 * D), BF),
            ],
            input_output_aliases={len(operands): 0} if chained else {},
            scratch_shapes=[
                pltpu.VMEM((tokens + T, 2 * D), F32),
                pltpu.VMEM((blocks, T, groups * D), BF),
                pltpu.SemaphoreType.DMA((blocks,)),
            ],
            compiler_params=pltpu.CompilerParams(vmem_limit_bytes=12 * 2**20),
            cost_estimate=work(3),
            name="tail",
        )(*operands, *([d_queries] if chained else []))
        d_queries = done[0]
        summed.append(done[1] + lax.ppermute(done[2], "ctx", core).astype(F32))
    d_keys = jnp.concatenate(
        [(x + y.astype(F32))[:, :D] for x, y in zip(summed, onward)], 1
    ).astype(BF)
    d_values = jnp.concatenate(
        [(x + y.astype(F32))[:, D:] for x, y in zip(summed, onward)], 1
    ).astype(BF)
    return attended, d_queries, d_keys, d_values


def body(queries, key_states, value_tensor, output_gradient, parent, block_owner, shards):
    heads = key_states.shape[1] // D
    me = lax.axis_index("ctx").astype(jnp.int32)
    info = jnp.concatenate([me[None], parent, block_owner])
    packed = [
        jnp.concatenate([key_states[:, h * D : (h + 1) * D], value_tensor[:, h * D : (h + 1) * D]], 1)
        for h in range(heads)
    ]
    if shards == LINKED:
        return linked_body(info, queries, output_gradient, packed)
    outputs = None
    summed = []
    for h in range(heads):
        gathered = lax.all_gather(packed[h], "ctx", axis=0, tiled=True)
        done = attend(info, queries, output_gradient, gathered, outputs, h, shards)
        outputs = done[:2]
        summed.append(lax.psum_scatter(done[2], "ctx", scatter_dimension=0, tiled=True))
    d_keys = jnp.concatenate([s[:, :D] for s in summed], 1).astype(BF)
    d_values = jnp.concatenate([s[:, D:] for s in summed], 1).astype(BF)
    return (outputs[0], outputs[1], d_keys, d_values)


def solution(mesh):
    tokens_split = P(("groups", "ctx"), "tp")
    return jax.shard_map(
        functools.partial(body, shards=mesh.shape["ctx"]),
        mesh=mesh,
        in_specs=(tokens_split,) * 4 + (P("groups"),) * 2,
        out_specs=(tokens_split,) * 4,
        check_vma=False,
    )
```

```python
import functools
import math

import jax
import jax.numpy as jnp
from jax import lax
import jax.experimental.pallas as pl
import jax.experimental.pallas.tpu as pltpu
from jax.sharding import PartitionSpec as P

HEAD_SIZE = 128
TREE_BLOCK_SIZE = 128
PATH_DEPTH_MAX = 16
QUERY_HEADS = 64
KEY_VALUE_HEADS = 8

D = HEAD_SIZE
T = TREE_BLOCK_SIZE
NT = (((1,), (1,)), ((), ()))
TN = (((0,), (0,)), ((), ()))
BF = jnp.bfloat16
F32 = jnp.float32
SCALE = 1.0 / math.sqrt(D)
LOG2E = math.log2(math.e)
LINKED = 4
WIDE = 2
ONES = 16
SAFE_EXPONENT = 96.0


def fill_table(info, table, me, blocks, group_blocks, depth):
    for b in range(blocks):
        mine = me * blocks + b

        def find(t, found):
            return jnp.where(info[1 + group_blocks + t] == mine, t, found)

        current = lax.fori_loop(0, group_blocks, find, jnp.int32(0))
        for d in range(depth):
            if d:
                current = jnp.where(current >= 0, info[1 + jnp.maximum(current, 0)], -1)
            owner = info[1 + group_blocks + jnp.maximum(current, 0)]
            table[b * depth + d] = jnp.where(current >= 0, owner, -1)


def attend_kernel(*refs, head, blocks, group_blocks, depth, groups, chained):
    info, q_ref, do_ref, gathered = refs[:4]
    at = 6 if chained else 4
    o_out, dq_out, sum_ref = refs[at : at + 3]
    kv, acc, kb, vb, pt, dst, o_buf, dq_buf, table, kv_sem, out_sem = refs[at + 3 :]
    source_copy = pltpu.make_async_copy(gathered, kv, kv_sem)
    source_copy.start()
    fill_table(info, table, info[0], blocks, group_blocks, depth)
    acc[...] = jnp.zeros_like(acc)
    source_copy.wait()

    tri = lax.broadcasted_iota(jnp.int32, (T, T), 0) <= lax.broadcasted_iota(jnp.int32, (T, T), 1)

    def place(b, d):
        return pl.ds(pl.multiple_of(jnp.maximum(table[b * depth + d], 0) * T, T), T)

    def out_copies(b):
        rows = pl.ds(pl.multiple_of(b * T, T), T)
        columns = pl.ds(head * groups * D, groups * D)
        return (
            pltpu.make_async_copy(o_buf.at[b], o_out.at[rows, columns], out_sem.at[0, b]),
            pltpu.make_async_copy(dq_buf.at[b], dq_out.at[rows, columns], out_sem.at[1, b]),
        )

    def block(b, carry):
        rows = pl.ds(pl.multiple_of(b * T, T), T)
        for d in range(depth):
            kb[pl.ds(d * T, T), :] = kv[place(b, d), :D]
            vb[pl.ds(d * T, T), :] = kv[place(b, d), D:]
        bias = [
            jnp.where(table[b * depth + d] >= 0, 0.0, -jnp.inf).astype(F32) for d in range(depth)
        ]
        for g in range(groups):
            col = pl.ds(g * T, T)
            head_col = pl.ds((head * groups + g) * D, D)
            scores = lax.dot_general(kb[...], q_ref[rows, head_col], NT, preferred_element_type=F32)
            dprobs = lax.dot_general(vb[...], do_ref[rows, head_col], NT, preferred_element_type=F32)
            parts = [scores[d * T : (d + 1) * T] * (SCALE * LOG2E) for d in range(depth)]
            parts[0] = jnp.where(tri, parts[0], -jnp.inf)
            highs = [jnp.max(x, axis=0, keepdims=True) + bias[d] for d, x in enumerate(parts)]
            high = functools.reduce(jnp.maximum, highs)
            exps = [jnp.exp2(x - (high - bias[d])) for d, x in enumerate(parts)]
            total = functools.reduce(
                jnp.add, [jnp.sum(x, axis=0, keepdims=True) for x in exps]
            )
            inverse = 1.0 / total
            dparts = [dprobs[d * T : (d + 1) * T] for d in range(depth)]
            inner = inverse * functools.reduce(
                jnp.add,
                [jnp.sum(x * y, axis=0, keepdims=True) for x, y in zip(exps, dparts)],
            )
            for d in range(depth):
                weights = exps[d] * inverse
                pt[pl.ds(d * T, T), col] = weights.astype(BF)
                dst[pl.ds(d * T, T), col] = (weights * (dparts[d] - inner)).astype(BF)
        q_rows = jnp.concatenate(
            [q_ref[rows, (head * groups + g) * D : (head * groups + g + 1) * D] for g in range(groups)], 0
        )
        do_rows = jnp.concatenate(
            [do_ref[rows, (head * groups + g) * D : (head * groups + g + 1) * D] for g in range(groups)], 0
        )
        dv = jnp.dot(pt[...], do_rows, preferred_element_type=F32)
        dk = jnp.dot(dst[...], q_rows, preferred_element_type=F32) * SCALE
        for d in range(depth):
            acc[place(b, d), :D] += dk[d * T : (d + 1) * T]
            acc[place(b, d), D:] += dv[d * T : (d + 1) * T]
        out_t = lax.dot_general(vb[...], pt[...], TN, preferred_element_type=F32)
        dq_t = lax.dot_general(kb[...], dst[...], TN, preferred_element_type=F32) * SCALE
        for g in range(groups):
            col = pl.ds(g * T, T)
            o_buf[b, :, col] = out_t[:, g * T : (g + 1) * T].T.astype(BF)
            dq_buf[b, :, col] = dq_t[:, g * T : (g + 1) * T].T.astype(BF)
        for copy in out_copies(b):
            copy.start()
        return carry

    lax.fori_loop(0, blocks, block, 0)
    sum_ref[...] = acc[...]
    for b in range(blocks):
        for copy in out_copies(b):
            copy.wait()


def attend(info, queries, output_gradient, gathered, outputs, head, shards):
    tokens = queries.shape[0]
    blocks = tokens // T
    group_blocks = blocks * shards
    depth = min(PATH_DEPTH_MAX, shards)
    groups = QUERY_HEADS // KEY_VALUE_HEADS
    vmem = pl.BlockSpec(memory_space=pltpu.VMEM)
    hbm = pl.BlockSpec(memory_space=pl.ANY)
    chained = outputs is not None
    operands = [
        info,
        pltpu.with_memory_space_constraint(queries, pltpu.VMEM),
        pltpu.with_memory_space_constraint(output_gradient, pltpu.VMEM),
        gathered,
        *(outputs if chained else ()),
    ]
    in_specs = [pl.BlockSpec(memory_space=pltpu.SMEM), vmem, vmem]
    in_specs += [hbm] * (len(operands) - 3)
    full = jax.ShapeDtypeStruct(queries.shape, BF)
    total_rows = tokens * shards
    sums = [jax.ShapeDtypeStruct((total_rows, 2 * D), F32)]
    kernel = functools.partial(
        attend_kernel,
        head=head,
        blocks=blocks,
        group_blocks=group_blocks,
        depth=depth,
        groups=groups,
        chained=chained,
    )
    flops = 12 * blocks * groups * depth * T * T * D
    return pl.pallas_call(
        kernel,
        in_specs=in_specs,
        out_specs=[hbm, hbm] + [vmem] * len(sums),
        out_shape=[full, full] + sums,
        input_output_aliases={4: 0, 5: 1} if chained else {},
        scratch_shapes=[
            pltpu.VMEM((total_rows, 2 * D), BF),
            pltpu.VMEM((total_rows, 2 * D), F32),
            pltpu.VMEM((depth * T, D), BF),
            pltpu.VMEM((depth * T, D), BF),
            pltpu.VMEM((depth * T, groups * T), BF),
            pltpu.VMEM((depth * T, groups * T), BF),
            pltpu.VMEM((blocks, T, groups * D), BF),
            pltpu.VMEM((blocks, T, groups * D), BF),
            pltpu.SMEM((blocks * depth,), jnp.int32),
            pltpu.SemaphoreType.DMA,
            pltpu.SemaphoreType.DMA((2, blocks)),
        ],
        compiler_params=pltpu.CompilerParams(vmem_limit_bytes=40 * 2**20),
        cost_estimate=pl.CostEstimate(
            flops=2 * flops, bytes_accessed=8 * tokens * groups * D, transcendentals=0
        ),
        name="attend",
    )(*operands)


def relation_table(info, table, blocks, depth):
    me = info[0]
    group_blocks = blocks * LINKED

    def walk(block, visit):
        current = jnp.int32(0)
        for t in range(group_blocks):
            current = jnp.where(info[1 + group_blocks + t] == block, t, current)
        for d in range(depth):
            if d:
                current = jnp.where(current >= 0, info[1 + jnp.maximum(current, 0)], -1)
            owner = info[1 + group_blocks + jnp.maximum(current, 0)]
            shard = lax.div(owner, jnp.int32(blocks))
            visit(current >= 0, shard, owner - shard * blocks)

    for b in range(blocks):
        for r in range(LINKED):
            table[b * LINKED + r] = -1

        def visit(live, shard, index):
            slot = b * LINKED + (shard ^ me)
            table[slot] = jnp.where(live, index, table[slot])

        walk(me * blocks + b, visit)
    for r in range(2):
        ends = [jnp.int32(blocks), jnp.int32(-1)]

        def visit(live, shard, index):
            mine = jnp.logical_and(live, shard == me)
            ends[0] = jnp.where(mine, jnp.minimum(ends[0], index), ends[0])
            ends[1] = jnp.where(mine, jnp.maximum(ends[1], index), ends[1])

        for b in range(blocks):
            walk((me ^ (2 + r)) * blocks + b, visit)
        for side in range(2):
            table[blocks * LINKED + 2 * r + side] = ends[side]


def row_span(index):
    return pl.ds(pl.multiple_of(jnp.maximum(index, 0) * T, T), T)


def live_factor(index):
    return jnp.where(index >= 0, 1.0, 0.0).astype(BF)


def norm_top(rows):
    wide = rows.astype(F32)
    return jnp.max(jnp.sum(wide * wide, axis=1, keepdims=True))


def causal(width):
    keys = lax.broadcasted_iota(jnp.int32, (T, T), 0)
    queries = lax.broadcasted_iota(jnp.int32, (T, T), 1)
    return jnp.concatenate([keys <= queries] * width, 1)


def near_kernel(*refs, head, blocks, heads, groups, depth):
    if head == 0:
        info, q_in, do_in, own, near = refs[:5]
        table, top, q_v, do_v, qt, dt, kbn, vtn, pn, dpn, on = refs[5:16]
        kv, vb, kv_sem, row_sem = refs[16:]
    else:
        table, qt, dt, own, near = refs[:5]
        top, kbn, vtn, pn, dpn, on = refs[5:11]
        kv, vb, kv_sem = refs[11:]

    kv_copies = [
        pltpu.make_async_copy(source, kv.at[i], kv_sem.at[i]) for i, source in enumerate((own, near))
    ]
    for copy in kv_copies:
        copy.start()
    if head == 0:

        def row_copies(b):
            rows = pl.ds(b * T, T)
            return (
                pltpu.make_async_copy(q_in.at[rows], q_v.at[rows], row_sem.at[0, b]),
                pltpu.make_async_copy(do_in.at[rows], do_v.at[rows], row_sem.at[1, b]),
            )

        for b in range(blocks):
            for copy in row_copies(b):
                copy.start()
        relation_table(info, table, blocks, depth)
        highest = jnp.zeros((1, heads * groups * T), F32)
        for b in range(blocks):
            for copy in row_copies(b):
                copy.wait()
            for g in range(heads * groups):
                col = pl.ds(g * D, D)
                qt[b, :, col] = q_v[pl.ds(b * T, T), col].T
                dt[b, :, col] = do_v[pl.ds(b * T, T), col].T
            wide = qt[b].astype(F32)
            highest = jnp.maximum(highest, jnp.sum(wide * wide, axis=0, keepdims=True))
        top[0] = jnp.max(highest)
    for copy in kv_copies:
        copy.wait()
    top[1 if head == 0 else 0] = jnp.maximum(norm_top(kv[0, :, :D]), norm_top(kv[1, :, :D]))
    for b in range(blocks):
        for r in range(2):
            index = table[b * LINKED + r]
            here = pl.ds(r * T, T)
            kbn[b, here, :] = kv[r, row_span(index), :D] * live_factor(index)
            values = kv[r, row_span(index), D:] * live_factor(index)
            vb[b, here, :] = values
            vtn[b, :D, here] = values.T
            vtn[b, D:, here] = jnp.full((ONES, T), live_factor(index), BF)
    tri = causal(WIDE)
    pieces = [
        (b, pl.ds(j * T, WIDE * T), pl.ds((head * groups + j) * D, WIDE * D))
        for b in range(blocks)
        for j in range(0, groups, WIDE)
    ]
    for b, col, head_col in pieces:
        scores = jnp.dot(kbn[b], qt[b, :, head_col], preferred_element_type=F32)
        exps = jnp.exp2(scores * (SCALE * LOG2E))
        pn[b, :T, col] = jnp.where(tri, exps[:T], 0.0).astype(BF)
        pn[b, T:, col] = exps[T:].astype(BF)
    for b, col, head_col in pieces:
        dpn[b, :, col] = jnp.dot(vb[b], dt[b, :, head_col], preferred_element_type=F32)
    for b, col, head_col in pieces:
        on[b, :, col] = jnp.dot(vtn[b], pn[b, :, col], preferred_element_type=F32)[: D + 8]


def far_kernel(*refs, head, blocks, groups, chained, direct):
    table, top, near_top, q_v, do_v, qt, dt, kbn, vtn, pn, dpn, on = refs[:12]
    sources = refs[12:14]
    at = 15 if chained else 14
    o_out, pn_out, dst, kb, stats = refs[at : at + 5]
    sent = refs[at + 5 : at + (8 if direct else 7)]
    pt, vb, vt, acc, o_buf, out_sem = refs[at + (8 if direct else 7) :]
    acc[...] = jnp.zeros_like(acc)
    for b in range(blocks):
        kb[b, :T, :] = kbn[b, T:]
        for r in range(2):
            index = table[b * LINKED + 2 + r]
            here = pl.ds(r * T, T)
            kb[b, pl.ds((1 + r) * T, T), :] = sources[r][row_span(index), :D] * live_factor(index)
            values = sources[r][row_span(index), D:] * live_factor(index)
            vb[b, here, :] = values
            vt[b, :D, here] = values.T
            vt[b, D:, here] = jnp.full((ONES, T), live_factor(index), BF)

    def out_copy(b):
        rows = pl.ds(pl.multiple_of(b * T, T), T)
        columns = pl.ds(head * groups * D, groups * D)
        return pltpu.make_async_copy(o_buf.at[b], o_out.at[rows, columns], out_sem.at[b])

    keys_top = jnp.maximum(norm_top(sources[0][:, :D]), norm_top(sources[1][:, :D]))
    keys_top = jnp.maximum(keys_top, near_top[1 if head == 0 else 0])
    safe = top[0] * keys_top <= (SAFE_EXPONENT / (SCALE * LOG2E)) ** 2

    @pl.when(safe)
    def _():
        pieces = [
            (b, j, pl.ds(j * T, WIDE * T), pl.ds((head * groups + j) * D, WIDE * D))
            for b in range(blocks)
            for j in range(0, groups, WIDE)
        ]
        for b, j, col, head_col in pieces:
            scores = jnp.dot(kb[b, T:], qt[b, :, head_col], preferred_element_type=F32)
            pt[b, T:, col] = jnp.exp2(scores * (SCALE * LOG2E)).astype(BF)
        for b, j, col, head_col in pieces:
            sums = jnp.dot(vt[b], pt[b, T:, col], preferred_element_type=F32)
            sums = sums[: D + 8] + on[b, :, col]
            inverse = 1.0 / sums[D : D + 1]
            out_t = sums[:D] * inverse
            inner = jnp.sum(out_t * dt[b, :, head_col].astype(F32), axis=0, keepdims=True)
            stats[b, :8, col] = jnp.broadcast_to(inverse, (8, WIDE * T))
            stats[b, 8:, col] = jnp.broadcast_to(inner, (8, WIDE * T))
            for w in range(WIDE):
                o_buf[b, :, pl.ds((j + w) * D, D)] = out_t[:, w * T : (w + 1) * T].astype(BF).T
            if j + WIDE == groups:
                out_copy(b).start()
        for b, j, col, head_col in pieces:
            dprobs = jnp.dot(vb[b], dt[b, :, head_col], preferred_element_type=F32)
            weights = pt[b, T:, col].astype(F32) * stats[b, :1, col]
            pt[b, T:, col] = weights.astype(BF)
            dst[b, T:, col] = (weights * (dprobs - stats[b, 8:9, col])).astype(BF)
        for b, j, col, head_col in pieces:
            weights = pn[b, T:, col].astype(F32) * stats[b, :1, col]
            pt[b, :T, col] = weights.astype(BF)
            dst[b, :T, col] = (weights * (dpn[b, T:, col] - stats[b, 8:9, col])).astype(BF)

    @pl.when(jnp.logical_not(safe))
    def _():
        tri = causal(1)

        def block(b, carry):
            bias = [
                jnp.where(table[b * LINKED + r] >= 0, 0.0, -jnp.inf).astype(F32)
                for r in range(LINKED)
            ]
            for g in range(groups):
                col = pl.ds(g * T, T)
                head_col = pl.ds((head * groups + g) * D, D)
                near_scores = jnp.dot(kbn[b], qt[b, :, head_col], preferred_element_type=F32)
                scores = jnp.dot(kb[b, T:], qt[b, :, head_col], preferred_element_type=F32)
                dprobs = jnp.dot(vb[b], dt[b, :, head_col], preferred_element_type=F32)
                dparts = [dpn[b, :T, col], dpn[b, T:, col], dprobs[:T], dprobs[T:]]
                parts = [near_scores[:T], near_scores[T:], scores[:T], scores[T:]]
                parts = [x * (SCALE * LOG2E) for x in parts]
                parts[0] = jnp.where(tri, parts[0], -jnp.inf)
                highs = [jnp.max(x, axis=0, keepdims=True) + bias[r] for r, x in enumerate(parts)]
                high = functools.reduce(jnp.maximum, highs)
                exps = [jnp.exp2(x - (high - bias[r])) for r, x in enumerate(parts)]
                total = functools.reduce(
                    jnp.add, [jnp.sum(x, axis=0, keepdims=True) for x in exps]
                )
                inverse = 1.0 / total
                inner = inverse * functools.reduce(
                    jnp.add,
                    [jnp.sum(x * y, axis=0, keepdims=True) for x, y in zip(exps, dparts)],
                )
                stats[b, :8, col] = jnp.ones((8, T), F32)
                stats[b, 8:, col] = jnp.broadcast_to(inner, (8, T))
                pn_out[b, :T, col] = (exps[0] * inverse).astype(BF)
                pn_out[b, T:, col] = (exps[1] * inverse).astype(BF)
                for r in range(3):
                    here = pl.ds(r * T, T)
                    weights = exps[1 + r] * inverse
                    pt[b, here, col] = weights.astype(BF)
                    dst[b, here, col] = (weights * (dparts[1 + r] - inner)).astype(BF)
                out_t = jnp.dot(
                    vtn[b], pn_out[b, :, col], preferred_element_type=F32
                ) + jnp.dot(vt[b], pt[b, T:, col], preferred_element_type=F32)
                o_buf[b, :, pl.ds(g * D, D)] = out_t[:D].astype(BF).T
            out_copy(b).start()
            return carry

        lax.fori_loop(0, blocks, block, 0)

    lows = [
        functools.reduce(
            jnp.minimum,
            [
                jnp.where(table[b * LINKED + r] >= 0, table[b * LINKED + r], blocks)
                for b in range(blocks)
            ],
        )
        for r in (2, 3)
    ]
    slots = 2 if direct else blocks
    for b in range(blocks):
        q_rows, do_rows = (stacked(ref, head, b, groups) for ref in (q_v, do_v))
        dv = jnp.dot(pt[b], do_rows, preferred_element_type=F32)
        dk = jnp.dot(dst[b], q_rows, preferred_element_type=F32) * SCALE
        places = [table[b * LINKED + 1 + r] for r in range(3)]
        for r, index in enumerate(places):
            slot = index
            if r:
                if direct:
                    slot = jnp.where(index == lows[r - 1], 0, 1)
                slot = blocks + slot + (r - 1) * slots
            here = row_span(jnp.where(index >= 0, slot, 3 * blocks))
            acc[here, :D] += dk[r * T : (r + 1) * T]
            acc[here, D:] += dv[r * T : (r + 1) * T]
    tokens = blocks * T
    ends = [0, tokens, tokens + slots * T, tokens + 2 * slots * T]
    if direct:
        for r in range(3):
            sent[r][...] = acc[ends[r] : ends[r + 1]].astype(BF)
    else:
        sent[0][:tokens] = acc[:tokens].astype(BF)
        sent[0][tokens:] = acc[ends[2] : ends[3]].astype(BF)
        sent[1][...] = acc[ends[1] : ends[2]].astype(BF)
    for b in range(blocks):
        out_copy(b).wait()


def stacked(ref, head, b, groups):
    return jnp.concatenate(
        [ref[pl.ds(b * T, T), pl.ds((head * groups + g) * D, D)] for g in range(groups)], 0
    )


def tail_kernel(*refs, head, blocks, groups, chained):
    q_v, do_v, kbn, pn, dpn, dst, kb, stats = refs[:8]
    at = 9 if chained else 8
    dq_out, own_ref = refs[at : at + 2]
    ptn, dsn, dq_buf, out_sem = refs[at + 2 :]

    def out_copy(b):
        rows = pl.ds(b * T, T)
        columns = pl.ds(head * groups * D, groups * D)
        return pltpu.make_async_copy(dq_buf.at[b], dq_out.at[rows, columns], out_sem.at[b])

    pieces = [(b, j, pl.ds(j * T, WIDE * T)) for b in range(blocks) for j in range(0, groups, WIDE)]
    for b, j, col in pieces:
        weights = pn[b, :T, col].astype(F32) * stats[b, :1, col]
        ptn[b, :, col] = weights.astype(BF)
        dsn[b, :, col] = (weights * (dpn[b, :T, col] - stats[b, 8:9, col])).astype(BF)
    for b, j, col in pieces:
        dq_t = lax.dot_general(kbn[b, :T], dsn[b, :, col], TN, preferred_element_type=F32)
        dq_t += lax.dot_general(kb[b], dst[b, :, col], TN, preferred_element_type=F32)
        dq_t = dq_t * SCALE
        for w in range(WIDE):
            dq_buf[b, :, pl.ds((j + w) * D, D)] = dq_t[:, w * T : (w + 1) * T].astype(BF).T
        if j + WIDE == groups:
            out_copy(b).start()
    for b in range(blocks):
        rows = pl.ds(b * T, T)
        q_rows, do_rows = (stacked(ref, head, b, groups) for ref in (q_v, do_v))
        own_ref[rows, :D] = jnp.dot(dsn[b], q_rows, preferred_element_type=F32) * SCALE
        own_ref[rows, D:] = jnp.dot(ptn[b], do_rows, preferred_element_type=F32)
    for b in range(blocks):
        out_copy(b).wait()


def finish_kernel(*refs, heads, blocks):
    table = refs[0]
    dk_ref, dv_ref, acc = refs[-3:]
    at = 1
    tokens = blocks * T
    for h in range(heads):
        own, core = refs[at : at + 2]
        at += 2
        acc[...] = own[...] + core[:tokens].astype(F32)
        if h + 1 == heads:
            acc[...] += refs[at][...].astype(F32)
            at += 1
        else:
            for r in range(2):
                for side in range(2):
                    index = jnp.minimum(table[blocks * LINKED + 2 * r + side], blocks - 1)
                    acc[row_span(index)] += refs[at + r][pl.ds(side * T, T)].astype(F32)
            at += 2
        dk_ref[:, pl.ds(h * D, D)] = acc[:, :D].astype(BF)
        dv_ref[:, pl.ds(h * D, D)] = acc[:, D:].astype(BF)


def work(microseconds):
    return pl.CostEstimate(flops=int(microseconds * 10**9), bytes_accessed=0, transcendentals=0)


def linked_body(info, queries, output_gradient, packed):
    tokens = queries.shape[0]
    heads = len(packed)
    blocks = tokens // T
    groups = QUERY_HEADS // KEY_VALUE_HEADS
    width = groups * T
    depth = min(PATH_DEPTH_MAX, LINKED)
    core = [(i, i ^ 1) for i in range(LINKED)]
    across = [(i, i ^ 2) for i in range(LINKED)]
    corner = [(i, i ^ 3) for i in range(LINKED)]
    near = [lax.ppermute(own, "ctx", core) for own in packed]
    far = [lax.ppermute(own, "ctx", across) for own in packed]

    vmem = pl.BlockSpec(memory_space=pltpu.VMEM)
    smem = pl.BlockSpec(memory_space=pltpu.SMEM)
    hbm = pl.BlockSpec(memory_space=pl.ANY)
    kept = pltpu.VMEM

    def keep(x):
        return pltpu.with_memory_space_constraint(x, pltpu.VMEM)

    def scalars(x):
        return pltpu.with_memory_space_constraint(x, pltpu.SMEM)

    def near_work(h, local):
        first = local is None
        parts = [
            kept((blocks, 2 * T, D), BF),
            kept((blocks, D + ONES, 2 * T), BF),
            kept((blocks, 2 * T, width), BF),
            kept((blocks, 2 * T, width), F32),
            kept((blocks, D + 8, width), F32),
        ]
        whole = [
            kept(queries.shape, BF),
            kept(queries.shape, BF),
            kept((blocks, D, heads * width), BF),
            kept((blocks, D, heads * width), BF),
        ]
        table_shape = pltpu.SMEM((blocks * LINKED + 4,), jnp.int32)
        if first:
            wide = pl.BlockSpec(memory_space=pltpu.HBM)
            operands = [
                info,
                pltpu.with_memory_space_constraint(queries, pltpu.HBM),
                pltpu.with_memory_space_constraint(output_gradient, pltpu.HBM),
            ]
            in_specs = [smem, wide, wide]
            out_specs = [smem, smem] + [vmem] * 9
            out_shape = [table_shape, pltpu.SMEM((2,), F32)] + whole + parts
        else:
            operands = [local[0], local[4], local[5]]
            in_specs = [smem, vmem, vmem]
            out_specs = [smem] + [vmem] * 5
            out_shape = [pltpu.SMEM((1,), F32)] + parts
        done = pl.pallas_call(
            functools.partial(
                near_kernel, head=h, blocks=blocks, heads=heads, groups=groups, depth=depth
            ),
            in_specs=in_specs + [hbm, hbm],
            out_specs=out_specs,
            out_shape=out_shape,
            scratch_shapes=[
                pltpu.VMEM((2, tokens, 2 * D), BF),
                pltpu.VMEM((blocks, 2 * T, D), BF),
                pltpu.SemaphoreType.DMA((2,)),
            ]
            + ([pltpu.SemaphoreType.DMA((2, blocks))] if first else []),
            compiler_params=pltpu.CompilerParams(vmem_limit_bytes=12 * 2**20),
            cost_estimate=work(4),
            name="near",
        )(*operands, packed[h], near[h])
        return [scalars(x) if x.ndim == 1 else keep(x) for x in done]

    shared = near_work(0, None)
    table, top = shared[:2]
    local = shared[2:6]
    far[0], _ = lax.optimization_barrier((far[0], shared[10]))
    diagonal = [lax.ppermute(far[0], "ctx", core)]
    near_parts = [[top] + shared[6:]]
    for h in range(1, heads):
        near_parts.append(near_work(h, [table, None] + local))
        far[h], _ = lax.optimization_barrier((far[h], near_parts[h][5]))
        diagonal.append(lax.ppermute(far[h], "ctx", core))

    attended = None
    probs = []
    arrivals = []
    for h in range(heads):
        chained = attended is not None
        direct = h + 1 < heads
        if direct:
            sent = [tokens, 2 * T, 2 * T]
        else:
            sent = [2 * tokens, tokens]
        operands = [table, top, near_parts[h][0], *local, *near_parts[h][1:]]
        operands += [keep(far[h]), keep(diagonal[h])]
        done = pl.pallas_call(
            functools.partial(
                far_kernel, head=h, blocks=blocks, groups=groups, chained=chained, direct=direct
            ),
            in_specs=[smem] * 3 + [vmem] * 11 + [hbm] * (1 if chained else 0),
            out_specs=[hbm] + [vmem] * (4 + len(sent)),
            out_shape=[
                jax.ShapeDtypeStruct(queries.shape, BF),
                kept((blocks, 2 * T, width), BF),
                kept((blocks, 3 * T, width), BF),
                kept((blocks, 3 * T, D), BF),
                kept((blocks, 16, width), F32),
            ]
            + [kept((rows, 2 * D), BF) for rows in sent],
            input_output_aliases={9: 1} | ({len(operands): 0} if chained else {}),
            scratch_shapes=[
                pltpu.VMEM((blocks, 3 * T, width), BF),
                pltpu.VMEM((blocks, 2 * T, D), BF),
                pltpu.VMEM((blocks, D + ONES, 2 * T), BF),
                pltpu.VMEM((3 * tokens + T, 2 * D), F32),
                pltpu.VMEM((blocks, T, groups * D), BF),
                pltpu.SemaphoreType.DMA((blocks,)),
            ],
            compiler_params=pltpu.CompilerParams(vmem_limit_bytes=12 * 2**20),
            cost_estimate=work(5),
            name="far",
        )(*operands, *([attended] if chained else []))
        attended = done[0]
        near_probs, *rest = [keep(x) for x in done[1:5]]
        _, kbn, _, _, dpn, _ = near_parts[h]
        probs.append([kbn, near_probs, dpn, *rest])
        if direct:
            to_core, to_far, to_corner = done[5:]
            arrivals.append(
                [
                    lax.ppermute(to_core, "ctx", core),
                    lax.ppermute(to_far, "ctx", across),
                    lax.ppermute(to_corner, "ctx", corner),
                ]
            )
        else:
            to_core, to_far = done[5:]
            if arrivals:
                to_core, arrivals[-1] = lax.optimization_barrier((to_core, arrivals[-1]))
            received = lax.ppermute(to_core, "ctx", core)
            sums = (to_far.astype(F32) + received[tokens:].astype(F32)).astype(BF)
            arrivals.append([received, lax.ppermute(sums, "ctx", across)])

    d_queries = None
    finishing = [table]
    for h in range(heads):
        chained = d_queries is not None
        operands = [local[0], local[1], *probs[h]]
        if not chained:
            operands[-1], _ = lax.optimization_barrier((operands[-1], sums))
            operands[-1] = keep(operands[-1])
        done = pl.pallas_call(
            functools.partial(tail_kernel, head=h, blocks=blocks, groups=groups, chained=chained),
            in_specs=[vmem] * 8 + ([hbm] if chained else []),
            out_specs=[hbm, vmem],
            out_shape=[jax.ShapeDtypeStruct(queries.shape, BF), kept((tokens, 2 * D), F32)],
            input_output_aliases={len(operands): 0} if chained else {},
            scratch_shapes=[
                pltpu.VMEM((blocks, T, width), BF),
                pltpu.VMEM((blocks, T, width), BF),
                pltpu.VMEM((blocks, T, groups * D), BF),
                pltpu.SemaphoreType.DMA((blocks,)),
            ],
            compiler_params=pltpu.CompilerParams(vmem_limit_bytes=12 * 2**20),
            cost_estimate=work(0.3),
            name="tail",
        )(*operands, *([d_queries] if chained else []))
        d_queries = done[0]
        finishing += [keep(done[1])] + [keep(x) for x in arrivals[h]]
    d_keys, d_values = pl.pallas_call(
        functools.partial(finish_kernel, heads=heads, blocks=blocks),
        in_specs=[smem] + [vmem] * (len(finishing) - 1),
        out_specs=[vmem, vmem],
        out_shape=[jax.ShapeDtypeStruct((tokens, heads * D), BF)] * 2,
        scratch_shapes=[pltpu.VMEM((tokens, 2 * D), F32)],
        name="finish",
    )(*finishing)
    return attended, d_queries, d_keys, d_values


def body(queries, key_states, value_tensor, output_gradient, parent, block_owner, shards):
    heads = key_states.shape[1] // D
    me = lax.axis_index("ctx").astype(jnp.int32)
    info = jnp.concatenate([me[None], parent, block_owner])
    packed = [
        jnp.concatenate([key_states[:, h * D : (h + 1) * D], value_tensor[:, h * D : (h + 1) * D]], 1)
        for h in range(heads)
    ]
    if shards == LINKED:
        return linked_body(info, queries, output_gradient, packed)
    outputs = None
    summed = []
    for h in range(heads):
        gathered = lax.all_gather(packed[h], "ctx", axis=0, tiled=True)
        done = attend(info, queries, output_gradient, gathered, outputs, h, shards)
        outputs = done[:2]
        summed.append(lax.psum_scatter(done[2], "ctx", scatter_dimension=0, tiled=True))
    d_keys = jnp.concatenate([s[:, :D] for s in summed], 1).astype(BF)
    d_values = jnp.concatenate([s[:, D:] for s in summed], 1).astype(BF)
    return (outputs[0], outputs[1], d_keys, d_values)


def solution(mesh):
    tokens_split = P(("groups", "ctx"), "tp")
    return jax.shard_map(
        functools.partial(body, shards=mesh.shape["ctx"]),
        mesh=mesh,
        in_specs=(tokens_split,) * 4 + (P("groups"),) * 2,
        out_specs=(tokens_split,) * 4,
        check_vma=False,
    )
```

```python
import functools
import math

import jax
import jax.numpy as jnp
from jax import lax
import jax.experimental.pallas as pl
import jax.experimental.pallas.tpu as pltpu
from jax.sharding import PartitionSpec as P

HEAD_SIZE = 128
TREE_BLOCK_SIZE = 128
PATH_DEPTH_MAX = 16
QUERY_HEADS = 64
KEY_VALUE_HEADS = 8

D = HEAD_SIZE
T = TREE_BLOCK_SIZE
NT = (((1,), (1,)), ((), ()))
TN = (((0,), (0,)), ((), ()))
BF = jnp.bfloat16
F32 = jnp.float32
SCALE = 1.0 / math.sqrt(D)
LOG2E = math.log2(math.e)
LINKED = 4
WIDE = 2
ONES = 16
SAFE_EXPONENT = 96.0


def fill_table(info, table, me, blocks, group_blocks, depth):
    for b in range(blocks):
        mine = me * blocks + b

        def find(t, found):
            return jnp.where(info[1 + group_blocks + t] == mine, t, found)

        current = lax.fori_loop(0, group_blocks, find, jnp.int32(0))
        for d in range(depth):
            if d:
                current = jnp.where(current >= 0, info[1 + jnp.maximum(current, 0)], -1)
            owner = info[1 + group_blocks + jnp.maximum(current, 0)]
            table[b * depth + d] = jnp.where(current >= 0, owner, -1)


def attend_kernel(*refs, head, blocks, group_blocks, depth, groups, chained):
    info, q_ref, do_ref, gathered = refs[:4]
    at = 6 if chained else 4
    o_out, dq_out, sum_ref = refs[at : at + 3]
    kv, acc, kb, vb, pt, dst, o_buf, dq_buf, table, kv_sem, out_sem = refs[at + 3 :]
    source_copy = pltpu.make_async_copy(gathered, kv, kv_sem)
    source_copy.start()
    fill_table(info, table, info[0], blocks, group_blocks, depth)
    acc[...] = jnp.zeros_like(acc)
    source_copy.wait()

    tri = lax.broadcasted_iota(jnp.int32, (T, T), 0) <= lax.broadcasted_iota(jnp.int32, (T, T), 1)

    def place(b, d):
        return pl.ds(pl.multiple_of(jnp.maximum(table[b * depth + d], 0) * T, T), T)

    def out_copies(b):
        rows = pl.ds(pl.multiple_of(b * T, T), T)
        columns = pl.ds(head * groups * D, groups * D)
        return (
            pltpu.make_async_copy(o_buf.at[b], o_out.at[rows, columns], out_sem.at[0, b]),
            pltpu.make_async_copy(dq_buf.at[b], dq_out.at[rows, columns], out_sem.at[1, b]),
        )

    def block(b, carry):
        rows = pl.ds(pl.multiple_of(b * T, T), T)
        for d in range(depth):
            kb[pl.ds(d * T, T), :] = kv[place(b, d), :D]
            vb[pl.ds(d * T, T), :] = kv[place(b, d), D:]
        bias = [
            jnp.where(table[b * depth + d] >= 0, 0.0, -jnp.inf).astype(F32) for d in range(depth)
        ]
        for g in range(groups):
            col = pl.ds(g * T, T)
            head_col = pl.ds((head * groups + g) * D, D)
            scores = lax.dot_general(kb[...], q_ref[rows, head_col], NT, preferred_element_type=F32)
            dprobs = lax.dot_general(vb[...], do_ref[rows, head_col], NT, preferred_element_type=F32)
            parts = [scores[d * T : (d + 1) * T] * (SCALE * LOG2E) for d in range(depth)]
            parts[0] = jnp.where(tri, parts[0], -jnp.inf)
            highs = [jnp.max(x, axis=0, keepdims=True) + bias[d] for d, x in enumerate(parts)]
            high = functools.reduce(jnp.maximum, highs)
            exps = [jnp.exp2(x - (high - bias[d])) for d, x in enumerate(parts)]
            total = functools.reduce(
                jnp.add, [jnp.sum(x, axis=0, keepdims=True) for x in exps]
            )
            inverse = 1.0 / total
            dparts = [dprobs[d * T : (d + 1) * T] for d in range(depth)]
            inner = inverse * functools.reduce(
                jnp.add,
                [jnp.sum(x * y, axis=0, keepdims=True) for x, y in zip(exps, dparts)],
            )
            for d in range(depth):
                weights = exps[d] * inverse
                pt[pl.ds(d * T, T), col] = weights.astype(BF)
                dst[pl.ds(d * T, T), col] = (weights * (dparts[d] - inner)).astype(BF)
        q_rows = jnp.concatenate(
            [q_ref[rows, (head * groups + g) * D : (head * groups + g + 1) * D] for g in range(groups)], 0
        )
        do_rows = jnp.concatenate(
            [do_ref[rows, (head * groups + g) * D : (head * groups + g + 1) * D] for g in range(groups)], 0
        )
        dv = jnp.dot(pt[...], do_rows, preferred_element_type=F32)
        dk = jnp.dot(dst[...], q_rows, preferred_element_type=F32) * SCALE
        for d in range(depth):
            acc[place(b, d), :D] += dk[d * T : (d + 1) * T]
            acc[place(b, d), D:] += dv[d * T : (d + 1) * T]
        out_t = lax.dot_general(vb[...], pt[...], TN, preferred_element_type=F32)
        dq_t = lax.dot_general(kb[...], dst[...], TN, preferred_element_type=F32) * SCALE
        for g in range(groups):
            col = pl.ds(g * T, T)
            o_buf[b, :, col] = out_t[:, g * T : (g + 1) * T].T.astype(BF)
            dq_buf[b, :, col] = dq_t[:, g * T : (g + 1) * T].T.astype(BF)
        for copy in out_copies(b):
            copy.start()
        return carry

    lax.fori_loop(0, blocks, block, 0)
    sum_ref[...] = acc[...]
    for b in range(blocks):
        for copy in out_copies(b):
            copy.wait()


def attend(info, queries, output_gradient, gathered, outputs, head, shards):
    tokens = queries.shape[0]
    blocks = tokens // T
    group_blocks = blocks * shards
    depth = min(PATH_DEPTH_MAX, shards)
    groups = QUERY_HEADS // KEY_VALUE_HEADS
    vmem = pl.BlockSpec(memory_space=pltpu.VMEM)
    hbm = pl.BlockSpec(memory_space=pl.ANY)
    chained = outputs is not None
    operands = [
        info,
        pltpu.with_memory_space_constraint(queries, pltpu.VMEM),
        pltpu.with_memory_space_constraint(output_gradient, pltpu.VMEM),
        gathered,
        *(outputs if chained else ()),
    ]
    in_specs = [pl.BlockSpec(memory_space=pltpu.SMEM), vmem, vmem]
    in_specs += [hbm] * (len(operands) - 3)
    full = jax.ShapeDtypeStruct(queries.shape, BF)
    total_rows = tokens * shards
    sums = [jax.ShapeDtypeStruct((total_rows, 2 * D), F32)]
    kernel = functools.partial(
        attend_kernel,
        head=head,
        blocks=blocks,
        group_blocks=group_blocks,
        depth=depth,
        groups=groups,
        chained=chained,
    )
    flops = 12 * blocks * groups * depth * T * T * D
    return pl.pallas_call(
        kernel,
        in_specs=in_specs,
        out_specs=[hbm, hbm] + [vmem] * len(sums),
        out_shape=[full, full] + sums,
        input_output_aliases={4: 0, 5: 1} if chained else {},
        scratch_shapes=[
            pltpu.VMEM((total_rows, 2 * D), BF),
            pltpu.VMEM((total_rows, 2 * D), F32),
            pltpu.VMEM((depth * T, D), BF),
            pltpu.VMEM((depth * T, D), BF),
            pltpu.VMEM((depth * T, groups * T), BF),
            pltpu.VMEM((depth * T, groups * T), BF),
            pltpu.VMEM((blocks, T, groups * D), BF),
            pltpu.VMEM((blocks, T, groups * D), BF),
            pltpu.SMEM((blocks * depth,), jnp.int32),
            pltpu.SemaphoreType.DMA,
            pltpu.SemaphoreType.DMA((2, blocks)),
        ],
        compiler_params=pltpu.CompilerParams(vmem_limit_bytes=40 * 2**20),
        cost_estimate=pl.CostEstimate(
            flops=2 * flops, bytes_accessed=8 * tokens * groups * D, transcendentals=0
        ),
        name="attend",
    )(*operands)


def relation_table(info, table, blocks, depth):
    me = info[0]
    group_blocks = blocks * LINKED

    def walk(block, visit):
        current = jnp.int32(0)
        for t in range(group_blocks):
            current = jnp.where(info[1 + group_blocks + t] == block, t, current)
        for d in range(depth):
            if d:
                current = jnp.where(current >= 0, info[1 + jnp.maximum(current, 0)], -1)
            owner = info[1 + group_blocks + jnp.maximum(current, 0)]
            shard = lax.div(owner, jnp.int32(blocks))
            visit(current >= 0, shard, owner - shard * blocks)

    for b in range(blocks):
        for r in range(LINKED):
            table[b * LINKED + r] = -1

        def visit(live, shard, index):
            slot = b * LINKED + (shard ^ me)
            table[slot] = jnp.where(live, index, table[slot])

        walk(me * blocks + b, visit)
    for r in range(2):
        ends = [jnp.int32(blocks), jnp.int32(-1)]

        def visit(live, shard, index):
            mine = jnp.logical_and(live, shard == me)
            ends[0] = jnp.where(mine, jnp.minimum(ends[0], index), ends[0])
            ends[1] = jnp.where(mine, jnp.maximum(ends[1], index), ends[1])

        for b in range(blocks):
            walk((me ^ (2 + r)) * blocks + b, visit)
        for side in range(2):
            table[blocks * LINKED + 2 * r + side] = ends[side]


def row_span(index):
    return pl.ds(pl.multiple_of(jnp.maximum(index, 0) * T, T), T)


def live_factor(index):
    return jnp.where(index >= 0, 1.0, 0.0).astype(BF)


def norm_top(rows):
    wide = rows.astype(F32)
    return jnp.max(jnp.sum(wide * wide, axis=1, keepdims=True))


def causal(width):
    keys = lax.broadcasted_iota(jnp.int32, (T, T), 0)
    queries = lax.broadcasted_iota(jnp.int32, (T, T), 1)
    return jnp.concatenate([keys <= queries] * width, 1)


def near_kernel(*refs, head, blocks, heads, groups, depth):
    if head == 0:
        info, q_v, do_in, own, near = refs[:5]
        table, top, do_v, qt, dt, kbn, vtn, pn, dpn, on = refs[5:15]
        kv, vb, kv_sem, row_sem = refs[15:]
    else:
        table, qt, dt, own, near = refs[:5]
        top, kbn, vtn, pn, dpn, on = refs[5:11]
        kv, vb, kv_sem = refs[11:]

    kv_copies = [
        pltpu.make_async_copy(source, kv.at[i], kv_sem.at[i]) for i, source in enumerate((own, near))
    ]
    for copy in kv_copies:
        copy.start()
    if head == 0:

        do_copy = pltpu.make_async_copy(do_in, do_v, row_sem)
        do_copy.start()
        relation_table(info, table, blocks, depth)
        highest = jnp.zeros((1, heads * groups * T), F32)
        for b in range(blocks):
            for g in range(heads * groups):
                col = pl.ds(g * D, D)
                qt[b, :, col] = q_v[pl.ds(b * T, T), col].T
            wide = qt[b].astype(F32)
            highest = jnp.maximum(highest, jnp.sum(wide * wide, axis=0, keepdims=True))
        top[0] = jnp.max(highest)
    for copy in kv_copies:
        copy.wait()
    top[1 if head == 0 else 0] = jnp.maximum(norm_top(kv[0, :, :D]), norm_top(kv[1, :, :D]))
    for b in range(blocks):
        for r in range(2):
            index = table[b * LINKED + r]
            here = pl.ds(r * T, T)
            kbn[b, here, :] = kv[r, row_span(index), :D] * live_factor(index)
            values = kv[r, row_span(index), D:] * live_factor(index)
            vb[b, here, :] = values
            vtn[b, :D, here] = values.T
            vtn[b, D:, here] = jnp.full((ONES, T), live_factor(index), BF)
    tri = causal(WIDE)
    pieces = [
        (b, pl.ds(j * T, WIDE * T), pl.ds((head * groups + j) * D, WIDE * D))
        for b in range(blocks)
        for j in range(0, groups, WIDE)
    ]
    for b, col, head_col in pieces:
        scores = jnp.dot(kbn[b], qt[b, :, head_col], preferred_element_type=F32)
        exps = jnp.exp2(scores * (SCALE * LOG2E))
        pn[b, :T, col] = jnp.where(tri, exps[:T], 0.0).astype(BF)
        pn[b, T:, col] = exps[T:].astype(BF)
    if head == 0:
        do_copy.wait()
        for b in range(blocks):
            for g in range(heads * groups):
                col = pl.ds(g * D, D)
                dt[b, :, col] = do_v[pl.ds(b * T, T), col].T
    for b, col, head_col in pieces:
        dpn[b, :, col] = jnp.dot(vb[b], dt[b, :, head_col], preferred_element_type=F32)
    for b, col, head_col in pieces:
        on[b, :, col] = jnp.dot(vtn[b], pn[b, :, col], preferred_element_type=F32)[: D + 8]


def far_kernel(*refs, head, blocks, groups, chained):
    table, top, near_top, q_v, do_v, qt, dt, kbn, vtn, pn, dpn, on = refs[:12]
    sources = refs[12:14]
    at = 15 if chained else 14
    o_out, pn_out, dst, kb, stats = refs[at : at + 5]
    sent = refs[at + 5 : at + 8]
    pt, vb, vt, acc, o_buf, out_sem = refs[at + 8 :]
    acc[...] = jnp.zeros_like(acc)
    for b in range(blocks):
        kb[b, :T, :] = kbn[b, T:]
        for r in range(2):
            index = table[b * LINKED + 2 + r]
            here = pl.ds(r * T, T)
            kb[b, pl.ds((1 + r) * T, T), :] = sources[r][row_span(index), :D] * live_factor(index)
            values = sources[r][row_span(index), D:] * live_factor(index)
            vb[b, here, :] = values
            vt[b, :D, here] = values.T
            vt[b, D:, here] = jnp.full((ONES, T), live_factor(index), BF)

    def out_copy(b):
        rows = pl.ds(pl.multiple_of(b * T, T), T)
        columns = pl.ds(head * groups * D, groups * D)
        return pltpu.make_async_copy(o_buf.at[b], o_out.at[rows, columns], out_sem.at[b])

    keys_top = jnp.maximum(norm_top(sources[0][:, :D]), norm_top(sources[1][:, :D]))
    keys_top = jnp.maximum(keys_top, near_top[1 if head == 0 else 0])
    safe = top[0] * keys_top <= (SAFE_EXPONENT / (SCALE * LOG2E)) ** 2

    @pl.when(safe)
    def _():
        pieces = [
            (b, j, pl.ds(j * T, WIDE * T), pl.ds((head * groups + j) * D, WIDE * D))
            for b in range(blocks)
            for j in range(0, groups, WIDE)
        ]
        for b, j, col, head_col in pieces:
            scores = jnp.dot(kb[b, T:], qt[b, :, head_col], preferred_element_type=F32)
            pt[b, T:, col] = jnp.exp2(scores * (SCALE * LOG2E)).astype(BF)
        for b, j, col, head_col in pieces:
            sums = jnp.dot(vt[b], pt[b, T:, col], preferred_element_type=F32)
            sums = sums[: D + 8] + on[b, :, col]
            inverse = 1.0 / sums[D : D + 1]
            out_t = sums[:D] * inverse
            inner = jnp.sum(out_t * dt[b, :, head_col].astype(F32), axis=0, keepdims=True)
            stats[b, :8, col] = jnp.broadcast_to(inverse, (8, WIDE * T))
            stats[b, 8:, col] = jnp.broadcast_to(inner, (8, WIDE * T))
            for w in range(WIDE):
                o_buf[b, :, pl.ds((j + w) * D, D)] = out_t[:, w * T : (w + 1) * T].astype(BF).T
            if j + WIDE == groups:
                out_copy(b).start()
        for b, j, col, head_col in pieces:
            dprobs = jnp.dot(vb[b], dt[b, :, head_col], preferred_element_type=F32)
            weights = pt[b, T:, col].astype(F32) * stats[b, :1, col]
            pt[b, T:, col] = weights.astype(BF)
            dst[b, T:, col] = (weights * (dprobs - stats[b, 8:9, col])).astype(BF)
        for b, j, col, head_col in pieces:
            weights = pn[b, T:, col].astype(F32) * stats[b, :1, col]
            pt[b, :T, col] = weights.astype(BF)
            dst[b, :T, col] = (weights * (dpn[b, T:, col] - stats[b, 8:9, col])).astype(BF)

    @pl.when(jnp.logical_not(safe))
    def _():
        tri = causal(1)

        def block(b, carry):
            bias = [
                jnp.where(table[b * LINKED + r] >= 0, 0.0, -jnp.inf).astype(F32)
                for r in range(LINKED)
            ]
            for g in range(groups):
                col = pl.ds(g * T, T)
                head_col = pl.ds((head * groups + g) * D, D)
                near_scores = jnp.dot(kbn[b], qt[b, :, head_col], preferred_element_type=F32)
                scores = jnp.dot(kb[b, T:], qt[b, :, head_col], preferred_element_type=F32)
                dprobs = jnp.dot(vb[b], dt[b, :, head_col], preferred_element_type=F32)
                dparts = [dpn[b, :T, col], dpn[b, T:, col], dprobs[:T], dprobs[T:]]
                parts = [near_scores[:T], near_scores[T:], scores[:T], scores[T:]]
                parts = [x * (SCALE * LOG2E) for x in parts]
                parts[0] = jnp.where(tri, parts[0], -jnp.inf)
                highs = [jnp.max(x, axis=0, keepdims=True) + bias[r] for r, x in enumerate(parts)]
                high = functools.reduce(jnp.maximum, highs)
                exps = [jnp.exp2(x - (high - bias[r])) for r, x in enumerate(parts)]
                total = functools.reduce(
                    jnp.add, [jnp.sum(x, axis=0, keepdims=True) for x in exps]
                )
                inverse = 1.0 / total
                inner = inverse * functools.reduce(
                    jnp.add,
                    [jnp.sum(x * y, axis=0, keepdims=True) for x, y in zip(exps, dparts)],
                )
                stats[b, :8, col] = jnp.ones((8, T), F32)
                stats[b, 8:, col] = jnp.broadcast_to(inner, (8, T))
                pn_out[b, :T, col] = (exps[0] * inverse).astype(BF)
                pn_out[b, T:, col] = (exps[1] * inverse).astype(BF)
                for r in range(3):
                    here = pl.ds(r * T, T)
                    weights = exps[1 + r] * inverse
                    pt[b, here, col] = weights.astype(BF)
                    dst[b, here, col] = (weights * (dparts[1 + r] - inner)).astype(BF)
                out_t = jnp.dot(
                    vtn[b], pn_out[b, :, col], preferred_element_type=F32
                ) + jnp.dot(vt[b], pt[b, T:, col], preferred_element_type=F32)
                o_buf[b, :, pl.ds(g * D, D)] = out_t[:D].astype(BF).T
            out_copy(b).start()
            return carry

        lax.fori_loop(0, blocks, block, 0)

    lows = [
        functools.reduce(
            jnp.minimum,
            [
                jnp.where(table[b * LINKED + r] >= 0, table[b * LINKED + r], blocks)
                for b in range(blocks)
            ],
        )
        for r in (2, 3)
    ]
    for b in range(blocks):
        q_rows, do_rows = (stacked(ref, head, b, groups) for ref in (q_v, do_v))
        dv = jnp.dot(pt[b], do_rows, preferred_element_type=F32)
        dk = jnp.dot(dst[b], q_rows, preferred_element_type=F32) * SCALE
        places = [table[b * LINKED + 1 + r] for r in range(3)]
        for r, index in enumerate(places):
            slot = index
            if r:
                slot = jnp.where(index == lows[r - 1], 0, 1) + blocks + (r - 1) * 2
            here = row_span(jnp.where(index >= 0, slot, blocks + 4))
            acc[here, :D] += dk[r * T : (r + 1) * T]
            acc[here, D:] += dv[r * T : (r + 1) * T]
    tokens = blocks * T
    ends = [0, tokens, tokens + 2 * T, tokens + 4 * T]
    for r in range(3):
        sent[r][...] = acc[ends[r] : ends[r + 1]].astype(BF)
    for b in range(blocks):
        out_copy(b).wait()


def stacked(ref, head, b, groups):
    return jnp.concatenate(
        [ref[pl.ds(b * T, T), pl.ds((head * groups + g) * D, D)] for g in range(groups)], 0
    )


def tail_kernel(*refs, head, blocks, groups, chained):
    q_v, do_v, kbn, pn, dpn, dst, kb, stats = refs[:8]
    at = 9 if chained else 8
    dq_out, own_ref = refs[at : at + 2]
    ptn, dsn, dq_buf, out_sem = refs[at + 2 :]

    def out_copy(b):
        rows = pl.ds(b * T, T)
        columns = pl.ds(head * groups * D, groups * D)
        return pltpu.make_async_copy(dq_buf.at[b], dq_out.at[rows, columns], out_sem.at[b])

    pieces = [(b, j, pl.ds(j * T, WIDE * T)) for b in range(blocks) for j in range(0, groups, WIDE)]
    for b, j, col in pieces:
        weights = pn[b, :T, col].astype(F32) * stats[b, :1, col]
        ptn[b, :, col] = weights.astype(BF)
        dsn[b, :, col] = (weights * (dpn[b, :T, col] - stats[b, 8:9, col])).astype(BF)
    for b, j, col in pieces:
        dq_t = lax.dot_general(kbn[b, :T], dsn[b, :, col], TN, preferred_element_type=F32)
        dq_t += lax.dot_general(kb[b], dst[b, :, col], TN, preferred_element_type=F32)
        dq_t = dq_t * SCALE
        for w in range(WIDE):
            dq_buf[b, :, pl.ds((j + w) * D, D)] = dq_t[:, w * T : (w + 1) * T].astype(BF).T
        if j + WIDE == groups:
            out_copy(b).start()
    for b in range(blocks):
        rows = pl.ds(b * T, T)
        q_rows, do_rows = (stacked(ref, head, b, groups) for ref in (q_v, do_v))
        own_ref[rows, :D] = jnp.dot(dsn[b], q_rows, preferred_element_type=F32) * SCALE
        own_ref[rows, D:] = jnp.dot(ptn[b], do_rows, preferred_element_type=F32)
    for b in range(blocks):
        out_copy(b).wait()


def finish_kernel(*refs, heads, blocks):
    table = refs[0]
    dk_ref, dv_ref, acc = refs[-3:]
    at = 1
    for h in range(heads):
        own, core = refs[at : at + 2]
        at += 2
        acc[...] = own[...] + core[...].astype(F32)
        for r in range(2):
            for side in range(2):
                index = jnp.minimum(table[blocks * LINKED + 2 * r + side], blocks - 1)
                acc[row_span(index)] += refs[at + r][pl.ds(side * T, T)].astype(F32)
        at += 2
        dk_ref[:, pl.ds(h * D, D)] = acc[:, :D].astype(BF)
        dv_ref[:, pl.ds(h * D, D)] = acc[:, D:].astype(BF)


def work(microseconds):
    return pl.CostEstimate(flops=int(microseconds * 10**9), bytes_accessed=0, transcendentals=0)


def linked_body(info, queries, output_gradient, packed):
    tokens = queries.shape[0]
    heads = len(packed)
    blocks = tokens // T
    groups = QUERY_HEADS // KEY_VALUE_HEADS
    width = groups * T
    depth = min(PATH_DEPTH_MAX, LINKED)
    core = [(i, i ^ 1) for i in range(LINKED)]
    across = [(i, i ^ 2) for i in range(LINKED)]
    corner = [(i, i ^ 3) for i in range(LINKED)]
    near = [lax.ppermute(own, "ctx", core) for own in packed]
    far = [lax.ppermute(own, "ctx", across) for own in packed]

    vmem = pl.BlockSpec(memory_space=pltpu.VMEM)
    smem = pl.BlockSpec(memory_space=pltpu.SMEM)
    hbm = pl.BlockSpec(memory_space=pl.ANY)
    kept = pltpu.VMEM

    def keep(x):
        return pltpu.with_memory_space_constraint(x, pltpu.VMEM)

    def scalars(x):
        return pltpu.with_memory_space_constraint(x, pltpu.SMEM)

    def near_work(h, local):
        first = local is None
        parts = [
            kept((blocks, 2 * T, D), BF),
            kept((blocks, D + ONES, 2 * T), BF),
            kept((blocks, 2 * T, width), BF),
            kept((blocks, 2 * T, width), F32),
            kept((blocks, D + 8, width), F32),
        ]
        whole = [
            kept(queries.shape, BF),
            kept((blocks, D, heads * width), BF),
            kept((blocks, D, heads * width), BF),
        ]
        table_shape = pltpu.SMEM((blocks * LINKED + 4,), jnp.int32)
        if first:
            wide = pl.BlockSpec(memory_space=pltpu.HBM)
            operands = [
                info,
                kept_queries,
                pltpu.with_memory_space_constraint(output_gradient, pltpu.HBM),
            ]
            in_specs = [smem, vmem, wide]
            out_specs = [smem, smem] + [vmem] * 8
            out_shape = [table_shape, pltpu.SMEM((2,), F32)] + whole + parts
        else:
            operands = [local[0], local[4], local[5]]
            in_specs = [smem, vmem, vmem]
            out_specs = [smem] + [vmem] * 5
            out_shape = [pltpu.SMEM((1,), F32)] + parts
        done = pl.pallas_call(
            functools.partial(
                near_kernel, head=h, blocks=blocks, heads=heads, groups=groups, depth=depth
            ),
            in_specs=in_specs + [hbm, hbm],
            out_specs=out_specs,
            out_shape=out_shape,
            scratch_shapes=[
                pltpu.VMEM((2, tokens, 2 * D), BF),
                pltpu.VMEM((blocks, 2 * T, D), BF),
                pltpu.SemaphoreType.DMA((2,)),
            ]
            + ([pltpu.SemaphoreType.DMA] if first else []),
            compiler_params=pltpu.CompilerParams(vmem_limit_bytes=12 * 2**20),
            cost_estimate=work(4),
            name="near",
        )(*operands, packed[h], near[h])
        return [scalars(x) if x.ndim == 1 else keep(x) for x in done]

    kept_queries = keep(queries)
    shared = near_work(0, None)
    table, top = shared[:2]
    local = [kept_queries] + shared[2:5]
    far[0], _ = lax.optimization_barrier((far[0], shared[9]))
    diagonal = [lax.ppermute(far[0], "ctx", core)]
    near_parts = [[top] + shared[5:]]
    for h in range(1, heads):
        near_parts.append(near_work(h, [table, None] + local))
        far[h], _ = lax.optimization_barrier((far[h], near_parts[h][5]))
        diagonal.append(lax.ppermute(far[h], "ctx", core))

    attended = None
    probs = []
    arrivals = []
    for h in range(heads):
        chained = attended is not None
        sent = [tokens, 2 * T, 2 * T]
        operands = [table, top, near_parts[h][0], *local, *near_parts[h][1:]]
        operands += [keep(far[h]), keep(diagonal[h])]
        done = pl.pallas_call(
            functools.partial(
                far_kernel, head=h, blocks=blocks, groups=groups, chained=chained
            ),
            in_specs=[smem] * 3 + [vmem] * 11 + [hbm] * (1 if chained else 0),
            out_specs=[hbm] + [vmem] * (4 + len(sent)),
            out_shape=[
                jax.ShapeDtypeStruct(queries.shape, BF),
                kept((blocks, 2 * T, width), BF),
                kept((blocks, 3 * T, width), BF),
                kept((blocks, 3 * T, D), BF),
                kept((blocks, 16, width), F32),
            ]
            + [kept((rows, 2 * D), BF) for rows in sent],
            input_output_aliases={9: 1} | ({len(operands): 0} if chained else {}),
            scratch_shapes=[
                pltpu.VMEM((blocks, 3 * T, width), BF),
                pltpu.VMEM((blocks, 2 * T, D), BF),
                pltpu.VMEM((blocks, D + ONES, 2 * T), BF),
                pltpu.VMEM((tokens + 5 * T, 2 * D), F32),
                pltpu.VMEM((blocks, T, groups * D), BF),
                pltpu.SemaphoreType.DMA((blocks,)),
            ],
            compiler_params=pltpu.CompilerParams(vmem_limit_bytes=12 * 2**20),
            cost_estimate=work(5),
            name="far",
        )(*operands, *([attended] if chained else []))
        attended = done[0]
        near_probs, *rest = [keep(x) for x in done[1:5]]
        _, kbn, _, _, dpn, _ = near_parts[h]
        probs.append([kbn, near_probs, dpn, *rest])
        to_core, to_far, to_corner = done[5:]
        arrivals.append(
            [
                lax.ppermute(to_core, "ctx", core),
                lax.ppermute(to_far, "ctx", across),
                lax.ppermute(to_corner, "ctx", corner),
            ]
        )

    d_queries = None
    finishing = [table]
    for h in range(heads):
        chained = d_queries is not None
        operands = [local[0], local[1], *probs[h]]
        if not chained and heads > 1:
            operands[-1], arrivals[0] = lax.optimization_barrier((operands[-1], arrivals[0]))
            operands[-1] = keep(operands[-1])
        done = pl.pallas_call(
            functools.partial(tail_kernel, head=h, blocks=blocks, groups=groups, chained=chained),
            in_specs=[vmem] * 8 + ([hbm] if chained else []),
            out_specs=[hbm, vmem],
            out_shape=[jax.ShapeDtypeStruct(queries.shape, BF), kept((tokens, 2 * D), F32)],
            input_output_aliases={len(operands): 0} if chained else {},
            scratch_shapes=[
                pltpu.VMEM((blocks, T, width), BF),
                pltpu.VMEM((blocks, T, width), BF),
                pltpu.VMEM((blocks, T, groups * D), BF),
                pltpu.SemaphoreType.DMA((blocks,)),
            ],
            compiler_params=pltpu.CompilerParams(vmem_limit_bytes=12 * 2**20),
            cost_estimate=work(1),
            name="tail",
        )(*operands, *([d_queries] if chained else []))
        d_queries = done[0]
        finishing += [keep(done[1])] + [keep(x) for x in arrivals[h]]
    d_keys, d_values = pl.pallas_call(
        functools.partial(finish_kernel, heads=heads, blocks=blocks),
        in_specs=[smem] + [vmem] * (len(finishing) - 1),
        out_specs=[vmem, vmem],
        out_shape=[jax.ShapeDtypeStruct((tokens, heads * D), BF)] * 2,
        scratch_shapes=[pltpu.VMEM((tokens, 2 * D), F32)],
        name="finish",
    )(*finishing)
    return attended, d_queries, d_keys, d_values


def body(queries, key_states, value_tensor, output_gradient, parent, block_owner, shards):
    heads = key_states.shape[1] // D
    me = lax.axis_index("ctx").astype(jnp.int32)
    info = jnp.concatenate([me[None], parent, block_owner])
    packed = [
        jnp.concatenate([key_states[:, h * D : (h + 1) * D], value_tensor[:, h * D : (h + 1) * D]], 1)
        for h in range(heads)
    ]
    if shards == LINKED:
        return linked_body(info, queries, output_gradient, packed)
    outputs = None
    summed = []
    for h in range(heads):
        gathered = lax.all_gather(packed[h], "ctx", axis=0, tiled=True)
        done = attend(info, queries, output_gradient, gathered, outputs, h, shards)
        outputs = done[:2]
        summed.append(lax.psum_scatter(done[2], "ctx", scatter_dimension=0, tiled=True))
    d_keys = jnp.concatenate([s[:, :D] for s in summed], 1).astype(BF)
    d_values = jnp.concatenate([s[:, D:] for s in summed], 1).astype(BF)
    return (outputs[0], outputs[1], d_keys, d_values)


def solution(mesh):
    tokens_split = P(("groups", "ctx"), "tp")
    return jax.shard_map(
        functools.partial(body, shards=mesh.shape["ctx"]),
        mesh=mesh,
        in_specs=(tokens_split,) * 4 + (P("groups"),) * 2,
        out_specs=(tokens_split,) * 4,
        check_vma=False,
    )
```

```python
import functools
import math

import jax
import jax.numpy as jnp
from jax import lax
import jax.experimental.pallas as pl
import jax.experimental.pallas.tpu as pltpu
from jax.sharding import PartitionSpec as P

HEAD_SIZE = 128
TREE_BLOCK_SIZE = 128
PATH_DEPTH_MAX = 16
QUERY_HEADS = 64
KEY_VALUE_HEADS = 8

D = HEAD_SIZE
T = TREE_BLOCK_SIZE
NT = (((1,), (1,)), ((), ()))
TN = (((0,), (0,)), ((), ()))
BF = jnp.bfloat16
F32 = jnp.float32
SCALE = 1.0 / math.sqrt(D)
LOG2E = math.log2(math.e)
LINKED = 4
WIDE = 2
ONES = 16
SAFE_EXPONENT = 96.0


def fill_table(info, table, me, blocks, group_blocks, depth):
    for b in range(blocks):
        mine = me * blocks + b

        def find(t, found):
            return jnp.where(info[1 + group_blocks + t] == mine, t, found)

        current = lax.fori_loop(0, group_blocks, find, jnp.int32(0))
        for d in range(depth):
            if d:
                current = jnp.where(current >= 0, info[1 + jnp.maximum(current, 0)], -1)
            owner = info[1 + group_blocks + jnp.maximum(current, 0)]
            table[b * depth + d] = jnp.where(current >= 0, owner, -1)


def attend_kernel(*refs, head, blocks, group_blocks, depth, groups, chained):
    info, q_ref, do_ref, gathered = refs[:4]
    at = 6 if chained else 4
    o_out, dq_out, sum_ref = refs[at : at + 3]
    kv, acc, kb, vb, pt, dst, o_buf, dq_buf, table, kv_sem, out_sem = refs[at + 3 :]
    source_copy = pltpu.make_async_copy(gathered, kv, kv_sem)
    source_copy.start()
    fill_table(info, table, info[0], blocks, group_blocks, depth)
    acc[...] = jnp.zeros_like(acc)
    source_copy.wait()

    tri = lax.broadcasted_iota(jnp.int32, (T, T), 0) <= lax.broadcasted_iota(jnp.int32, (T, T), 1)

    def place(b, d):
        return pl.ds(pl.multiple_of(jnp.maximum(table[b * depth + d], 0) * T, T), T)

    def out_copies(b):
        rows = pl.ds(pl.multiple_of(b * T, T), T)
        columns = pl.ds(head * groups * D, groups * D)
        return (
            pltpu.make_async_copy(o_buf.at[b], o_out.at[rows, columns], out_sem.at[0, b]),
            pltpu.make_async_copy(dq_buf.at[b], dq_out.at[rows, columns], out_sem.at[1, b]),
        )

    def block(b, carry):
        rows = pl.ds(pl.multiple_of(b * T, T), T)
        for d in range(depth):
            kb[pl.ds(d * T, T), :] = kv[place(b, d), :D]
            vb[pl.ds(d * T, T), :] = kv[place(b, d), D:]
        bias = [
            jnp.where(table[b * depth + d] >= 0, 0.0, -jnp.inf).astype(F32) for d in range(depth)
        ]
        for g in range(groups):
            col = pl.ds(g * T, T)
            head_col = pl.ds((head * groups + g) * D, D)
            scores = lax.dot_general(kb[...], q_ref[rows, head_col], NT, preferred_element_type=F32)
            dprobs = lax.dot_general(vb[...], do_ref[rows, head_col], NT, preferred_element_type=F32)
            parts = [scores[d * T : (d + 1) * T] * (SCALE * LOG2E) for d in range(depth)]
            parts[0] = jnp.where(tri, parts[0], -jnp.inf)
            highs = [jnp.max(x, axis=0, keepdims=True) + bias[d] for d, x in enumerate(parts)]
            high = functools.reduce(jnp.maximum, highs)
            exps = [jnp.exp2(x - (high - bias[d])) for d, x in enumerate(parts)]
            total = functools.reduce(
                jnp.add, [jnp.sum(x, axis=0, keepdims=True) for x in exps]
            )
            inverse = 1.0 / total
            dparts = [dprobs[d * T : (d + 1) * T] for d in range(depth)]
            inner = inverse * functools.reduce(
                jnp.add,
                [jnp.sum(x * y, axis=0, keepdims=True) for x, y in zip(exps, dparts)],
            )
            for d in range(depth):
                weights = exps[d] * inverse
                pt[pl.ds(d * T, T), col] = weights.astype(BF)
                dst[pl.ds(d * T, T), col] = (weights * (dparts[d] - inner)).astype(BF)
        q_rows = jnp.concatenate(
            [q_ref[rows, (head * groups + g) * D : (head * groups + g + 1) * D] for g in range(groups)], 0
        )
        do_rows = jnp.concatenate(
            [do_ref[rows, (head * groups + g) * D : (head * groups + g + 1) * D] for g in range(groups)], 0
        )
        dv = jnp.dot(pt[...], do_rows, preferred_element_type=F32)
        dk = jnp.dot(dst[...], q_rows, preferred_element_type=F32) * SCALE
        for d in range(depth):
            acc[place(b, d), :D] += dk[d * T : (d + 1) * T]
            acc[place(b, d), D:] += dv[d * T : (d + 1) * T]
        out_t = lax.dot_general(vb[...], pt[...], TN, preferred_element_type=F32)
        dq_t = lax.dot_general(kb[...], dst[...], TN, preferred_element_type=F32) * SCALE
        for g in range(groups):
            col = pl.ds(g * T, T)
            o_buf[b, :, col] = out_t[:, g * T : (g + 1) * T].T.astype(BF)
            dq_buf[b, :, col] = dq_t[:, g * T : (g + 1) * T].T.astype(BF)
        for copy in out_copies(b):
            copy.start()
        return carry

    lax.fori_loop(0, blocks, block, 0)
    sum_ref[...] = acc[...]
    for b in range(blocks):
        for copy in out_copies(b):
            copy.wait()


def attend(info, queries, output_gradient, gathered, outputs, head, shards):
    tokens = queries.shape[0]
    blocks = tokens // T
    group_blocks = blocks * shards
    depth = min(PATH_DEPTH_MAX, shards)
    groups = QUERY_HEADS // KEY_VALUE_HEADS
    vmem = pl.BlockSpec(memory_space=pltpu.VMEM)
    hbm = pl.BlockSpec(memory_space=pl.ANY)
    chained = outputs is not None
    operands = [
        info,
        pltpu.with_memory_space_constraint(queries, pltpu.VMEM),
        pltpu.with_memory_space_constraint(output_gradient, pltpu.VMEM),
        gathered,
        *(outputs if chained else ()),
    ]
    in_specs = [pl.BlockSpec(memory_space=pltpu.SMEM), vmem, vmem]
    in_specs += [hbm] * (len(operands) - 3)
    full = jax.ShapeDtypeStruct(queries.shape, BF)
    total_rows = tokens * shards
    sums = [jax.ShapeDtypeStruct((total_rows, 2 * D), F32)]
    kernel = functools.partial(
        attend_kernel,
        head=head,
        blocks=blocks,
        group_blocks=group_blocks,
        depth=depth,
        groups=groups,
        chained=chained,
    )
    flops = 12 * blocks * groups * depth * T * T * D
    return pl.pallas_call(
        kernel,
        in_specs=in_specs,
        out_specs=[hbm, hbm] + [vmem] * len(sums),
        out_shape=[full, full] + sums,
        input_output_aliases={4: 0, 5: 1} if chained else {},
        scratch_shapes=[
            pltpu.VMEM((total_rows, 2 * D), BF),
            pltpu.VMEM((total_rows, 2 * D), F32),
            pltpu.VMEM((depth * T, D), BF),
            pltpu.VMEM((depth * T, D), BF),
            pltpu.VMEM((depth * T, groups * T), BF),
            pltpu.VMEM((depth * T, groups * T), BF),
            pltpu.VMEM((blocks, T, groups * D), BF),
            pltpu.VMEM((blocks, T, groups * D), BF),
            pltpu.SMEM((blocks * depth,), jnp.int32),
            pltpu.SemaphoreType.DMA,
            pltpu.SemaphoreType.DMA((2, blocks)),
        ],
        compiler_params=pltpu.CompilerParams(vmem_limit_bytes=40 * 2**20),
        cost_estimate=pl.CostEstimate(
            flops=2 * flops, bytes_accessed=8 * tokens * groups * D, transcendentals=0
        ),
        name="attend",
    )(*operands)


def relation_table(info, table, blocks, depth):
    me = info[0]
    group_blocks = blocks * LINKED

    def walk(block, visit):
        current = jnp.int32(0)
        for t in range(group_blocks):
            current = jnp.where(info[1 + group_blocks + t] == block, t, current)
        for d in range(depth):
            if d:
                current = jnp.where(current >= 0, info[1 + jnp.maximum(current, 0)], -1)
            owner = info[1 + group_blocks + jnp.maximum(current, 0)]
            shard = lax.div(owner, jnp.int32(blocks))
            visit(current >= 0, shard, owner - shard * blocks)

    for b in range(blocks):
        for r in range(LINKED):
            table[b * LINKED + r] = -1

        def visit(live, shard, index):
            slot = b * LINKED + (shard ^ me)
            table[slot] = jnp.where(live, index, table[slot])

        walk(me * blocks + b, visit)
    for r in range(2):
        ends = [jnp.int32(blocks), jnp.int32(-1)]

        def visit(live, shard, index):
            mine = jnp.logical_and(live, shard == me)
            ends[0] = jnp.where(mine, jnp.minimum(ends[0], index), ends[0])
            ends[1] = jnp.where(mine, jnp.maximum(ends[1], index), ends[1])

        for b in range(blocks):
            walk((me ^ (2 + r)) * blocks + b, visit)
        for side in range(2):
            table[blocks * LINKED + 2 * r + side] = ends[side]


def row_span(index):
    return pl.ds(pl.multiple_of(jnp.maximum(index, 0) * T, T), T)


def live_factor(index):
    return jnp.where(index >= 0, 1.0, 0.0).astype(BF)


def norm_top(rows):
    wide = rows.astype(F32)
    return jnp.max(jnp.sum(wide * wide, axis=1, keepdims=True))


def causal(width):
    keys = lax.broadcasted_iota(jnp.int32, (T, T), 0)
    queries = lax.broadcasted_iota(jnp.int32, (T, T), 1)
    return jnp.concatenate([keys <= queries] * width, 1)


def near_kernel(*refs, head, blocks, heads, groups, depth):
    if head == 0:
        info, q_v, do_in, own, near = refs[:5]
        table, top, do_v, qt, dt, kbn, vtn, pn, dpn, on = refs[5:15]
        kv, vb, kv_sem, row_sem = refs[15:]
    else:
        table, qt, dt, own, near = refs[:5]
        top, kbn, vtn, pn, dpn, on = refs[5:11]
        kv, vb, kv_sem = refs[11:]

    kv_copies = [
        pltpu.make_async_copy(source, kv.at[i], kv_sem.at[i]) for i, source in enumerate((own, near))
    ]
    for copy in kv_copies:
        copy.start()
    if head == 0:

        do_copy = pltpu.make_async_copy(do_in, do_v, row_sem)
        do_copy.start()
        relation_table(info, table, blocks, depth)
        highest = jnp.zeros((1, heads * groups * T), F32)
        for b in range(blocks):
            for g in range(heads * groups):
                col = pl.ds(g * D, D)
                qt[b, :, col] = q_v[pl.ds(b * T, T), col].T
            wide = qt[b].astype(F32)
            highest = jnp.maximum(highest, jnp.sum(wide * wide, axis=0, keepdims=True))
        top[0] = jnp.max(highest)
    for copy in kv_copies:
        copy.wait()
    top[1 if head == 0 else 0] = jnp.maximum(norm_top(kv[0, :, :D]), norm_top(kv[1, :, :D]))
    for b in range(blocks):
        for r in range(2):
            index = table[b * LINKED + r]
            here = pl.ds(r * T, T)
            kbn[b, here, :] = kv[r, row_span(index), :D] * live_factor(index)
            values = kv[r, row_span(index), D:] * live_factor(index)
            vb[b, here, :] = values
            vtn[b, :D, here] = values.T
            vtn[b, D:, here] = jnp.full((ONES, T), live_factor(index), BF)
    tri = causal(WIDE)
    pieces = [
        (b, pl.ds(j * T, WIDE * T), pl.ds((head * groups + j) * D, WIDE * D))
        for b in range(blocks)
        for j in range(0, groups, WIDE)
    ]
    for b, col, head_col in pieces:
        scores = jnp.dot(kbn[b], qt[b, :, head_col], preferred_element_type=F32)
        exps = jnp.exp2(scores * (SCALE * LOG2E))
        pn[b, :T, col] = jnp.where(tri, exps[:T], 0.0).astype(BF)
        pn[b, T:, col] = exps[T:].astype(BF)
    if head == 0:
        do_copy.wait()
        for b in range(blocks):
            for g in range(heads * groups):
                col = pl.ds(g * D, D)
                dt[b, :, col] = do_v[pl.ds(b * T, T), col].T
    for b, col, head_col in pieces:
        dpn[b, :, col] = jnp.dot(vb[b], dt[b, :, head_col], preferred_element_type=F32)
    for b, col, head_col in pieces:
        on[b, :, col] = jnp.dot(vtn[b], pn[b, :, col], preferred_element_type=F32)[: D + 8]


def far_kernel(*refs, head, blocks, groups, chained):
    table, top, near_top, q_v, do_v, qt, dt, kbn, vtn, pn, dpn, on = refs[:12]
    sources = refs[12:14]
    at = 15 if chained else 14
    o_out, pn_out, dst, kb, stats = refs[at : at + 5]
    sent = refs[at + 5 : at + 8]
    pt, vb, vt, acc, o_buf, out_sem = refs[at + 8 :]
    acc[...] = jnp.zeros_like(acc)
    for b in range(blocks):
        kb[b, :T, :] = kbn[b, T:]
        for r in range(2):
            index = table[b * LINKED + 2 + r]
            here = pl.ds(r * T, T)
            kb[b, pl.ds((1 + r) * T, T), :] = sources[r][row_span(index), :D] * live_factor(index)
            values = sources[r][row_span(index), D:] * live_factor(index)
            vb[b, here, :] = values
            vt[b, :D, here] = values.T
            vt[b, D:, here] = jnp.full((ONES, T), live_factor(index), BF)

    def out_copy(b):
        rows = pl.ds(pl.multiple_of(b * T, T), T)
        columns = pl.ds(head * groups * D, groups * D)
        return pltpu.make_async_copy(o_buf.at[b], o_out.at[rows, columns], out_sem.at[b])

    keys_top = jnp.maximum(norm_top(sources[0][:, :D]), norm_top(sources[1][:, :D]))
    keys_top = jnp.maximum(keys_top, near_top[1 if head == 0 else 0])
    safe = top[0] * keys_top <= (SAFE_EXPONENT / (SCALE * LOG2E)) ** 2

    @pl.when(safe)
    def _():
        pieces = [
            (b, j, pl.ds(j * T, WIDE * T), pl.ds((head * groups + j) * D, WIDE * D))
            for b in range(blocks)
            for j in range(0, groups, WIDE)
        ]
        for b, j, col, head_col in pieces:
            scores = jnp.dot(kb[b, T:], qt[b, :, head_col], preferred_element_type=F32)
            pt[b, T:, col] = jnp.exp2(scores * (SCALE * LOG2E)).astype(BF)
        for b, j, col, head_col in pieces:
            sums = jnp.dot(vt[b], pt[b, T:, col], preferred_element_type=F32)
            sums = sums[: D + 8] + on[b, :, col]
            inverse = 1.0 / sums[D : D + 1]
            out_t = (sums[:D] * inverse).astype(BF)
            inner = jnp.sum(
                out_t.astype(F32) * dt[b, :, head_col].astype(F32), axis=0, keepdims=True
            )
            stats[b, :8, col] = jnp.broadcast_to(inverse, (8, WIDE * T))
            stats[b, 8:, col] = jnp.broadcast_to(inner, (8, WIDE * T))
            for w in range(WIDE):
                o_buf[b, :, pl.ds((j + w) * D, D)] = out_t[:, w * T : (w + 1) * T].T
            if j + WIDE == groups:
                out_copy(b).start()
        for b, j, col, head_col in pieces:
            dprobs = jnp.dot(vb[b], dt[b, :, head_col], preferred_element_type=F32)
            weights = pt[b, T:, col].astype(F32) * stats[b, :1, col]
            pt[b, T:, col] = weights.astype(BF)
            dst[b, T:, col] = (weights * (dprobs - stats[b, 8:9, col])).astype(BF)
        for b, j, col, head_col in pieces:
            weights = pn[b, T:, col].astype(F32) * stats[b, :1, col]
            pt[b, :T, col] = weights.astype(BF)
            dst[b, :T, col] = (weights * (dpn[b, T:, col] - stats[b, 8:9, col])).astype(BF)

    @pl.when(jnp.logical_not(safe))
    def _():
        tri = causal(1)

        def block(b, carry):
            bias = [
                jnp.where(table[b * LINKED + r] >= 0, 0.0, -jnp.inf).astype(F32)
                for r in range(LINKED)
            ]
            for g in range(groups):
                col = pl.ds(g * T, T)
                head_col = pl.ds((head * groups + g) * D, D)
                near_scores = jnp.dot(kbn[b], qt[b, :, head_col], preferred_element_type=F32)
                scores = jnp.dot(kb[b, T:], qt[b, :, head_col], preferred_element_type=F32)
                dprobs = jnp.dot(vb[b], dt[b, :, head_col], preferred_element_type=F32)
                dparts = [dpn[b, :T, col], dpn[b, T:, col], dprobs[:T], dprobs[T:]]
                parts = [near_scores[:T], near_scores[T:], scores[:T], scores[T:]]
                parts = [x * (SCALE * LOG2E) for x in parts]
                parts[0] = jnp.where(tri, parts[0], -jnp.inf)
                highs = [jnp.max(x, axis=0, keepdims=True) + bias[r] for r, x in enumerate(parts)]
                high = functools.reduce(jnp.maximum, highs)
                exps = [jnp.exp2(x - (high - bias[r])) for r, x in enumerate(parts)]
                total = functools.reduce(
                    jnp.add, [jnp.sum(x, axis=0, keepdims=True) for x in exps]
                )
                inverse = 1.0 / total
                for r in range(LINKED):
                    weights = (exps[r] * inverse).astype(BF)
                    if r < 2:
                        pn_out[b, pl.ds(r * T, T), col] = weights
                    if r > 0:
                        pt[b, pl.ds((r - 1) * T, T), col] = weights
                out_t = jnp.dot(
                    vtn[b], pn_out[b, :, col], preferred_element_type=F32
                ) + jnp.dot(vt[b], pt[b, T:, col], preferred_element_type=F32)
                out_t = out_t[:D].astype(BF)
                inner = jnp.sum(
                    out_t.astype(F32) * dt[b, :, head_col].astype(F32), axis=0, keepdims=True
                )
                stats[b, :8, col] = jnp.ones((8, T), F32)
                stats[b, 8:, col] = jnp.broadcast_to(inner, (8, T))
                for r in range(3):
                    dscores = exps[1 + r] * inverse * (dparts[1 + r] - inner)
                    dst[b, pl.ds(r * T, T), col] = dscores.astype(BF)
                o_buf[b, :, pl.ds(g * D, D)] = out_t.T
            out_copy(b).start()
            return carry

        lax.fori_loop(0, blocks, block, 0)

    lows = [
        functools.reduce(
            jnp.minimum,
            [
                jnp.where(table[b * LINKED + r] >= 0, table[b * LINKED + r], blocks)
                for b in range(blocks)
            ],
        )
        for r in (2, 3)
    ]
    for b in range(blocks):
        q_rows, do_rows = (stacked(ref, head, b, groups) for ref in (q_v, do_v))
        dv = jnp.dot(pt[b], do_rows, preferred_element_type=F32)
        dk = jnp.dot(dst[b], q_rows, preferred_element_type=F32) * SCALE
        places = [table[b * LINKED + 1 + r] for r in range(3)]
        for r, index in enumerate(places):
            slot = index
            if r:
                slot = jnp.where(index == lows[r - 1], 0, 1) + blocks + (r - 1) * 2
            here = row_span(jnp.where(index >= 0, slot, blocks + 4))
            acc[here, :D] += dk[r * T : (r + 1) * T]
            acc[here, D:] += dv[r * T : (r + 1) * T]
    tokens = blocks * T
    ends = [0, tokens, tokens + 2 * T, tokens + 4 * T]
    for r in range(3):
        sent[r][...] = acc[ends[r] : ends[r + 1]].astype(BF)
    for b in range(blocks):
        out_copy(b).wait()


def stacked(ref, head, b, groups):
    return jnp.concatenate(
        [ref[pl.ds(b * T, T), pl.ds((head * groups + g) * D, D)] for g in range(groups)], 0
    )


def tail_kernel(*refs, head, blocks, groups, chained):
    q_v, do_v, kbn, pn, dpn, dst, kb, stats = refs[:8]
    at = 9 if chained else 8
    dq_out, own_ref = refs[at : at + 2]
    ptn, dsn, dq_buf, out_sem = refs[at + 2 :]

    def out_copy(b):
        rows = pl.ds(b * T, T)
        columns = pl.ds(head * groups * D, groups * D)
        return pltpu.make_async_copy(dq_buf.at[b], dq_out.at[rows, columns], out_sem.at[b])

    pieces = [(b, j, pl.ds(j * T, WIDE * T)) for b in range(blocks) for j in range(0, groups, WIDE)]
    for b, j, col in pieces:
        weights = pn[b, :T, col].astype(F32) * stats[b, :1, col]
        ptn[b, :, col] = weights.astype(BF)
        dsn[b, :, col] = (weights * (dpn[b, :T, col] - stats[b, 8:9, col])).astype(BF)
    for b, j, col in pieces:
        dq_t = lax.dot_general(kbn[b, :T], dsn[b, :, col], TN, preferred_element_type=F32)
        dq_t += lax.dot_general(kb[b], dst[b, :, col], TN, preferred_element_type=F32)
        dq_t = dq_t * SCALE
        for w in range(WIDE):
            dq_buf[b, :, pl.ds((j + w) * D, D)] = dq_t[:, w * T : (w + 1) * T].astype(BF).T
        if j + WIDE == groups:
            out_copy(b).start()
    for b in range(blocks):
        rows = pl.ds(b * T, T)
        q_rows, do_rows = (stacked(ref, head, b, groups) for ref in (q_v, do_v))
        own_ref[rows, :D] = jnp.dot(dsn[b], q_rows, preferred_element_type=F32) * SCALE
        own_ref[rows, D:] = jnp.dot(ptn[b], do_rows, preferred_element_type=F32)
    for b in range(blocks):
        out_copy(b).wait()


def finish_kernel(*refs, heads, blocks):
    table = refs[0]
    dk_ref, dv_ref, acc = refs[-3:]
    at = 1
    for h in range(heads):
        own, core = refs[at : at + 2]
        at += 2
        acc[...] = own[...] + core[...].astype(F32)
        for r in range(2):
            for side in range(2):
                index = jnp.minimum(table[blocks * LINKED + 2 * r + side], blocks - 1)
                acc[row_span(index)] += refs[at + r][pl.ds(side * T, T)].astype(F32)
        at += 2
        dk_ref[:, pl.ds(h * D, D)] = acc[:, :D].astype(BF)
        dv_ref[:, pl.ds(h * D, D)] = acc[:, D:].astype(BF)


def work(microseconds):
    return pl.CostEstimate(flops=int(microseconds * 10**9), bytes_accessed=0, transcendentals=0)


def linked_body(info, queries, output_gradient, packed):
    tokens = queries.shape[0]
    heads = len(packed)
    blocks = tokens // T
    groups = QUERY_HEADS // KEY_VALUE_HEADS
    width = groups * T
    depth = min(PATH_DEPTH_MAX, LINKED)
    core = [(i, i ^ 1) for i in range(LINKED)]
    across = [(i, i ^ 2) for i in range(LINKED)]
    corner = [(i, i ^ 3) for i in range(LINKED)]
    near = [lax.ppermute(own, "ctx", core) for own in packed]
    far = [lax.ppermute(own, "ctx", across) for own in packed]

    vmem = pl.BlockSpec(memory_space=pltpu.VMEM)
    smem = pl.BlockSpec(memory_space=pltpu.SMEM)
    hbm = pl.BlockSpec(memory_space=pl.ANY)
    kept = pltpu.VMEM

    def keep(x):
        return pltpu.with_memory_space_constraint(x, pltpu.VMEM)

    def scalars(x):
        return pltpu.with_memory_space_constraint(x, pltpu.SMEM)

    def near_work(h, local):
        first = local is None
        parts = [
            kept((blocks, 2 * T, D), BF),
            kept((blocks, D + ONES, 2 * T), BF),
            kept((blocks, 2 * T, width), BF),
            kept((blocks, 2 * T, width), F32),
            kept((blocks, D + 8, width), F32),
        ]
        whole = [
            kept(queries.shape, BF),
            kept((blocks, D, heads * width), BF),
            kept((blocks, D, heads * width), BF),
        ]
        table_shape = pltpu.SMEM((blocks * LINKED + 4,), jnp.int32)
        if first:
            wide = pl.BlockSpec(memory_space=pltpu.HBM)
            operands = [
                info,
                kept_queries,
                pltpu.with_memory_space_constraint(output_gradient, pltpu.HBM),
            ]
            in_specs = [smem, vmem, wide]
            out_specs = [smem, smem] + [vmem] * 8
            out_shape = [table_shape, pltpu.SMEM((2,), F32)] + whole + parts
        else:
            operands = [local[0], local[4], local[5]]
            in_specs = [smem, vmem, vmem]
            out_specs = [smem] + [vmem] * 5
            out_shape = [pltpu.SMEM((1,), F32)] + parts
        done = pl.pallas_call(
            functools.partial(
                near_kernel, head=h, blocks=blocks, heads=heads, groups=groups, depth=depth
            ),
            in_specs=in_specs + [hbm, hbm],
            out_specs=out_specs,
            out_shape=out_shape,
            scratch_shapes=[
                pltpu.VMEM((2, tokens, 2 * D), BF),
                pltpu.VMEM((blocks, 2 * T, D), BF),
                pltpu.SemaphoreType.DMA((2,)),
            ]
            + ([pltpu.SemaphoreType.DMA] if first else []),
            compiler_params=pltpu.CompilerParams(vmem_limit_bytes=12 * 2**20),
            cost_estimate=work(4),
            name="near",
        )(*operands, packed[h], near[h])
        return [scalars(x) if x.ndim == 1 else keep(x) for x in done]

    kept_queries = keep(queries)
    shared = near_work(0, None)
    table, top = shared[:2]
    local = [kept_queries] + shared[2:5]
    far[0], _ = lax.optimization_barrier((far[0], shared[9]))
    diagonal = [lax.ppermute(far[0], "ctx", core)]
    near_parts = [[top] + shared[5:]]
    for h in range(1, heads):
        near_parts.append(near_work(h, [table, None] + local))
        far[h], _ = lax.optimization_barrier((far[h], near_parts[h][5]))
        diagonal.append(lax.ppermute(far[h], "ctx", core))

    attended = None
    probs = []
    arrivals = []
    for h in range(heads):
        chained = attended is not None
        sent = [tokens, 2 * T, 2 * T]
        operands = [table, top, near_parts[h][0], *local, *near_parts[h][1:]]
        operands += [keep(far[h]), keep(diagonal[h])]
        done = pl.pallas_call(
            functools.partial(
                far_kernel, head=h, blocks=blocks, groups=groups, chained=chained
            ),
            in_specs=[smem] * 3 + [vmem] * 11 + [hbm] * (1 if chained else 0),
            out_specs=[hbm] + [vmem] * (4 + len(sent)),
            out_shape=[
                jax.ShapeDtypeStruct(queries.shape, BF),
                kept((blocks, 2 * T, width), BF),
                kept((blocks, 3 * T, width), BF),
                kept((blocks, 3 * T, D), BF),
                kept((blocks, 16, width), F32),
            ]
            + [kept((rows, 2 * D), BF) for rows in sent],
            input_output_aliases={9: 1} | ({len(operands): 0} if chained else {}),
            scratch_shapes=[
                pltpu.VMEM((blocks, 3 * T, width), BF),
                pltpu.VMEM((blocks, 2 * T, D), BF),
                pltpu.VMEM((blocks, D + ONES, 2 * T), BF),
                pltpu.VMEM((tokens + 5 * T, 2 * D), F32),
                pltpu.VMEM((blocks, T, groups * D), BF),
                pltpu.SemaphoreType.DMA((blocks,)),
            ],
            compiler_params=pltpu.CompilerParams(vmem_limit_bytes=12 * 2**20),
            cost_estimate=work(5),
            name="far",
        )(*operands, *([attended] if chained else []))
        attended = done[0]
        near_probs, *rest = [keep(x) for x in done[1:5]]
        _, kbn, _, _, dpn, _ = near_parts[h]
        probs.append([kbn, near_probs, dpn, *rest])
        to_core, to_far, to_corner = done[5:]
        arrivals.append(
            [
                lax.ppermute(to_core, "ctx", core),
                lax.ppermute(to_far, "ctx", across),
                lax.ppermute(to_corner, "ctx", corner),
            ]
        )

    d_queries = None
    finishing = [table]
    for h in range(heads):
        chained = d_queries is not None
        operands = [local[0], local[1], *probs[h]]
        if not chained and heads > 1:
            operands[-1], arrivals[0] = lax.optimization_barrier((operands[-1], arrivals[0]))
            operands[-1] = keep(operands[-1])
        done = pl.pallas_call(
            functools.partial(tail_kernel, head=h, blocks=blocks, groups=groups, chained=chained),
            in_specs=[vmem] * 8 + ([hbm] if chained else []),
            out_specs=[hbm, vmem],
            out_shape=[jax.ShapeDtypeStruct(queries.shape, BF), kept((tokens, 2 * D), F32)],
            input_output_aliases={len(operands): 0} if chained else {},
            scratch_shapes=[
                pltpu.VMEM((blocks, T, width), BF),
                pltpu.VMEM((blocks, T, width), BF),
                pltpu.VMEM((blocks, T, groups * D), BF),
                pltpu.SemaphoreType.DMA((blocks,)),
            ],
            compiler_params=pltpu.CompilerParams(vmem_limit_bytes=12 * 2**20),
            cost_estimate=work(1),
            name="tail",
        )(*operands, *([d_queries] if chained else []))
        d_queries = done[0]
        finishing += [keep(done[1])] + [keep(x) for x in arrivals[h]]
    d_keys, d_values = pl.pallas_call(
        functools.partial(finish_kernel, heads=heads, blocks=blocks),
        in_specs=[smem] + [vmem] * (len(finishing) - 1),
        out_specs=[vmem, vmem],
        out_shape=[jax.ShapeDtypeStruct((tokens, heads * D), BF)] * 2,
        scratch_shapes=[pltpu.VMEM((tokens, 2 * D), F32)],
        name="finish",
    )(*finishing)
    return attended, d_queries, d_keys, d_values


def body(queries, key_states, value_tensor, output_gradient, parent, block_owner, shards):
    heads = key_states.shape[1] // D
    me = lax.axis_index("ctx").astype(jnp.int32)
    info = jnp.concatenate([me[None], parent, block_owner])
    packed = [
        jnp.concatenate([key_states[:, h * D : (h + 1) * D], value_tensor[:, h * D : (h + 1) * D]], 1)
        for h in range(heads)
    ]
    if shards == LINKED:
        return linked_body(info, queries, output_gradient, packed)
    outputs = None
    summed = []
    for h in range(heads):
        gathered = lax.all_gather(packed[h], "ctx", axis=0, tiled=True)
        done = attend(info, queries, output_gradient, gathered, outputs, h, shards)
        outputs = done[:2]
        summed.append(lax.psum_scatter(done[2], "ctx", scatter_dimension=0, tiled=True))
    d_keys = jnp.concatenate([s[:, :D] for s in summed], 1).astype(BF)
    d_values = jnp.concatenate([s[:, D:] for s in summed], 1).astype(BF)
    return (outputs[0], outputs[1], d_keys, d_values)


def solution(mesh):
    tokens_split = P(("groups", "ctx"), "tp")
    return jax.shard_map(
        functools.partial(body, shards=mesh.shape["ctx"]),
        mesh=mesh,
        in_specs=(tokens_split,) * 4 + (P("groups"),) * 2,
        out_specs=(tokens_split,) * 4,
        check_vma=False,
    )
```

```python
import functools
import math

import jax
import jax.numpy as jnp
from jax import lax
import jax.experimental.pallas as pl
import jax.experimental.pallas.tpu as pltpu
from jax.sharding import PartitionSpec as P

HEAD_SIZE = 128
TREE_BLOCK_SIZE = 128
PATH_DEPTH_MAX = 16
QUERY_HEADS = 64
KEY_VALUE_HEADS = 8

D = HEAD_SIZE
T = TREE_BLOCK_SIZE
NT = (((1,), (1,)), ((), ()))
TN = (((0,), (0,)), ((), ()))
BF = jnp.bfloat16
F32 = jnp.float32
SCALE = 1.0 / math.sqrt(D)
LOG2E = math.log2(math.e)
LINKED = 4
WIDE = 2
ONES = 16
SAFE_EXPONENT = 96.0


def fill_table(info, table, me, blocks, group_blocks, depth):
    for b in range(blocks):
        mine = me * blocks + b

        def find(t, found):
            return jnp.where(info[1 + group_blocks + t] == mine, t, found)

        current = lax.fori_loop(0, group_blocks, find, jnp.int32(0))
        for d in range(depth):
            if d:
                current = jnp.where(current >= 0, info[1 + jnp.maximum(current, 0)], -1)
            owner = info[1 + group_blocks + jnp.maximum(current, 0)]
            table[b * depth + d] = jnp.where(current >= 0, owner, -1)


def attend_kernel(*refs, head, blocks, group_blocks, depth, groups, chained):
    info, q_ref, do_ref, gathered = refs[:4]
    at = 6 if chained else 4
    o_out, dq_out, sum_ref = refs[at : at + 3]
    kv, acc, kb, vb, pt, dst, o_buf, dq_buf, table, kv_sem, out_sem = refs[at + 3 :]
    source_copy = pltpu.make_async_copy(gathered, kv, kv_sem)
    source_copy.start()
    fill_table(info, table, info[0], blocks, group_blocks, depth)
    acc[...] = jnp.zeros_like(acc)
    source_copy.wait()

    tri = lax.broadcasted_iota(jnp.int32, (T, T), 0) <= lax.broadcasted_iota(jnp.int32, (T, T), 1)

    def place(b, d):
        return pl.ds(pl.multiple_of(jnp.maximum(table[b * depth + d], 0) * T, T), T)

    def out_copies(b):
        rows = pl.ds(pl.multiple_of(b * T, T), T)
        columns = pl.ds(head * groups * D, groups * D)
        return (
            pltpu.make_async_copy(o_buf.at[b], o_out.at[rows, columns], out_sem.at[0, b]),
            pltpu.make_async_copy(dq_buf.at[b], dq_out.at[rows, columns], out_sem.at[1, b]),
        )

    def block(b, carry):
        rows = pl.ds(pl.multiple_of(b * T, T), T)
        for d in range(depth):
            kb[pl.ds(d * T, T), :] = kv[place(b, d), :D]
            vb[pl.ds(d * T, T), :] = kv[place(b, d), D:]
        bias = [
            jnp.where(table[b * depth + d] >= 0, 0.0, -jnp.inf).astype(F32) for d in range(depth)
        ]
        for g in range(groups):
            col = pl.ds(g * T, T)
            head_col = pl.ds((head * groups + g) * D, D)
            scores = lax.dot_general(kb[...], q_ref[rows, head_col], NT, preferred_element_type=F32)
            dprobs = lax.dot_general(vb[...], do_ref[rows, head_col], NT, preferred_element_type=F32)
            parts = [scores[d * T : (d + 1) * T] * (SCALE * LOG2E) for d in range(depth)]
            parts[0] = jnp.where(tri, parts[0], -jnp.inf)
            highs = [jnp.max(x, axis=0, keepdims=True) + bias[d] for d, x in enumerate(parts)]
            high = functools.reduce(jnp.maximum, highs)
            exps = [jnp.exp2(x - (high - bias[d])) for d, x in enumerate(parts)]
            total = functools.reduce(
                jnp.add, [jnp.sum(x, axis=0, keepdims=True) for x in exps]
            )
            inverse = 1.0 / total
            dparts = [dprobs[d * T : (d + 1) * T] for d in range(depth)]
            inner = inverse * functools.reduce(
                jnp.add,
                [jnp.sum(x * y, axis=0, keepdims=True) for x, y in zip(exps, dparts)],
            )
            for d in range(depth):
                weights = exps[d] * inverse
                pt[pl.ds(d * T, T), col] = weights.astype(BF)
                dst[pl.ds(d * T, T), col] = (weights * (dparts[d] - inner)).astype(BF)
        q_rows = jnp.concatenate(
            [q_ref[rows, (head * groups + g) * D : (head * groups + g + 1) * D] for g in range(groups)], 0
        )
        do_rows = jnp.concatenate(
            [do_ref[rows, (head * groups + g) * D : (head * groups + g + 1) * D] for g in range(groups)], 0
        )
        dv = jnp.dot(pt[...], do_rows, preferred_element_type=F32)
        dk = jnp.dot(dst[...], q_rows, preferred_element_type=F32) * SCALE
        for d in range(depth):
            acc[place(b, d), :D] += dk[d * T : (d + 1) * T]
            acc[place(b, d), D:] += dv[d * T : (d + 1) * T]
        out_t = lax.dot_general(vb[...], pt[...], TN, preferred_element_type=F32)
        dq_t = lax.dot_general(kb[...], dst[...], TN, preferred_element_type=F32) * SCALE
        for g in range(groups):
            col = pl.ds(g * T, T)
            o_buf[b, :, col] = out_t[:, g * T : (g + 1) * T].T.astype(BF)
            dq_buf[b, :, col] = dq_t[:, g * T : (g + 1) * T].T.astype(BF)
        for copy in out_copies(b):
            copy.start()
        return carry

    lax.fori_loop(0, blocks, block, 0)
    sum_ref[...] = acc[...]
    for b in range(blocks):
        for copy in out_copies(b):
            copy.wait()


def attend(info, queries, output_gradient, gathered, outputs, head, shards):
    tokens = queries.shape[0]
    blocks = tokens // T
    group_blocks = blocks * shards
    depth = min(PATH_DEPTH_MAX, shards)
    groups = QUERY_HEADS // KEY_VALUE_HEADS
    vmem = pl.BlockSpec(memory_space=pltpu.VMEM)
    hbm = pl.BlockSpec(memory_space=pl.ANY)
    chained = outputs is not None
    operands = [
        info,
        pltpu.with_memory_space_constraint(queries, pltpu.VMEM),
        pltpu.with_memory_space_constraint(output_gradient, pltpu.VMEM),
        gathered,
        *(outputs if chained else ()),
    ]
    in_specs = [pl.BlockSpec(memory_space=pltpu.SMEM), vmem, vmem]
    in_specs += [hbm] * (len(operands) - 3)
    full = jax.ShapeDtypeStruct(queries.shape, BF)
    total_rows = tokens * shards
    sums = [jax.ShapeDtypeStruct((total_rows, 2 * D), F32)]
    kernel = functools.partial(
        attend_kernel,
        head=head,
        blocks=blocks,
        group_blocks=group_blocks,
        depth=depth,
        groups=groups,
        chained=chained,
    )
    flops = 12 * blocks * groups * depth * T * T * D
    return pl.pallas_call(
        kernel,
        in_specs=in_specs,
        out_specs=[hbm, hbm] + [vmem] * len(sums),
        out_shape=[full, full] + sums,
        input_output_aliases={4: 0, 5: 1} if chained else {},
        scratch_shapes=[
            pltpu.VMEM((total_rows, 2 * D), BF),
            pltpu.VMEM((total_rows, 2 * D), F32),
            pltpu.VMEM((depth * T, D), BF),
            pltpu.VMEM((depth * T, D), BF),
            pltpu.VMEM((depth * T, groups * T), BF),
            pltpu.VMEM((depth * T, groups * T), BF),
            pltpu.VMEM((blocks, T, groups * D), BF),
            pltpu.VMEM((blocks, T, groups * D), BF),
            pltpu.SMEM((blocks * depth,), jnp.int32),
            pltpu.SemaphoreType.DMA,
            pltpu.SemaphoreType.DMA((2, blocks)),
        ],
        compiler_params=pltpu.CompilerParams(vmem_limit_bytes=40 * 2**20),
        cost_estimate=pl.CostEstimate(
            flops=2 * flops, bytes_accessed=8 * tokens * groups * D, transcendentals=0
        ),
        name="attend",
    )(*operands)


def relation_table(info, table, blocks, depth):
    me = info[0]
    group_blocks = blocks * LINKED

    def walk(block, visit):
        current = jnp.int32(0)
        for t in range(group_blocks):
            current = jnp.where(info[1 + group_blocks + t] == block, t, current)
        for d in range(depth):
            if d:
                current = jnp.where(current >= 0, info[1 + jnp.maximum(current, 0)], -1)
            owner = info[1 + group_blocks + jnp.maximum(current, 0)]
            shard = lax.div(owner, jnp.int32(blocks))
            visit(current >= 0, shard, owner - shard * blocks)

    for b in range(blocks):
        for r in range(LINKED):
            table[b * LINKED + r] = -1

        def visit(live, shard, index):
            slot = b * LINKED + (shard ^ me)
            table[slot] = jnp.where(live, index, table[slot])

        walk(me * blocks + b, visit)
    for r in range(2):
        ends = [jnp.int32(blocks), jnp.int32(-1)]

        def visit(live, shard, index):
            mine = jnp.logical_and(live, shard == me)
            ends[0] = jnp.where(mine, jnp.minimum(ends[0], index), ends[0])
            ends[1] = jnp.where(mine, jnp.maximum(ends[1], index), ends[1])

        for b in range(blocks):
            walk((me ^ (2 + r)) * blocks + b, visit)
        for side in range(2):
            table[blocks * LINKED + 2 * r + side] = ends[side]


def row_span(index):
    return pl.ds(pl.multiple_of(jnp.maximum(index, 0) * T, T), T)


def live_factor(index):
    return jnp.where(index >= 0, 1.0, 0.0).astype(BF)


def norm_top(rows):
    wide = rows.astype(F32)
    return jnp.sum(jnp.max(wide * wide, axis=0, keepdims=True))


def causal(width):
    keys = lax.broadcasted_iota(jnp.int32, (T, T), 0)
    queries = lax.broadcasted_iota(jnp.int32, (T, T), 1)
    return jnp.concatenate([keys <= queries] * width, 1)


def near_kernel(*refs, head, blocks, heads, groups, depth):
    if head == 0:
        info, q_v, do_in, own, near = refs[:5]
        table, top, do_v, qt, dt, kbn, vtn, pn, dpn, on = refs[5:15]
        kv, vb, kv_sem, row_sem = refs[15:]
    else:
        table, qt, dt, own, near = refs[:5]
        top, kbn, vtn, pn, dpn, on = refs[5:11]
        kv, vb, kv_sem = refs[11:]

    kv_copies = [
        pltpu.make_async_copy(source, kv.at[i], kv_sem.at[i]) for i, source in enumerate((own, near))
    ]
    for copy in kv_copies:
        copy.start()
    if head == 0:

        do_copy = pltpu.make_async_copy(do_in, do_v, row_sem)
        do_copy.start()
        relation_table(info, table, blocks, depth)
        highest = jnp.zeros((1, heads * groups * T), F32)
        for b in range(blocks):
            for g in range(heads * groups):
                col = pl.ds(g * D, D)
                qt[b, :, col] = q_v[pl.ds(b * T, T), col].T
            wide = qt[b].astype(F32)
            highest = jnp.maximum(highest, jnp.sum(wide * wide, axis=0, keepdims=True))
        top[0] = jnp.max(highest)
    for copy in kv_copies:
        copy.wait()
    top[1 if head == 0 else 0] = jnp.maximum(norm_top(kv[0, :, :D]), norm_top(kv[1, :, :D]))
    for b in range(blocks):
        for r in range(2):
            index = table[b * LINKED + r]
            here = pl.ds(r * T, T)
            kbn[b, here, :] = kv[r, row_span(index), :D] * live_factor(index)
            values = kv[r, row_span(index), D:] * live_factor(index)
            vb[b, here, :] = values
            vtn[b, :D, here] = values.T
            vtn[b, D:, here] = jnp.full((ONES, T), live_factor(index), BF)
    tri = causal(WIDE)
    pieces = [
        (b, pl.ds(j * T, WIDE * T), pl.ds((head * groups + j) * D, WIDE * D))
        for b in range(blocks)
        for j in range(0, groups, WIDE)
    ]
    for b, col, head_col in pieces:
        scores = jnp.dot(kbn[b], qt[b, :, head_col], preferred_element_type=F32)
        exps = jnp.exp2(scores * (SCALE * LOG2E))
        pn[b, :T, col] = jnp.where(tri, exps[:T], 0.0).astype(BF)
        pn[b, T:, col] = exps[T:].astype(BF)
    if head == 0:
        do_copy.wait()
        for b in range(blocks):
            for g in range(heads * groups):
                col = pl.ds(g * D, D)
                dt[b, :, col] = do_v[pl.ds(b * T, T), col].T
    for b, col, head_col in pieces:
        dpn[b, :, col] = jnp.dot(vb[b], dt[b, :, head_col], preferred_element_type=F32)
    for b, col, head_col in pieces:
        on[b, :, col] = jnp.dot(vtn[b], pn[b, :, col], preferred_element_type=F32)[: D + 8]


def far_kernel(*refs, head, blocks, groups, chained):
    table, top, near_top, q_v, do_v, qt, dt, kbn, vtn, pn, dpn, on = refs[:12]
    sources = refs[12:14]
    at = 15 if chained else 14
    o_out, pn_out, dst, kb, stats = refs[at : at + 5]
    sent = refs[at + 5 : at + 8]
    pt, vb, vt, acc, o_buf, out_sem = refs[at + 8 :]
    acc[...] = jnp.zeros_like(acc)
    for b in range(blocks):
        kb[b, :T, :] = kbn[b, T:]
        for r in range(2):
            index = table[b * LINKED + 2 + r]
            here = pl.ds(r * T, T)
            kb[b, pl.ds((1 + r) * T, T), :] = sources[r][row_span(index), :D] * live_factor(index)
            values = sources[r][row_span(index), D:] * live_factor(index)
            vb[b, here, :] = values
            vt[b, :D, here] = values.T
            vt[b, D:, here] = jnp.full((ONES, T), live_factor(index), BF)

    def out_copy(b):
        rows = pl.ds(pl.multiple_of(b * T, T), T)
        columns = pl.ds(head * groups * D, groups * D)
        return pltpu.make_async_copy(o_buf.at[b], o_out.at[rows, columns], out_sem.at[b])

    keys_top = jnp.maximum(norm_top(sources[0][:, :D]), norm_top(sources[1][:, :D]))
    keys_top = jnp.maximum(keys_top, near_top[1 if head == 0 else 0])
    safe = top[0] * keys_top <= (SAFE_EXPONENT / (SCALE * LOG2E)) ** 2

    @pl.when(safe)
    def _():
        pieces = [
            (b, j, pl.ds(j * T, WIDE * T), pl.ds((head * groups + j) * D, WIDE * D))
            for b in range(blocks)
            for j in range(0, groups, WIDE)
        ]
        for b, j, col, head_col in pieces:
            scores = jnp.dot(kb[b, T:], qt[b, :, head_col], preferred_element_type=F32)
            pt[b, T:, col] = jnp.exp2(scores * (SCALE * LOG2E)).astype(BF)
        for b, j, col, head_col in pieces:
            sums = jnp.dot(vt[b], pt[b, T:, col], preferred_element_type=F32)
            sums = sums[: D + 8] + on[b, :, col]
            inverse = 1.0 / sums[D : D + 1]
            out_t = (sums[:D] * inverse).astype(BF)
            inner = jnp.sum(
                out_t.astype(F32) * dt[b, :, head_col].astype(F32), axis=0, keepdims=True
            )
            stats[b, :8, col] = jnp.broadcast_to(inverse, (8, WIDE * T))
            stats[b, 8:, col] = jnp.broadcast_to(inner, (8, WIDE * T))
            for w in range(WIDE):
                o_buf[b, :, pl.ds((j + w) * D, D)] = out_t[:, w * T : (w + 1) * T].T
            if j + WIDE == groups:
                out_copy(b).start()
        for b, j, col, head_col in pieces:
            dprobs = jnp.dot(vb[b], dt[b, :, head_col], preferred_element_type=F32)
            weights = pt[b, T:, col].astype(F32) * stats[b, :1, col]
            pt[b, T:, col] = weights.astype(BF)
            dst[b, T:, col] = (weights * (dprobs - stats[b, 8:9, col])).astype(BF)
        for b, j, col, head_col in pieces:
            weights = pn[b, T:, col].astype(F32) * stats[b, :1, col]
            pt[b, :T, col] = weights.astype(BF)
            dst[b, :T, col] = (weights * (dpn[b, T:, col] - stats[b, 8:9, col])).astype(BF)

    @pl.when(jnp.logical_not(safe))
    def _():
        tri = causal(1)

        def block(b, carry):
            bias = [
                jnp.where(table[b * LINKED + r] >= 0, 0.0, -jnp.inf).astype(F32)
                for r in range(LINKED)
            ]
            for g in range(groups):
                col = pl.ds(g * T, T)
                head_col = pl.ds((head * groups + g) * D, D)
                near_scores = jnp.dot(kbn[b], qt[b, :, head_col], preferred_element_type=F32)
                scores = jnp.dot(kb[b, T:], qt[b, :, head_col], preferred_element_type=F32)
                dprobs = jnp.dot(vb[b], dt[b, :, head_col], preferred_element_type=F32)
                dparts = [dpn[b, :T, col], dpn[b, T:, col], dprobs[:T], dprobs[T:]]
                parts = [near_scores[:T], near_scores[T:], scores[:T], scores[T:]]
                parts = [x * (SCALE * LOG2E) for x in parts]
                parts[0] = jnp.where(tri, parts[0], -jnp.inf)
                highs = [jnp.max(x, axis=0, keepdims=True) + bias[r] for r, x in enumerate(parts)]
                high = functools.reduce(jnp.maximum, highs)
                exps = [jnp.exp2(x - (high - bias[r])) for r, x in enumerate(parts)]
                total = functools.reduce(
                    jnp.add, [jnp.sum(x, axis=0, keepdims=True) for x in exps]
                )
                inverse = 1.0 / total
                for r in range(LINKED):
                    weights = (exps[r] * inverse).astype(BF)
                    if r < 2:
                        pn_out[b, pl.ds(r * T, T), col] = weights
                    if r > 0:
                        pt[b, pl.ds((r - 1) * T, T), col] = weights
                out_t = jnp.dot(
                    vtn[b], pn_out[b, :, col], preferred_element_type=F32
                ) + jnp.dot(vt[b], pt[b, T:, col], preferred_element_type=F32)
                out_t = out_t[:D].astype(BF)
                inner = jnp.sum(
                    out_t.astype(F32) * dt[b, :, head_col].astype(F32), axis=0, keepdims=True
                )
                stats[b, :8, col] = jnp.ones((8, T), F32)
                stats[b, 8:, col] = jnp.broadcast_to(inner, (8, T))
                for r in range(3):
                    dscores = exps[1 + r] * inverse * (dparts[1 + r] - inner)
                    dst[b, pl.ds(r * T, T), col] = dscores.astype(BF)
                o_buf[b, :, pl.ds(g * D, D)] = out_t.T
            out_copy(b).start()
            return carry

        lax.fori_loop(0, blocks, block, 0)

    lows = [
        functools.reduce(
            jnp.minimum,
            [
                jnp.where(table[b * LINKED + r] >= 0, table[b * LINKED + r], blocks)
                for b in range(blocks)
            ],
        )
        for r in (2, 3)
    ]
    for b in range(blocks):
        q_rows, do_rows = (stacked(ref, head, b, groups) for ref in (q_v, do_v))
        dv = jnp.dot(pt[b], do_rows, preferred_element_type=F32)
        dk = jnp.dot(dst[b], q_rows, preferred_element_type=F32) * SCALE
        places = [table[b * LINKED + 1 + r] for r in range(3)]
        for r, index in enumerate(places):
            slot = index
            if r:
                slot = jnp.where(index == lows[r - 1], 0, 1) + blocks + (r - 1) * 2
            here = row_span(jnp.where(index >= 0, slot, blocks + 4))
            acc[here, :D] += dk[r * T : (r + 1) * T]
            acc[here, D:] += dv[r * T : (r + 1) * T]
    tokens = blocks * T
    ends = [0, tokens, tokens + 2 * T, tokens + 4 * T]
    for r in range(3):
        sent[r][...] = acc[ends[r] : ends[r + 1]].astype(BF)
    for b in range(blocks):
        out_copy(b).wait()


def stacked(ref, head, b, groups):
    return jnp.concatenate(
        [ref[pl.ds(b * T, T), pl.ds((head * groups + g) * D, D)] for g in range(groups)], 0
    )


def tail_kernel(*refs, head, blocks, groups, chained):
    q_v, do_v, kbn, pn, dpn, dst, kb, stats = refs[:8]
    at = 9 if chained else 8
    dq_out, own_ref = refs[at : at + 2]
    ptn, dsn, dq_buf, out_sem = refs[at + 2 :]

    def out_copy(b):
        rows = pl.ds(b * T, T)
        columns = pl.ds(head * groups * D, groups * D)
        return pltpu.make_async_copy(dq_buf.at[b], dq_out.at[rows, columns], out_sem.at[b])

    pieces = [(b, j, pl.ds(j * T, WIDE * T)) for b in range(blocks) for j in range(0, groups, WIDE)]
    for b, j, col in pieces:
        weights = pn[b, :T, col].astype(F32) * stats[b, :1, col]
        ptn[b, :, col] = weights.astype(BF)
        dsn[b, :, col] = (weights * (dpn[b, :T, col] - stats[b, 8:9, col])).astype(BF)
    for b, j, col in pieces:
        dq_t = lax.dot_general(kbn[b, :T], dsn[b, :, col], TN, preferred_element_type=F32)
        dq_t += lax.dot_general(kb[b], dst[b, :, col], TN, preferred_element_type=F32)
        dq_t = dq_t * SCALE
        for w in range(WIDE):
            dq_buf[b, :, pl.ds((j + w) * D, D)] = dq_t[:, w * T : (w + 1) * T].astype(BF).T
        if j + WIDE == groups:
            out_copy(b).start()
    for b in range(blocks):
        rows = pl.ds(b * T, T)
        q_rows, do_rows = (stacked(ref, head, b, groups) for ref in (q_v, do_v))
        own_ref[rows, :D] = jnp.dot(dsn[b], q_rows, preferred_element_type=F32) * SCALE
        own_ref[rows, D:] = jnp.dot(ptn[b], do_rows, preferred_element_type=F32)
    for b in range(blocks):
        out_copy(b).wait()


def finish_kernel(*refs, heads, blocks):
    table = refs[0]
    dk_ref, dv_ref, acc = refs[-3:]
    at = 1
    for h in range(heads):
        own, core = refs[at : at + 2]
        at += 2
        acc[...] = own[...] + core[...].astype(F32)
        for r in range(2):
            for side in range(2):
                index = jnp.minimum(table[blocks * LINKED + 2 * r + side], blocks - 1)
                acc[row_span(index)] += refs[at + r][pl.ds(side * T, T)].astype(F32)
        at += 2
        dk_ref[:, pl.ds(h * D, D)] = acc[:, :D].astype(BF)
        dv_ref[:, pl.ds(h * D, D)] = acc[:, D:].astype(BF)


def work(microseconds):
    return pl.CostEstimate(flops=int(microseconds * 10**9), bytes_accessed=0, transcendentals=0)


def linked_body(info, queries, output_gradient, packed):
    tokens = queries.shape[0]
    heads = len(packed)
    blocks = tokens // T
    groups = QUERY_HEADS // KEY_VALUE_HEADS
    width = groups * T
    depth = min(PATH_DEPTH_MAX, LINKED)
    core = [(i, i ^ 1) for i in range(LINKED)]
    across = [(i, i ^ 2) for i in range(LINKED)]
    corner = [(i, i ^ 3) for i in range(LINKED)]
    near = [lax.ppermute(own, "ctx", core) for own in packed]
    far = [lax.ppermute(own, "ctx", across) for own in packed]

    vmem = pl.BlockSpec(memory_space=pltpu.VMEM)
    smem = pl.BlockSpec(memory_space=pltpu.SMEM)
    hbm = pl.BlockSpec(memory_space=pl.ANY)
    kept = pltpu.VMEM

    def keep(x):
        return pltpu.with_memory_space_constraint(x, pltpu.VMEM)

    def scalars(x):
        return pltpu.with_memory_space_constraint(x, pltpu.SMEM)

    def near_work(h, local):
        first = local is None
        parts = [
            kept((blocks, 2 * T, D), BF),
            kept((blocks, D + ONES, 2 * T), BF),
            kept((blocks, 2 * T, width), BF),
            kept((blocks, 2 * T, width), F32),
            kept((blocks, D + 8, width), F32),
        ]
        whole = [
            kept(queries.shape, BF),
            kept((blocks, D, heads * width), BF),
            kept((blocks, D, heads * width), BF),
        ]
        table_shape = pltpu.SMEM((blocks * LINKED + 4,), jnp.int32)
        if first:
            wide = pl.BlockSpec(memory_space=pltpu.HBM)
            operands = [
                info,
                kept_queries,
                pltpu.with_memory_space_constraint(output_gradient, pltpu.HBM),
            ]
            in_specs = [smem, vmem, wide]
            out_specs = [smem, smem] + [vmem] * 8
            out_shape = [table_shape, pltpu.SMEM((2,), F32)] + whole + parts
        else:
            operands = [local[0], local[4], local[5]]
            in_specs = [smem, vmem, vmem]
            out_specs = [smem] + [vmem] * 5
            out_shape = [pltpu.SMEM((1,), F32)] + parts
        done = pl.pallas_call(
            functools.partial(
                near_kernel, head=h, blocks=blocks, heads=heads, groups=groups, depth=depth
            ),
            in_specs=in_specs + [hbm, hbm],
            out_specs=out_specs,
            out_shape=out_shape,
            scratch_shapes=[
                pltpu.VMEM((2, tokens, 2 * D), BF),
                pltpu.VMEM((blocks, 2 * T, D), BF),
                pltpu.SemaphoreType.DMA((2,)),
            ]
            + ([pltpu.SemaphoreType.DMA] if first else []),
            compiler_params=pltpu.CompilerParams(vmem_limit_bytes=12 * 2**20),
            cost_estimate=work(4),
            name="near",
        )(*operands, packed[h], near[h])
        return [scalars(x) if x.ndim == 1 else keep(x) for x in done]

    kept_queries = keep(queries)
    shared = near_work(0, None)
    table, top = shared[:2]
    local = [kept_queries] + shared[2:5]
    far[0], _ = lax.optimization_barrier((far[0], shared[9]))
    diagonal = [lax.ppermute(far[0], "ctx", core)]
    near_parts = [[top] + shared[5:]]
    for h in range(1, heads):
        near_parts.append(near_work(h, [table, None] + local))
        far[h], _ = lax.optimization_barrier((far[h], near_parts[h][5]))
        diagonal.append(lax.ppermute(far[h], "ctx", core))

    attended = None
    probs = []
    arrivals = []
    for h in range(heads):
        chained = attended is not None
        sent = [tokens, 2 * T, 2 * T]
        operands = [table, top, near_parts[h][0], *local, *near_parts[h][1:]]
        operands += [keep(far[h]), keep(diagonal[h])]
        done = pl.pallas_call(
            functools.partial(
                far_kernel, head=h, blocks=blocks, groups=groups, chained=chained
            ),
            in_specs=[smem] * 3 + [vmem] * 11 + [hbm] * (1 if chained else 0),
            out_specs=[hbm] + [vmem] * (4 + len(sent)),
            out_shape=[
                jax.ShapeDtypeStruct(queries.shape, BF),
                kept((blocks, 2 * T, width), BF),
                kept((blocks, 3 * T, width), BF),
                kept((blocks, 3 * T, D), BF),
                kept((blocks, 16, width), F32),
            ]
            + [kept((rows, 2 * D), BF) for rows in sent],
            input_output_aliases={9: 1} | ({len(operands): 0} if chained else {}),
            scratch_shapes=[
                pltpu.VMEM((blocks, 3 * T, width), BF),
                pltpu.VMEM((blocks, 2 * T, D), BF),
                pltpu.VMEM((blocks, D + ONES, 2 * T), BF),
                pltpu.VMEM((tokens + 5 * T, 2 * D), F32),
                pltpu.VMEM((blocks, T, groups * D), BF),
                pltpu.SemaphoreType.DMA((blocks,)),
            ],
            compiler_params=pltpu.CompilerParams(vmem_limit_bytes=12 * 2**20),
            cost_estimate=work(5),
            name="far",
        )(*operands, *([attended] if chained else []))
        attended = done[0]
        near_probs, *rest = [keep(x) for x in done[1:5]]
        _, kbn, _, _, dpn, _ = near_parts[h]
        probs.append([kbn, near_probs, dpn, *rest])
        to_core, to_far, to_corner = done[5:]
        arrivals.append(
            [
                lax.ppermute(to_core, "ctx", core),
                lax.ppermute(to_far, "ctx", across),
                lax.ppermute(to_corner, "ctx", corner),
            ]
        )

    d_queries = None
    finishing = [table]
    for h in range(heads):
        chained = d_queries is not None
        operands = [local[0], local[1], *probs[h]]
        if not chained and heads > 1:
            operands[-1], arrivals[0] = lax.optimization_barrier((operands[-1], arrivals[0]))
            operands[-1] = keep(operands[-1])
        done = pl.pallas_call(
            functools.partial(tail_kernel, head=h, blocks=blocks, groups=groups, chained=chained),
            in_specs=[vmem] * 8 + ([hbm] if chained else []),
            out_specs=[hbm, vmem],
            out_shape=[jax.ShapeDtypeStruct(queries.shape, BF), kept((tokens, 2 * D), F32)],
            input_output_aliases={len(operands): 0} if chained else {},
            scratch_shapes=[
                pltpu.VMEM((blocks, T, width), BF),
                pltpu.VMEM((blocks, T, width), BF),
                pltpu.VMEM((blocks, T, groups * D), BF),
                pltpu.SemaphoreType.DMA((blocks,)),
            ],
            compiler_params=pltpu.CompilerParams(vmem_limit_bytes=12 * 2**20),
            cost_estimate=work(1),
            name="tail",
        )(*operands, *([d_queries] if chained else []))
        d_queries = done[0]
        finishing += [keep(done[1])] + [keep(x) for x in arrivals[h]]
    d_keys, d_values = pl.pallas_call(
        functools.partial(finish_kernel, heads=heads, blocks=blocks),
        in_specs=[smem] + [vmem] * (len(finishing) - 1),
        out_specs=[vmem, vmem],
        out_shape=[jax.ShapeDtypeStruct((tokens, heads * D), BF)] * 2,
        scratch_shapes=[pltpu.VMEM((tokens, 2 * D), F32)],
        name="finish",
    )(*finishing)
    return attended, d_queries, d_keys, d_values


def body(queries, key_states, value_tensor, output_gradient, parent, block_owner, shards):
    heads = key_states.shape[1] // D
    me = lax.axis_index("ctx").astype(jnp.int32)
    info = jnp.concatenate([me[None], parent, block_owner])
    packed = [
        jnp.concatenate([key_states[:, h * D : (h + 1) * D], value_tensor[:, h * D : (h + 1) * D]], 1)
        for h in range(heads)
    ]
    if shards == LINKED:
        return linked_body(info, queries, output_gradient, packed)
    outputs = None
    summed = []
    for h in range(heads):
        gathered = lax.all_gather(packed[h], "ctx", axis=0, tiled=True)
        done = attend(info, queries, output_gradient, gathered, outputs, h, shards)
        outputs = done[:2]
        summed.append(lax.psum_scatter(done[2], "ctx", scatter_dimension=0, tiled=True))
    d_keys = jnp.concatenate([s[:, :D] for s in summed], 1).astype(BF)
    d_values = jnp.concatenate([s[:, D:] for s in summed], 1).astype(BF)
    return (outputs[0], outputs[1], d_keys, d_values)


def solution(mesh):
    tokens_split = P(("groups", "ctx"), "tp")
    return jax.shard_map(
        functools.partial(body, shards=mesh.shape["ctx"]),
        mesh=mesh,
        in_specs=(tokens_split,) * 4 + (P("groups"),) * 2,
        out_specs=(tokens_split,) * 4,
        check_vma=False,
    )
```
